32 devices in a mesh: table: 4 (over z), rep: 8 (over y, x, core).
Axes of the slice: x: 2, y: 2, z: 4, core: 2. Of those that a mesh axis runs over, the one named last changes fastest.
Arguments:
- activations: bfloat16 [4096, 3456], P(('table', 'rep')), may hold values from -6 to 6
- cotangent: bfloat16 [4096, 3456], P(('table', 'rep')), may hold values from -6 to 6
- down_weight: bfloat16 [256, 3456], replicated, may hold values from -0.109375 to 0.109375
- up_weight: bfloat16 [256, 3456], replicated, may hold values from -0.375 to 0.375
- bias: float32 [3456], replicated, may hold values from -3 to 3
- bag_ids: int32 [4096, 26, 4], P(('table', 'rep')), may hold values from 0 to 511
- bag_lengths: int32 [4096, 26], P(('table', 'rep')), may hold values from 1 to 4
- feature_table_slot: int32 [26], replicated, may hold values from 0 to 27, as said below
Outputs:
- dense_grad: bfloat16 [4096, 128], P(('table', 'rep'))
- up_grad: float32 [256, 3456], P('rep', 'table')
- down_grad: float32 [256, 3456], P('rep', 'table')
- bias_grad: float32 [3456], replicated
- row_grad: float32 [8, 28, 512, 128], P('rep', 'table')
The draws below stay inside these ranges and needn't reach their ends.
Inputs may be any that keep to these rules, and one draw needn't show every extreme that they name: `feature_table_slot`: distinct slots, one for each feature; slot s belongs to the table owner s // 7.
All inputs are finite; a program needn't handle non-finite values.
Results may differ from the reference program's by a relative error of at most 0.0051.
Values may be sent and summed in bfloat16 or wider, within the bound.
No kernel may reach another device: no remote copies, remote signals or barrier semaphores. Data moves between devices by JAX's collectives and lax.ppermute only.
A program may use at most 64 MiB of HBM per device.

```python
import math
import jax
import jax.numpy as jnp
import numpy as np
from jax import lax

EMBED_WIDTH = 128
SPARSE_FEATURES = 26
D = 3456
R = 256
BAG = 4
TABLE_REACH_ROWS = 512
TOK_DEV = 128
TOKENS = 4096
TABLE_SLOTS = 28
N_TABLE = 4
N_REP = 8


def draw_feature_table_slot(key, part):
    key = jax.random.fold_in(key, 11)
    initial_key, order_key = jax.random.split(key)
    chosen_rows = jax.random.permutation(initial_key, TABLE_SLOTS - 2)[:SPARSE_FEATURES - 2] + 1
    complete_table = jnp.concatenate([jnp.array([0], jnp.int32), chosen_rows.astype(jnp.int32), jnp.array([TABLE_SLOTS - 1], jnp.int32)])
    order = jax.random.permutation(order_key, SPARSE_FEATURES)
    return complete_table[order].astype(jnp.int32)


def plant(drawn, key, least, largest):
    dims = drawn.shape
    spot = [jax.random.randint(jax.random.fold_in(key, axis), (), 0, dims[axis]) for axis in range(len(dims))]
    drawn = drawn.at[tuple(spot)].set(least)
    longest = dims.index(max(dims))
    spot[longest] = (spot[longest] + 1) % dims[longest]
    return drawn.at[tuple(spot)].set(largest)


def shard_levels(stream_key, dims, cuts, least, top_value):
    factor_of, own = 1.0, jax.random.fold_in(stream_key, 6)
    for dim, parts in cuts:
        draws = jnp.exp(jax.random.uniform(jax.random.fold_in(own, dim), (parts,), jnp.float32, least / len(cuts), top_value / len(cuts)))
        factor_of = factor_of * jnp.repeat(draws, dims[dim] // parts).reshape([-1 if axis == dim else 1 for axis in range(len(dims))])
    return factor_of


def rank_table(number_of, lean):
    portions = [(1 << 20) // math.isqrt(standing ** lean) + 1 for standing in range(1, number_of + 1)]
    spread = 1 + sum(portions) // (1 << 30)
    return np.cumsum(np.array([max(1, weight // spread) for weight in portions]))


def ranked_ids(stream_key, shape, amount, skew):
    table = rank_table(amount, skew)
    lot = jax.random.randint(jax.random.fold_in(stream_key, 1), shape, 0, int(table[amount - 1]))
    grade = jnp.searchsorted(jnp.asarray(table, jnp.int32), lot, side="right")
    return jax.random.permutation(jax.random.fold_in(stream_key, 2), amount)[grade].astype(jnp.int32)


def centred(stream_key, shape, width, bound, cuts=(), kind=jnp.bfloat16):
    drawn = jax.random.normal(stream_key, shape, jnp.float32) * width
    if len(cuts) > 0:
        drawn = shard_levels(stream_key, shape, cuts, -0.22, 0.18) * drawn
    return jnp.clip(drawn, min=-bound, max=bound).astype(kind)


def setup_inputs(seed: int = 0) -> dict:
    keys = jax.random.split(jax.random.key(seed), 9)
    return {
        "activations": centred(keys[0], (TOKENS, D), 1.0, 6.0, ((0, 32),)),
        "cotangent": centred(keys[1], (TOKENS, D), 1.0, 6.0, ((0, 32),)),
        "down_weight": centred(keys[2], (R, D), D ** -0.5, 0.109375),
        "up_weight": centred(keys[3], (R, D), R ** -0.5, 0.375),
        "bias": centred(keys[4], (D,), 0.5, 3.0, (), jnp.float32),
        "bag_ids": plant(ranked_ids(keys[5], (TOKENS, SPARSE_FEATURES, BAG), TABLE_REACH_ROWS, 2), jax.random.fold_in(keys[5], 3), 0, TABLE_REACH_ROWS - 1).astype(jnp.int32),
        "bag_lengths": plant(jax.random.randint(keys[6], (TOKENS, SPARSE_FEATURES), 1, BAG + 1), jax.random.fold_in(keys[6], 1), 1, BAG).astype(jnp.int32),
        "feature_table_slot": draw_feature_table_slot(jax.random.fold_in(keys[8], 71), 0),
    }


def reference(activations, cotangent, down_weight, up_weight, bias, bag_ids, bag_lengths, feature_table_slot):
    rows = TOK_DEV * N_REP
    x_blocks = activations.reshape(N_TABLE, rows, D)
    g_blocks = cotangent.reshape(N_TABLE, rows, D)

    def step(carry, pieces):
        up_acc, down_acc, bias_acc = carry
        x, g = pieces
        hidden = jnp.dot(x, down_weight.T, preferred_element_type=jnp.float32).astype(jnp.bfloat16)
        mixed = jnp.dot(hidden, up_weight, preferred_element_type=jnp.float32) + bias
        gf = g.astype(jnp.float32)
        scaled = gf * x.astype(jnp.float32)
        scaled_b = scaled.astype(jnp.bfloat16)
        back_hidden = jnp.dot(scaled_b, up_weight.T, preferred_element_type=jnp.float32).astype(jnp.bfloat16)
        input_grad = gf * (1.0 + mixed) + jnp.dot(back_hidden, down_weight, preferred_element_type=jnp.float32)
        up_acc = up_acc + jnp.dot(hidden.T, scaled_b, preferred_element_type=jnp.float32)
        down_acc = down_acc + jnp.dot(back_hidden.T, x, preferred_element_type=jnp.float32)
        bias_acc = bias_acc + lax.optimization_barrier(jnp.sum(scaled, axis=0))
        return ((up_acc, down_acc, bias_acc), (input_grad[:, :EMBED_WIDTH].astype(jnp.bfloat16), input_grad[:, EMBED_WIDTH:].astype(jnp.bfloat16)))
    start = (jnp.zeros((R, D), jnp.float32), jnp.zeros((R, D), jnp.float32), jnp.zeros((D,), jnp.float32))
    (up_acc, down_acc, bias_acc), (dense_part, pooled_part) = lax.scan(step, start, (x_blocks, g_blocks))
    scale = 1.0 / math.sqrt(TOKENS)
    dense_grad = dense_part.reshape(TOKENS, EMBED_WIDTH)
    pooled = pooled_part.reshape(N_TABLE, N_REP, TOK_DEV, SPARSE_FEATURES, EMBED_WIDTH).transpose(1, 0, 2, 3, 4)
    entries = jnp.arange(BAG, dtype=jnp.int32)
    masked = jnp.where(entries[None, None, :] < bag_lengths[:, :, None], bag_ids, -1)
    masked = masked.reshape(N_TABLE, N_REP, TOK_DEV, SPARSE_FEATURES, BAG).transpose(1, 0, 2, 3, 4)
    table_rows = jnp.arange(TABLE_REACH_ROWS, dtype=jnp.int32)

    def group(pieces):
        grads, ids = pieces
        grads = grads.reshape(N_TABLE * TOK_DEV, SPARSE_FEATURES, EMBED_WIDTH).astype(jnp.float32)
        ids = ids.reshape(N_TABLE * TOK_DEV, SPARSE_FEATURES, BAG)
        count = jnp.zeros((N_TABLE * TOK_DEV, SPARSE_FEATURES, TABLE_REACH_ROWS), jnp.float32)
        for entry in range(BAG):
            count = count + (ids[:, :, entry, None] == table_rows).astype(jnp.float32)
        each_feature = jnp.einsum('sfr,sfc->frc', count, grads)
        return jnp.zeros((TABLE_SLOTS, TABLE_REACH_ROWS, EMBED_WIDTH), jnp.float32).at[feature_table_slot].set(each_feature)
    row_grad = lax.map(group, (pooled, masked))
    return (dense_grad, up_acc * scale, down_acc * scale, bias_acc * scale, row_grad)
```

```python
import functools
import math

import jax
import jax.numpy as jnp
from jax import lax
from jax.experimental import pallas as pl
from jax.experimental.pallas import tpu as pltpu
from jax.sharding import PartitionSpec as P

EMBED_WIDTH = 128
SPARSE_FEATURES = 26
BAG = 4
TABLE_REACH_ROWS = 512
F32 = jnp.float32
BF16 = jnp.bfloat16
VMEM_LIMIT = 48 * 1024 * 1024


def column_chunk(width):
    blocks = width // EMBED_WIDTH
    for parts in (3, 2, 1):
        if blocks % parts == 0:
            return width // parts


def params(*semantics):
    return pltpu.CompilerParams(
        dimension_semantics=semantics or None, vmem_limit_bytes=VMEM_LIMIT
    )


def order_matrix(rep_index, size, block, bits):
    out_row = lax.broadcasted_iota(jnp.int32, (size, size), 0)
    in_row = lax.broadcasted_iota(jnp.int32, (size, size), 1)
    source = out_row % block
    position = out_row // block
    for place, bit in enumerate(bits):
        flag = (position // (1 << (len(bits) - 1 - place))) % 2
        own = (rep_index // bit) % 2
        source = source + jnp.where(flag == own, 0, bit) * block
    return (source == in_row).astype(F32).astype(BF16)


def hidden_kernel(
    up_bits, down_bits, rep_ref, act_ref, cot_ref, dw_ref, uw_ref,
    hidden_ref, back_ref, keep_ref, send_ref, hidden_acc, back_acc,
):
    step = pl.program_id(0)

    @pl.when(step == 0)
    def _():
        hidden_acc[...] = jnp.zeros_like(hidden_acc)
        back_acc[...] = jnp.zeros_like(back_acc)

    act = act_ref[...]
    scaled_b = (cot_ref[...].astype(F32) * act.astype(F32)).astype(BF16)
    dims = (((1,), (1,)), ((), ()))
    hidden_acc[...] += lax.dot_general(act, dw_ref[...], dims, preferred_element_type=F32)
    back_acc[...] += lax.dot_general(scaled_b, uw_ref[...], dims, preferred_element_type=F32)

    @pl.when(step == pl.num_programs(0) - 1)
    def _():
        hidden = hidden_acc[...].astype(BF16)
        back = back_acc[...].astype(BF16)
        hidden_ref[...] = hidden
        back_ref[...] = back
        rank = hidden.shape[1]
        half = rank // 2
        block = rank >> len(up_bits)
        for which, (value, bits) in enumerate(((hidden, up_bits), (back, down_bits))):
            order = order_matrix(rep_ref[0], rank, block, bits)
            rows = lax.dot_general(order, value, dims, preferred_element_type=F32).astype(BF16)
            keep_ref[which] = rows[:half]
            send_ref[which] = rows[half:]


def hidden_call(act, cot, dw, uw, rep_index, up_bits, down_bits):
    tokens, width = act.shape
    rank = dw.shape[0]
    chunk = column_chunk(width)
    wide = pl.BlockSpec((tokens, chunk), lambda i: (0, i))
    weight = pl.BlockSpec((rank, chunk), lambda i: (0, i))
    factor = pl.BlockSpec((tokens, rank), lambda i: (0, 0))
    rows = pl.BlockSpec((2, rank // 2, tokens), lambda i: (0, 0, 0))
    return pl.pallas_call(
        functools.partial(hidden_kernel, up_bits, down_bits),
        grid=(width // chunk,),
        in_specs=[pl.BlockSpec(memory_space=pltpu.SMEM), wide, wide, weight, weight],
        out_specs=[factor, factor, rows, rows],
        out_shape=[
            jax.ShapeDtypeStruct((tokens, rank), BF16),
            jax.ShapeDtypeStruct((tokens, rank), BF16),
            jax.ShapeDtypeStruct((2, rank // 2, tokens), BF16),
            jax.ShapeDtypeStruct((2, rank // 2, tokens), BF16),
        ],
        scratch_shapes=[pltpu.VMEM((tokens, rank), F32), pltpu.VMEM((tokens, rank), F32)],
        compiler_params=params("arbitrary"),
        cost_estimate=pl.CostEstimate(
            flops=4 * tokens * rank * width, bytes_accessed=4 * (tokens + rank) * width, transcendentals=0
        ),
    )(rep_index, act, cot, dw, uw)


def grad_kernel(
    n_table, slots, feature_ref, hidden_ref, back_ref, cot_ref, dw_ref, uw_ref, bias_ref, dense_ref, *rest
):
    outs, store = rest[:n_table], rest[n_table]
    step = pl.program_id(0)
    blocks = cot_ref.shape[1] // EMBED_WIDTH
    mixed = jnp.dot(hidden_ref[...], uw_ref[...], preferred_element_type=F32) + bias_ref[...]
    grad = cot_ref[...].astype(F32) * (1.0 + mixed) + jnp.dot(
        back_ref[...], dw_ref[...], preferred_element_type=F32
    )
    grad = grad.astype(BF16)
    for block in range(blocks):
        store[step * blocks + block] = grad[:, block * EMBED_WIDTH : (block + 1) * EMBED_WIDTH]

    @pl.when(step == pl.num_programs(0) - 1)
    def _():
        store[SPARSE_FEATURES + 1] = jnp.zeros(store.shape[1:], BF16)
        dense_ref[...] = store[0]
        for shift in range(n_table):
            for slot in range(slots):
                outs[shift][slot] = store[feature_ref[shift * slots + slot] + 1]


def grad_call(features, hidden, back, cot, dw, uw, bias, n_table, slots):
    tokens, width = cot.shape
    rank = dw.shape[0]
    chunk = column_chunk(width)
    factor = pl.BlockSpec((tokens, rank), lambda i: (0, 0))
    weight = pl.BlockSpec((rank, chunk), lambda i: (0, i))
    part = pl.BlockSpec((slots, tokens, EMBED_WIDTH), lambda i: (0, 0, 0))
    return pl.pallas_call(
        functools.partial(grad_kernel, n_table, slots),
        grid=(width // chunk,),
        in_specs=[
            pl.BlockSpec(memory_space=pltpu.SMEM),
            factor,
            factor,
            pl.BlockSpec((tokens, chunk), lambda i: (0, i)),
            weight,
            weight,
            pl.BlockSpec((1, chunk), lambda i: (0, i)),
        ],
        out_specs=[pl.BlockSpec((tokens, EMBED_WIDTH), lambda i: (0, 0))] + [part] * n_table,
        out_shape=[jax.ShapeDtypeStruct((tokens, EMBED_WIDTH), BF16)]
        + [jax.ShapeDtypeStruct((slots, tokens, EMBED_WIDTH), BF16)] * n_table,
        scratch_shapes=[pltpu.VMEM((SPARSE_FEATURES + 2, tokens, EMBED_WIDTH), BF16)],
        compiler_params=params("arbitrary"),
        cost_estimate=pl.CostEstimate(
            flops=4 * tokens * rank * width, bytes_accessed=4 * (tokens + rank) * width, transcendentals=0
        ),
    )(features, hidden, back, cot, dw, uw, bias.reshape(1, width))


def ids_kernel(n_table, slots, feature_ref, ids_ref, length_ref, *outs):
    entries = lax.broadcasted_iota(jnp.int32, ids_ref.shape[1:], 0)
    for shift in range(n_table):
        for slot in range(slots):
            feature = feature_ref[shift * slots + slot]
            at = jnp.minimum(feature, SPARSE_FEATURES - 1)
            length = jnp.where(feature < SPARSE_FEATURES, length_ref[at], 0)
            outs[shift][slot] = jnp.where(entries < length, ids_ref[at], -1)


def ids_call(features, bag_ids, bag_lengths, n_table, slots):
    tokens = bag_ids.shape[0]
    ids = jnp.transpose(bag_ids, (1, 2, 0))
    lengths = jnp.transpose(bag_lengths, (1, 0))[:, None, :]
    vmem = pl.BlockSpec(memory_space=pltpu.VMEM)
    return pl.pallas_call(
        functools.partial(ids_kernel, n_table, slots),
        in_specs=[pl.BlockSpec(memory_space=pltpu.SMEM), vmem, vmem],
        out_specs=[vmem] * n_table,
        out_shape=[jax.ShapeDtypeStruct((slots, BAG, tokens), jnp.int32)] * n_table,
        compiler_params=params(),
    )(features, ids, lengths)


def terms_kernel(
    keep_ref, other_ref, act_ref, act_other_ref, cot_ref, cot_other_ref,
    up_keep_ref, up_send_ref, down_keep_ref, down_send_ref, bias_ref,
):
    act = jnp.concatenate([act_ref[...], act_other_ref[...]], axis=0)
    cot = jnp.concatenate([cot_ref[...], cot_other_ref[...]], axis=0)
    scaled = cot.astype(F32) * act.astype(F32)
    bias_ref[...] = jnp.sum(scaled, axis=0, keepdims=True)
    hidden = jnp.concatenate([keep_ref[0], other_ref[0]], axis=1)
    back = jnp.concatenate([keep_ref[1], other_ref[1]], axis=1)
    up = jnp.dot(hidden, scaled.astype(BF16), preferred_element_type=F32)
    down = jnp.dot(back, act, preferred_element_type=F32)
    half = up.shape[0] // 2
    up_keep_ref[...] = up[:half]
    up_send_ref[...] = up[half:].astype(BF16)
    down_keep_ref[...] = down[:half]
    down_send_ref[...] = down[half:].astype(BF16)


def terms_call(keep, other, act, act_other, cot, cot_other):
    tokens, width = act.shape
    rows = keep.shape[1]
    chunk = column_chunk(width)
    factor = pl.BlockSpec(keep.shape, lambda i: (0, 0, 0))
    wide = pl.BlockSpec((tokens, chunk), lambda i: (0, i))
    half = pl.BlockSpec((rows // 2, chunk), lambda i: (0, i))
    return pl.pallas_call(
        terms_kernel,
        grid=(width // chunk,),
        in_specs=[factor, factor, wide, wide, wide, wide],
        out_specs=[half, half, half, half, pl.BlockSpec((1, chunk), lambda i: (0, i))],
        out_shape=[
            jax.ShapeDtypeStruct((rows // 2, width), F32),
            jax.ShapeDtypeStruct((rows // 2, width), BF16),
            jax.ShapeDtypeStruct((rows // 2, width), F32),
            jax.ShapeDtypeStruct((rows // 2, width), BF16),
            jax.ShapeDtypeStruct((1, width), F32),
        ],
        compiler_params=params("arbitrary"),
        cost_estimate=pl.CostEstimate(
            flops=8 * tokens * rows * width, bytes_accessed=8 * tokens * width + 6 * rows * width, transcendentals=0
        ),
    )(keep, other, act, act_other, cot, cot_other)


def split_kernel(
    n_table, scale, table_ref, up_keep_ref, up_in_ref, down_keep_ref, down_in_ref, own_ref, *rest
):
    sends, store = rest[: n_table - 1], rest[n_table - 1]
    columns = own_ref.shape[2]
    pairs = ((up_keep_ref, up_in_ref), (down_keep_ref, down_in_ref))
    for which, (keep, arrived) in enumerate(pairs):
        total = (keep[...] + arrived[...].astype(F32)) * scale
        for table in range(n_table):
            store[table, which] = total[:, table * columns : (table + 1) * columns]
    own_ref[...] = store[table_ref[0]]
    for shift in range(1, n_table):
        sends[shift - 1][...] = store[(table_ref[0] + shift) % n_table].astype(BF16)


def split_call(table_index, up_keep, up_in, down_keep, down_in, n_table, scale):
    rows, width = up_keep.shape
    columns = width // n_table
    vmem = pl.BlockSpec(memory_space=pltpu.VMEM)
    return pl.pallas_call(
        functools.partial(split_kernel, n_table, scale),
        in_specs=[pl.BlockSpec(memory_space=pltpu.SMEM), vmem, vmem, vmem, vmem],
        out_specs=[vmem] * n_table,
        out_shape=[jax.ShapeDtypeStruct((2, rows, columns), F32)]
        + [jax.ShapeDtypeStruct((2, rows, columns), BF16)] * (n_table - 1),
        scratch_shapes=[pltpu.VMEM((n_table, 2, rows, columns), F32)],
        compiler_params=params(),
    )(table_index, up_keep, up_in, down_keep, down_in)


def rows_kernel(n_table, *refs):
    ids, grads, out_ref = refs[:n_table], refs[n_table : 2 * n_table], refs[2 * n_table]
    tokens = grads[0].shape[1]
    rows = lax.broadcasted_iota(jnp.int32, (TABLE_REACH_ROWS, tokens), 0)
    counts = []
    for source in range(n_table):
        count = jnp.zeros((TABLE_REACH_ROWS, tokens), F32)
        for entry in range(BAG):
            count = count + jnp.where(ids[source][0, entry : entry + 1, :] == rows, 1.0, 0.0)
        counts.append(count.astype(BF16))
    count = jnp.concatenate(counts, axis=1)
    grad = jnp.concatenate([grad_ref[0] for grad_ref in grads], axis=0)
    out_ref[0, 0] = jnp.dot(count, grad, preferred_element_type=F32)


def rows_call(ids, grads):
    n_table = len(ids)
    slots, _, tokens = ids[0].shape
    id_spec = pl.BlockSpec((1, BAG, tokens), lambda i: (i, 0, 0))
    grad_spec = pl.BlockSpec((1, tokens, EMBED_WIDTH), lambda i: (i, 0, 0))
    return pl.pallas_call(
        functools.partial(rows_kernel, n_table),
        grid=(slots,),
        in_specs=[id_spec] * n_table + [grad_spec] * n_table,
        out_specs=pl.BlockSpec((1, 1, TABLE_REACH_ROWS, EMBED_WIDTH), lambda i: (0, i, 0, 0)),
        out_shape=jax.ShapeDtypeStruct((1, slots, TABLE_REACH_ROWS, EMBED_WIDTH), F32),
        compiler_params=params("arbitrary"),
        cost_estimate=pl.CostEstimate(
            flops=2 * slots * n_table * tokens * TABLE_REACH_ROWS * EMBED_WIDTH,
            bytes_accessed=4 * slots * TABLE_REACH_ROWS * EMBED_WIDTH,
            transcendentals=0,
        ),
    )(*ids, *grads)


def body(
    activations, cotangent, down_weight, up_weight, bias, bag_ids, bag_lengths, feature_table_slot
):
    tokens = activations.shape[0]
    n_table = lax.axis_size("table")
    n_rep = lax.axis_size("rep")
    slots = (SPARSE_FEATURES + n_table - 1) // n_table
    scale = 1.0 / math.sqrt(tokens * n_table * n_rep)
    table_index = lax.axis_index("table").astype(jnp.int32)
    rep_index = lax.axis_index("rep").astype(jnp.int32)
    far_bits = [1 << k for k in range(1, n_rep.bit_length() - 1)]
    up_bits, down_bits = [1] + far_bits, [1] + far_bits[::-1]

    def swap(value, axis, bit):
        size = n_rep if axis == "rep" else n_table
        return lax.ppermute(value, axis, [(k, k ^ bit) for k in range(size)])

    def shifted(value, shift):
        return lax.ppermute(value, "table", [(k, (k + shift) % n_table) for k in range(n_table)])

    act_other = swap(activations, "rep", 1)
    cot_other = swap(cotangent, "rep", 1)

    owners = (table_index + jnp.arange(n_table, dtype=jnp.int32)) % n_table
    wanted = (owners[:, None] * slots + jnp.arange(slots, dtype=jnp.int32)[None, :]).reshape(-1)
    matches = feature_table_slot[None, :] == wanted[:, None]
    numbers = jnp.arange(SPARSE_FEATURES, dtype=jnp.int32)
    features = jnp.min(jnp.where(matches, numbers[None, :], SPARSE_FEATURES), axis=1)

    id_parts = ids_call(features, bag_ids, bag_lengths, n_table, slots)
    id_parts = [id_parts[0]] + [shifted(id_parts[k], k) for k in range(1, n_table)]

    hidden, back, keep, send = hidden_call(
        activations, cotangent, down_weight, up_weight, rep_index.reshape(1), up_bits, down_bits
    )
    other = swap(send, "rep", 1)
    dense_grad, *grad_parts = grad_call(
        features, hidden, back, cotangent, down_weight, up_weight, bias, n_table, slots
    )
    grad_parts = [grad_parts[0]] + [shifted(grad_parts[k], k) for k in range(1, n_table)]

    up_keep, up_send, down_keep, down_send, bias_sum = terms_call(
        keep, other, activations, act_other, cotangent, cot_other
    )
    for place, (up_bit, down_bit) in enumerate(zip(up_bits[1:], down_bits[1:])):
        up_in = swap(up_send, "rep", up_bit)
        down_in = swap(down_send, "rep", down_bit)
        bias_sum = bias_sum + swap(bias_sum, "rep", up_bit)
        if place < len(far_bits) - 1:
            half = up_keep.shape[0] // 2
            up = up_keep + up_in.astype(F32)
            down = down_keep + down_in.astype(F32)
            up_keep, up_send = up[:half], up[half:].astype(BF16)
            down_keep, down_send = down[:half], down[half:].astype(BF16)
    bit = 1
    while bit < n_table:
        bias_sum = bias_sum + swap(bias_sum, "table", bit)
        bit *= 2
    bias_grad = bias_sum.reshape(-1) * scale
    total, *sends = split_call(
        table_index.reshape(1), up_keep, up_in, down_keep, down_in, n_table, scale
    )
    arrived = [shifted(value, k + 1) for k, value in enumerate(sends)]
    total = functools.reduce(lambda a, b: a + b.astype(F32), arrived, total)
    up_grad, down_grad = total[0], total[1]
    row_grad = rows_call(id_parts, grad_parts)
    return (dense_grad, up_grad, down_grad, bias_grad, row_grad)


def solution(mesh):
    placed = (
        P(("table", "rep"), None),
        P(("table", "rep"), None),
        P(),
        P(),
        P(),
        P(("table", "rep"), None, None),
        P(("table", "rep"), None),
        P(),
    )
    return jax.shard_map(
        body,
        mesh=mesh,
        in_specs=placed,
        out_specs=(
            P(("table", "rep"), None),
            P("rep", "table"),
            P("rep", "table"),
            P(),
            P("rep", "table", None, None),
        ),
        check_vma=False,
    )
```

```python
import functools
import math

import jax
import jax.numpy as jnp
from jax import lax
from jax.experimental import pallas as pl
from jax.experimental.pallas import tpu as pltpu
from jax.sharding import PartitionSpec as P

EMBED_WIDTH = 128
SPARSE_FEATURES = 26
BAG = 4
TABLE_REACH_ROWS = 512
EMPTY = TABLE_REACH_ROWS // 2
BIAS_ROWS = 32
F32 = jnp.float32
BF16 = jnp.bfloat16
MIB = 1024 * 1024
NT = (((1,), (1,)), ((), ()))
ANY = pl.BlockSpec(memory_space=pl.ANY)
VMEM = pl.BlockSpec(memory_space=pltpu.VMEM)
SMEM = pl.BlockSpec(memory_space=pltpu.SMEM)


def params(mib):
    return pltpu.CompilerParams(vmem_limit_bytes=mib * MIB)


def pieces_of(width):
    blocks = width // EMBED_WIDTH
    parts = max(p for p in (3, 2, 1) if blocks % p == 0)
    step = width // parts
    return [(k * step, step) for k in range(parts)]


def fetch(pairs, width, sems):
    copies = {}
    for place, (start, size) in enumerate(pieces_of(width)):
        for which, (source, target) in enumerate(pairs):
            part = pl.ds(start, size)
            copy = pltpu.make_async_copy(
                source.at[:, part], target.at[:, part], sems.at[which, place]
            )
            copy.start()
            copies[which, place] = copy
    return lambda which, place: copies[which, place].wait()


def factors(act, cot, down, up, width, wait):
    hidden = back = None
    for place, (start, size) in enumerate(pieces_of(width)):
        part = slice(start, start + size)
        wait(0, place)
        wait(1, place)
        value = act[:, part]
        term = lax.dot_general(value, down[:, part], NT, preferred_element_type=F32)
        hidden = term if hidden is None else hidden + term
        wait(2, place)
        wait(3, place)
        scaled_b = (cot[:, part].astype(F32) * value.astype(F32)).astype(BF16)
        term = lax.dot_general(scaled_b, up[:, part], NT, preferred_element_type=F32)
        back = term if back is None else back + term
    return hidden.astype(BF16), back.astype(BF16)


def input_kernel(
    n_table, slots, table_ref, owner_ref, act_hbm, cot_hbm, down_hbm, up_hbm, bias_ref, ids_ref, length_ref,
    hidden_ref, back_ref, dense_ref, *rest,
):
    outs = rest[:n_table]
    act, cot, down, up, store, id_store, feature_ref, sems = rest[n_table:]
    tokens, width = act.shape
    wait = fetch(((act_hbm, act), (down_hbm, down), (cot_hbm, cot), (up_hbm, up)), width, sems)
    for place in range(n_table * slots):
        feature_ref[place] = SPARSE_FEATURES
    for feature in range(SPARSE_FEATURES):
        slot = owner_ref[feature]
        shift = lax.rem(lax.div(slot, slots) + n_table - table_ref[0], n_table)
        feature_ref[shift * slots + lax.rem(slot, slots)] = feature
    store[SPARSE_FEATURES + 1] = jnp.zeros(store.shape[1:], BF16)
    id_store[...] = jnp.full(id_store.shape, EMPTY, F32)
    entries = lax.broadcasted_iota(jnp.int32, (BAG, tokens), 0)
    for shift in range(n_table):
        for slot in range(slots):
            feature = feature_ref[shift * slots + slot]
            at = jnp.minimum(feature, SPARSE_FEATURES - 1)
            length = jnp.where(feature < SPARSE_FEATURES, length_ref[pl.ds(at, 1), :], 0)
            ids = jnp.where(entries < length, ids_ref[at] - EMPTY, EMPTY)
            id_store[shift, slot * BAG : (slot + 1) * BAG, :] = ids.astype(F32)
        outs[shift][slots * tokens :, :] = id_store[shift].astype(BF16)
    hidden, back = factors(act, cot, down, up, width, wait)
    hidden_ref[...] = hidden
    back_ref[...] = back
    blocks = 3
    for first in range(0, width // EMBED_WIDTH, blocks):
        part = slice(first * EMBED_WIDTH, (first + blocks) * EMBED_WIDTH)
        mixed = jnp.dot(hidden, up[:, part], preferred_element_type=F32)
        tail = jnp.dot(back, down[:, part], preferred_element_type=F32)
        for k in range(blocks):
            block = first + k
            mine = slice(k * EMBED_WIDTH, (k + 1) * EMBED_WIDTH)
            cols = slice(block * EMBED_WIDTH, (block + 1) * EMBED_WIDTH)
            bias = bias_ref[block : block + 1, :]
            grad = cot[:, cols].astype(F32) * (1.0 + (mixed[:, mine] + bias)) + tail[:, mine]
            store[block] = grad.astype(BF16)
    dense_ref[...] = store[0]
    for shift in range(n_table):
        for slot in range(slots):
            rows = slice(slot * tokens, (slot + 1) * tokens)
            outs[shift][rows, :] = store[feature_ref[shift * slots + slot] + 1]


def input_call(table_index, owners, act, cot, down, up, bias, ids, lengths, n_table, slots):
    tokens, width = act.shape
    rank = down.shape[0]
    id_rows = -(-slots * BAG // 16) * 16
    parts = len(pieces_of(width))
    return pl.pallas_call(
        functools.partial(input_kernel, n_table, slots),
        in_specs=[SMEM, SMEM, ANY, ANY, ANY, ANY, VMEM, VMEM, VMEM],
        out_specs=[VMEM] * (3 + n_table),
        out_shape=[
            jax.ShapeDtypeStruct((tokens, rank), BF16),
            jax.ShapeDtypeStruct((tokens, rank), BF16),
            jax.ShapeDtypeStruct((tokens, EMBED_WIDTH), BF16),
        ]
        + [jax.ShapeDtypeStruct((slots * tokens + id_rows, EMBED_WIDTH), BF16)] * n_table,
        scratch_shapes=[
            pltpu.VMEM((tokens, width), BF16),
            pltpu.VMEM((tokens, width), BF16),
            pltpu.VMEM((rank, width), BF16),
            pltpu.VMEM((rank, width), BF16),
            pltpu.VMEM((SPARSE_FEATURES + 2, tokens, EMBED_WIDTH), BF16),
            pltpu.VMEM((n_table, id_rows, EMBED_WIDTH), F32),
            pltpu.SMEM((n_table * slots,), jnp.int32),
            pltpu.SemaphoreType.DMA((4, parts)),
        ],
        compiler_params=params(60),
        cost_estimate=pl.CostEstimate(
            flops=8 * tokens * rank * width, bytes_accessed=4 * (tokens + rank) * width, transcendentals=0
        ),
    )(table_index, owners, act, cot, down, up, bias, ids, lengths)


def order_matrix(rep_index, rows, size, block, bits):
    out_row = lax.broadcasted_iota(jnp.int32, (rows, size), 0)
    in_row = lax.broadcasted_iota(jnp.int32, (rows, size), 1)
    source = lax.rem(out_row, block)
    position = lax.div(out_row, block)
    for place, bit in enumerate(bits):
        flag = lax.rem(lax.div(position, 1 << (len(bits) - 1 - place)), 2)
        own = lax.rem(lax.div(rep_index, bit), 2)
        source = source + jnp.where(flag == own, 0, bit) * block
    return (source == in_row).astype(F32).astype(BF16)


def bias_terms(value):
    high = value.astype(BF16).astype(F32)
    return high, (value - high).astype(BF16).astype(F32)


def put_bias(ref, width, high, low):
    if ref.shape[0] >= 2 * BIAS_ROWS:
        both = jnp.concatenate([high, low], axis=0).astype(BF16)
        ref[: 2 * BIAS_ROWS, width : width + EMBED_WIDTH] = both
    else:
        ref[:BIAS_ROWS, width : width + EMBED_WIDTH] = high.astype(BF16)
        ref[:BIAS_ROWS, width + EMBED_WIDTH : width + 2 * EMBED_WIDTH] = low.astype(BF16)


def get_bias(ref, width):
    if ref.shape[0] >= 2 * BIAS_ROWS:
        both = ref[: 2 * BIAS_ROWS, width : width + EMBED_WIDTH].astype(F32)
        return both[:BIAS_ROWS] + both[BIAS_ROWS:]
    high = ref[:BIAS_ROWS, width : width + EMBED_WIDTH].astype(F32)
    return high + ref[:BIAS_ROWS, width + EMBED_WIDTH : width + 2 * EMBED_WIDTH].astype(F32)


def extra_columns(rows):
    return EMBED_WIDTH if rows >= 2 * BIAS_ROWS else 2 * EMBED_WIDTH


def terms_kernel(
    ride, up_bits, down_bits, rep_ref, hidden_ref, back_ref, act_hbm, cot_hbm, act_other_hbm, cot_other_hbm,
    down_hbm, up_hbm, up_keep_ref, up_send_ref, down_keep_ref, down_send_ref, bias_ref,
    act, cot, act_other, cot_other, down, up, sems,
):
    tokens, width = act.shape
    rank = down.shape[0]
    wait = fetch(
        (
            (act_other_hbm, act_other), (down_hbm, down), (cot_other_hbm, cot_other), (up_hbm, up),
            (act_hbm, act), (cot_hbm, cot),
        ),
        width,
        sems,
    )
    half, block = rank // 2, rank >> len(up_bits)
    up_order = order_matrix(rep_ref[0], half, rank, block, up_bits)
    down_order = order_matrix(rep_ref[0], half, rank, block, down_bits)
    hidden_other, back_other = factors(act_other, cot_other, down, up, width, wait)
    hidden = jnp.concatenate([hidden_ref[...], hidden_other], axis=0)
    back = jnp.concatenate([back_ref[...], back_other], axis=0)
    hidden = lax.dot_general(up_order, hidden, NT, preferred_element_type=F32).astype(BF16)
    back = lax.dot_general(down_order, back, NT, preferred_element_type=F32).astype(BF16)
    for place in range(len(pieces_of(width))):
        wait(4, place)
        wait(5, place)
    blocks = 3
    keep = half // 2
    if width // EMBED_WIDTH < BIAS_ROWS:
        bias_ref[...] = jnp.zeros_like(bias_ref)
    for first in range(0, width // EMBED_WIDTH, blocks):
        part = slice(first * EMBED_WIDTH, (first + blocks) * EMBED_WIDTH)
        values = jnp.concatenate([act[:, part], act_other[:, part]], axis=0)
        grads = jnp.concatenate([cot[:, part], cot_other[:, part]], axis=0)
        scaled = grads.astype(F32) * values.astype(F32)
        sums = jnp.sum(scaled, axis=0, keepdims=True)
        for k in range(blocks):
            bias_ref[first + k : first + k + 1, :] = sums[:, k * EMBED_WIDTH : (k + 1) * EMBED_WIDTH]
        up_part = jnp.dot(hidden, scaled.astype(BF16), preferred_element_type=F32)
        up_keep_ref[:, part] = up_part[:keep]
        up_send_ref[:, part] = up_part[keep:].astype(BF16)
        down_part = jnp.dot(back, values, preferred_element_type=F32)
        down_keep_ref[:, part] = down_part[:keep]
        down_send_ref[:, part] = down_part[keep:].astype(BF16)
    if ride:
        high, low = bias_terms(bias_ref[...])
        put_bias(up_send_ref, width, high, low)
        bias_ref[...] = high + low


def terms_call(
    rep_index, hidden, back, act, cot, act_other, cot_other, down, up, ride, up_bits, down_bits
):
    tokens, width = act.shape
    rank = down.shape[0]
    rows = rank // 4
    extra = extra_columns(rows) if ride else 0
    parts = len(pieces_of(width))
    wide = pltpu.VMEM((tokens, width), BF16)
    return pl.pallas_call(
        functools.partial(terms_kernel, ride, up_bits, down_bits),
        in_specs=[SMEM, VMEM, VMEM] + [ANY] * 6,
        out_specs=[VMEM] * 5,
        out_shape=[
            jax.ShapeDtypeStruct((rows, width), F32),
            jax.ShapeDtypeStruct((rows, width + extra), BF16),
            jax.ShapeDtypeStruct((rows, width), F32),
            jax.ShapeDtypeStruct((rows, width), BF16),
            jax.ShapeDtypeStruct((BIAS_ROWS, EMBED_WIDTH), F32),
        ],
        scratch_shapes=[
            wide, wide, wide, wide,
            pltpu.VMEM((rank, width), BF16),
            pltpu.VMEM((rank, width), BF16),
            pltpu.SemaphoreType.DMA((6, parts)),
        ],
        compiler_params=params(60),
        cost_estimate=pl.CostEstimate(
            flops=8 * tokens * rank * width, bytes_accessed=8 * tokens * width + 4 * rank * width, transcendentals=0
        ),
    )(rep_index, hidden, back, act, cot, act_other, cot_other, down, up)


def halve_kernel(
    up_keep_ref, up_in_ref, down_keep_ref, down_in_ref, bias_ref,
    up_out_ref, up_send_ref, down_out_ref, down_send_ref, bias_out_ref,
):
    rows, width = up_keep_ref.shape
    half = rows // 2
    up = up_keep_ref[...] + up_in_ref[:, :width].astype(F32)
    up_out_ref[...] = up[:half]
    up_send_ref[:, :width] = up[half:].astype(BF16)
    down = down_keep_ref[...] + down_in_ref[...].astype(F32)
    down_out_ref[...] = down[:half]
    down_send_ref[...] = down[half:].astype(BF16)
    high, low = bias_terms(bias_ref[...] + get_bias(up_in_ref, width))
    put_bias(up_send_ref, width, high, low)
    bias_out_ref[...] = high + low


def halve_call(up_keep, up_in, down_keep, down_in, bias_sum):
    rows, width = up_keep.shape
    half = rows // 2
    return pl.pallas_call(
        halve_kernel,
        in_specs=[VMEM] * 5,
        out_specs=[VMEM] * 5,
        out_shape=[
            jax.ShapeDtypeStruct((half, width), F32),
            jax.ShapeDtypeStruct((half, width + extra_columns(half)), BF16),
            jax.ShapeDtypeStruct((half, width), F32),
            jax.ShapeDtypeStruct((half, width), BF16),
            jax.ShapeDtypeStruct(bias_sum.shape, F32),
        ],
        compiler_params=params(16),
    )(up_keep, up_in, down_keep, down_in, bias_sum)


def split_kernel(
    ride, n_table, scale, table_ref, up_keep_ref, up_in_ref, down_keep_ref, down_in_ref, bias_ref,
    own_ref, bias_out_ref, *rest,
):
    sends, store = rest[: n_table - 1], rest[n_table - 1]
    columns = own_ref.shape[2]
    width = up_keep_ref.shape[1]
    pairs = ((up_keep_ref, up_in_ref), (down_keep_ref, down_in_ref))
    for which, (keep, arrived) in enumerate(pairs):
        total = (keep[...] + arrived[:, :width].astype(F32)) * scale
        for table in range(n_table):
            store[table, which] = total[:, table * columns : (table + 1) * columns]
    own_ref[...] = store[table_ref[0]]
    start = -(-columns // EMBED_WIDTH) * EMBED_WIDTH
    bias = bias_ref[...]
    if ride:
        high, low = bias_terms(bias + get_bias(up_in_ref, width))
        bias = high + low
    bias_out_ref[...] = bias
    for shift in range(1, n_table):
        value = store[lax.rem(table_ref[0] + shift, n_table)].astype(BF16)
        sends[shift - 1][:, :, :columns] = value
        if ride:
            sends[shift - 1][0, :BIAS_ROWS, start:] = high.astype(BF16)
            sends[shift - 1][1, :BIAS_ROWS, start:] = low.astype(BF16)


def split_call(table_index, up_keep, up_in, down_keep, down_in, bias_sum, n_table, scale, ride):
    rows, width = up_keep.shape
    columns = width // n_table
    sent = -(-columns // EMBED_WIDTH) * EMBED_WIDTH + EMBED_WIDTH if ride else columns
    return pl.pallas_call(
        functools.partial(split_kernel, ride, n_table, scale),
        in_specs=[SMEM] + [VMEM] * 5,
        out_specs=[VMEM] * (n_table + 1),
        out_shape=[
            jax.ShapeDtypeStruct((2, rows, columns), F32),
            jax.ShapeDtypeStruct(bias_sum.shape, F32),
        ]
        + [jax.ShapeDtypeStruct((2, rows, sent), BF16)] * (n_table - 1),
        scratch_shapes=[pltpu.VMEM((n_table, 2, rows, columns), F32)],
        compiler_params=params(16),
    )(table_index, up_keep, up_in, down_keep, down_in, bias_sum)


def finish_kernel(ride, n_table, scale, table_ref, own_ref, bias_ref, *rest):
    arrived = rest[: n_table - 1]
    up_ref, down_ref, bias_out_ref, store = rest[n_table - 1 :]
    columns = own_ref.shape[2]
    start = -(-columns // EMBED_WIDTH) * EMBED_WIDTH
    up, down = own_ref[0], own_ref[1]
    store[table_ref[0]] = bias_ref[...]
    for shift in range(1, n_table):
        value = arrived[shift - 1]
        up = up + value[0, :, :columns].astype(F32)
        down = down + value[1, :, :columns].astype(F32)
        if ride:
            source = lax.rem(table_ref[0] + n_table - shift, n_table)
            high = value[0, :BIAS_ROWS, start:].astype(F32)
            store[source] = high + value[1, :BIAS_ROWS, start:].astype(F32)
    up_ref[...] = up
    down_ref[...] = down
    total = bias_ref[...]
    if ride:
        total = store[0]
        for table in range(1, n_table):
            total = total + store[table]
    bias_out_ref[...] = total * scale


def finish_call(table_index, own, bias_sum, arrived, scale, ride):
    n_table = len(arrived) + 1
    _, rows, columns = own.shape
    return pl.pallas_call(
        functools.partial(finish_kernel, ride, n_table, scale),
        in_specs=[SMEM] + [VMEM] * (n_table + 1),
        out_specs=[VMEM] * 3,
        out_shape=[
            jax.ShapeDtypeStruct((rows, columns), F32),
            jax.ShapeDtypeStruct((rows, columns), F32),
            jax.ShapeDtypeStruct(bias_sum.shape, F32),
        ],
        scratch_shapes=[pltpu.VMEM((n_table,) + bias_sum.shape, F32)],
        compiler_params=params(16),
    )(table_index, own, bias_sum, *arrived)


def rows_kernel(n_table, slots, *refs):
    parts, out_ref = refs[:n_table], refs[n_table]
    id_store = refs[n_table + 1]
    tokens = (parts[0].shape[0] - id_store.shape[1]) // slots
    slot = pl.program_id(0)

    @pl.when(slot == 0)
    def _():
        for source in range(n_table):
            ids = parts[source][slots * tokens :, :].astype(F32).astype(jnp.int32)
            id_store[source] = ids + EMPTY

    rows = lax.broadcasted_iota(jnp.int32, (TABLE_REACH_ROWS, tokens), 0)
    counts, grads = [], []
    for source in range(n_table):
        count = jnp.zeros((TABLE_REACH_ROWS, tokens), F32)
        for entry in range(BAG):
            ids = id_store[source, pl.ds(slot * BAG + entry, 1), :]
            count = count + jnp.where(ids == rows, 1.0, 0.0)
        counts.append(count.astype(BF16))
        grads.append(parts[source][pl.ds(pl.multiple_of(slot * tokens, tokens), tokens), :])
    count = jnp.concatenate(counts, axis=1)
    grad = jnp.concatenate(grads, axis=0)
    out_ref[0, 0] = jnp.dot(count, grad, preferred_element_type=F32)


def rows_call(parts, slots):
    n_table = len(parts)
    id_rows = -(-slots * BAG // 16) * 16
    tokens = (parts[0].shape[0] - id_rows) // slots
    whole = pl.BlockSpec(parts[0].shape, lambda i: (0, 0))
    return pl.pallas_call(
        functools.partial(rows_kernel, n_table, slots),
        grid=(slots,),
        in_specs=[whole] * n_table,
        out_specs=pl.BlockSpec((1, 1, TABLE_REACH_ROWS, EMBED_WIDTH), lambda i: (0, i, 0, 0)),
        out_shape=jax.ShapeDtypeStruct((1, slots, TABLE_REACH_ROWS, EMBED_WIDTH), F32),
        scratch_shapes=[pltpu.VMEM((n_table, id_rows, tokens), jnp.int32)],
        compiler_params=params(32),
        cost_estimate=pl.CostEstimate(
            flops=2 * slots * n_table * tokens * TABLE_REACH_ROWS * EMBED_WIDTH,
            bytes_accessed=4 * slots * TABLE_REACH_ROWS * EMBED_WIDTH,
            transcendentals=0,
        ),
    )(*parts)


def body(
    activations, cotangent, down_weight, up_weight, bias, bag_ids, bag_lengths, feature_table_slot
):
    tokens, width = activations.shape
    rank = down_weight.shape[0]
    n_table = lax.axis_size("table")
    n_rep = lax.axis_size("rep")
    slots = (SPARSE_FEATURES + n_table - 1) // n_table
    scale = 1.0 / math.sqrt(tokens * n_table * n_rep)
    table_index = lax.axis_index("table").astype(jnp.int32).reshape(1)
    rep_index = lax.axis_index("rep").astype(jnp.int32).reshape(1)
    far_bits = [1 << k for k in range(1, n_rep.bit_length() - 1)]
    up_bits, down_bits = [1] + far_bits, [1] + far_bits[::-1]
    ride = rank // n_rep >= BIAS_ROWS

    def swap(value, axis, bit):
        size = n_rep if axis == "rep" else n_table
        return lax.ppermute(value, axis, [(k, k ^ bit) for k in range(size)])

    def shifted(value, shift):
        return lax.ppermute(value, "table", [(k, (k + shift) % n_table) for k in range(n_table)])

    act_other = swap(activations, "rep", 1)
    cot_other = swap(cotangent, "rep", 1)
    hidden, back, dense_grad, *parts = input_call(
        table_index, feature_table_slot, activations, cotangent, down_weight, up_weight,
        bias.reshape(-1, EMBED_WIDTH), jnp.transpose(bag_ids, (1, 2, 0)), jnp.transpose(bag_lengths, (1, 0)),
        n_table, slots,
    )
    parts = [parts[0]] + [shifted(parts[k], k) for k in range(1, n_table)]
    up_keep, up_send, down_keep, down_send, bias_sum = terms_call(
        rep_index, hidden, back, activations, cotangent, act_other, cot_other, down_weight, up_weight,
        ride, up_bits, down_bits,
    )
    for place, (up_bit, down_bit) in enumerate(zip(up_bits[1:], down_bits[1:])):
        up_in = swap(up_send, "rep", up_bit)
        down_in = swap(down_send, "rep", down_bit)
        if not ride:
            bias_sum = bias_sum + swap(bias_sum, "rep", up_bit)
        if place == len(far_bits) - 1:
            break
        if ride:
            up_keep, up_send, down_keep, down_send, bias_sum = halve_call(
                up_keep, up_in, down_keep, down_in, bias_sum
            )
        else:
            half = up_keep.shape[0] // 2
            up = up_keep + up_in.astype(F32)
            down = down_keep + down_in.astype(F32)
            up_keep, up_send = up[:half], up[half:].astype(BF16)
            down_keep, down_send = down[:half], down[half:].astype(BF16)
    if not ride:
        for bit in [1 << k for k in range(n_table.bit_length() - 1)]:
            bias_sum = bias_sum + swap(bias_sum, "table", bit)
    own, bias_sum, *sends = split_call(
        table_index, up_keep, up_in, down_keep, down_in, bias_sum, n_table, scale, ride
    )
    arrived = [shifted(value, k + 1) for k, value in enumerate(sends)]
    up_grad, down_grad, bias_grad = finish_call(table_index, own, bias_sum, arrived, scale, ride)
    parts, _ = lax.optimization_barrier((parts, own))
    row_grad = rows_call(parts, slots)
    bias_grad = bias_grad[: width // EMBED_WIDTH].reshape(width)
    return (dense_grad, up_grad, down_grad, bias_grad, row_grad)


def solution(mesh):
    placed = (
        P(("table", "rep"), None),
        P(("table", "rep"), None),
        P(),
        P(),
        P(),
        P(("table", "rep"), None, None),
        P(("table", "rep"), None),
        P(),
    )
    return jax.shard_map(
        body,
        mesh=mesh,
        in_specs=placed,
        out_specs=(
            P(("table", "rep"), None),
            P("rep", "table"),
            P("rep", "table"),
            P(),
            P("rep", "table", None, None),
        ),
        check_vma=False,
    )
```

```python
import functools
import math

import jax
import jax.numpy as jnp
from jax import lax
from jax.experimental import pallas as pl
from jax.experimental.pallas import tpu as pltpu
from jax.sharding import PartitionSpec as P

EMBED_WIDTH = 128
SPARSE_FEATURES = 26
BAG = 4
TABLE_REACH_ROWS = 512
EMPTY = TABLE_REACH_ROWS // 2
BIAS_ROWS = 32
F32 = jnp.float32
BF16 = jnp.bfloat16
MIB = 1024 * 1024
NT = (((1,), (1,)), ((), ()))
ANY = pl.BlockSpec(memory_space=pl.ANY)
VMEM = pl.BlockSpec(memory_space=pltpu.VMEM)
SMEM = pl.BlockSpec(memory_space=pltpu.SMEM)


def params(mib):
    return pltpu.CompilerParams(vmem_limit_bytes=mib * MIB)


def pieces_of(width):
    blocks = width // EMBED_WIDTH
    parts = max(p for p in (9, 3, 1) if blocks % p == 0)
    step = width // parts
    return [(k * step, step) for k in range(parts)]


def order_matrix(rep_index, size, block, bits):
    out_row = lax.broadcasted_iota(jnp.int32, (size, size), 0)
    in_row = lax.broadcasted_iota(jnp.int32, (size, size), 1)
    source = lax.rem(out_row, block)
    position = lax.div(out_row, block)
    for place, bit in enumerate(bits):
        flag = lax.rem(lax.div(position, 1 << (len(bits) - 1 - place)), 2)
        own = lax.rem(lax.div(rep_index, bit), 2)
        source = source + jnp.where(flag == own, 0, bit) * block
    return (source == in_row).astype(F32).astype(BF16)


def input_kernel(
    n_table, slots, up_bits, down_bits, table_ref, rep_ref, owner_ref,
    act_hbm, cot_hbm, down_hbm, up_hbm, bias_ref, ids_ref, length_ref,
    keep_hbm, send_hbm, dense_hbm, *rest,
):
    outs = rest[:n_table]
    act, cot, down, up, keep, send, store, message, id_store, feature_ref, in_sems, out_sems = rest[n_table:]
    tokens, width = act.shape
    rank = down.shape[0]
    half = rank // 2
    pieces = pieces_of(width)
    arrays = ((act_hbm, act), (down_hbm, down), (cot_hbm, cot), (up_hbm, up))
    fetched = []
    for place, (start, size) in enumerate(pieces):
        part = pl.ds(start, size)
        fetched.append(
            [
                pltpu.make_async_copy(source.at[:, part], target.at[:, part], in_sems.at[which, place])
                for which, (source, target) in enumerate(arrays)
            ]
        )
        for copy in fetched[-1]:
            copy.start()
    block = rank >> len(up_bits)
    up_order = order_matrix(rep_ref[0], rank, block, up_bits)
    down_order = order_matrix(rep_ref[0], rank, block, down_bits)
    for place in range(n_table * slots):
        feature_ref[place] = SPARSE_FEATURES
    for feature in range(SPARSE_FEATURES):
        slot = owner_ref[feature]
        shift = lax.rem(lax.div(slot, slots) + n_table - table_ref[0], n_table)
        feature_ref[shift * slots + lax.rem(slot, slots)] = feature
    store[SPARSE_FEATURES + 1] = jnp.zeros(store.shape[1:], BF16)
    id_store[...] = jnp.full(id_store.shape, EMPTY, F32)
    entries = lax.broadcasted_iota(jnp.int32, (BAG, tokens), 0)
    for shift in range(n_table):
        for slot in range(slots):
            feature = feature_ref[shift * slots + slot]
            at = jnp.minimum(feature, SPARSE_FEATURES - 1)
            length = jnp.where(feature < SPARSE_FEATURES, length_ref[pl.ds(at, 1), :], 0)
            ids = jnp.where(entries < length, ids_ref[at] - EMPTY, EMPTY)
            id_store[shift, slot * BAG : (slot + 1) * BAG, :] = ids.astype(F32)
        message[shift, slots * tokens :, :] = id_store[shift].astype(BF16)
    hidden = back = None
    for (start, size), copies in zip(pieces, fetched):
        part = slice(start, start + size)
        for copy in copies:
            copy.wait()
        value = act[:, part]
        term = lax.dot_general(value, down[:, part], NT, preferred_element_type=F32)
        hidden = term if hidden is None else hidden + term
        scaled_b = (cot[:, part].astype(F32) * value.astype(F32)).astype(BF16)
        term = lax.dot_general(scaled_b, up[:, part], NT, preferred_element_type=F32)
        back = term if back is None else back + term
    hidden, back = hidden.astype(BF16), back.astype(BF16)
    rows = lax.dot_general(up_order, hidden, NT, preferred_element_type=F32).astype(BF16)
    keep[0], send[0] = rows[:half], rows[half:]
    rows = lax.dot_general(down_order, back, NT, preferred_element_type=F32).astype(BF16)
    keep[1], send[1] = rows[:half], rows[half:]
    written = [
        pltpu.make_async_copy(send, send_hbm, out_sems.at[0]),
        pltpu.make_async_copy(keep, keep_hbm, out_sems.at[1]),
    ]
    for copy in written:
        copy.start()
    blocks = 3
    for first in range(0, width // EMBED_WIDTH, blocks):
        part = slice(first * EMBED_WIDTH, (first + blocks) * EMBED_WIDTH)
        mixed = jnp.dot(hidden, up[:, part], preferred_element_type=F32)
        tail = jnp.dot(back, down[:, part], preferred_element_type=F32)
        for k in range(blocks):
            place = first + k
            mine = slice(k * EMBED_WIDTH, (k + 1) * EMBED_WIDTH)
            cols = slice(place * EMBED_WIDTH, (place + 1) * EMBED_WIDTH)
            bias = bias_ref[place : place + 1, :]
            grad = cot[:, cols].astype(F32) * (1.0 + (mixed[:, mine] + bias)) + tail[:, mine]
            store[place] = grad.astype(BF16)
    written.append(pltpu.make_async_copy(store.at[0], dense_hbm, out_sems.at[2]))
    written[-1].start()
    for shift in range(n_table):
        for slot in range(slots):
            rows = slice(slot * tokens, (slot + 1) * tokens)
            message[shift, rows, :] = store[feature_ref[shift * slots + slot] + 1]
        written.append(pltpu.make_async_copy(message.at[shift], outs[shift], out_sems.at[3 + shift]))
        written[-1].start()
    for copy in written:
        copy.wait()


def input_call(
    table_index, rep_index, owners, act, cot, down, up, bias, ids, lengths, n_table, slots, up_bits, down_bits
):
    tokens, width = act.shape
    rank = down.shape[0]
    id_rows = -(-slots * BAG // 16) * 16
    sent = slots * tokens + id_rows
    return pl.pallas_call(
        functools.partial(input_kernel, n_table, slots, up_bits, down_bits),
        in_specs=[SMEM, SMEM, SMEM, ANY, ANY, ANY, ANY, VMEM, VMEM, VMEM],
        out_specs=[ANY] * (3 + n_table),
        out_shape=[
            jax.ShapeDtypeStruct((2, rank // 2, tokens), BF16),
            jax.ShapeDtypeStruct((2, rank // 2, tokens), BF16),
            jax.ShapeDtypeStruct((tokens, EMBED_WIDTH), BF16),
        ]
        + [jax.ShapeDtypeStruct((sent, EMBED_WIDTH), BF16)] * n_table,
        scratch_shapes=[
            pltpu.VMEM((tokens, width), BF16),
            pltpu.VMEM((tokens, width), BF16),
            pltpu.VMEM((rank, width), BF16),
            pltpu.VMEM((rank, width), BF16),
            pltpu.VMEM((2, rank // 2, tokens), BF16),
            pltpu.VMEM((2, rank // 2, tokens), BF16),
            pltpu.VMEM((SPARSE_FEATURES + 2, tokens, EMBED_WIDTH), BF16),
            pltpu.VMEM((n_table, sent, EMBED_WIDTH), BF16),
            pltpu.VMEM((n_table, id_rows, EMBED_WIDTH), F32),
            pltpu.SMEM((n_table * slots,), jnp.int32),
            pltpu.SemaphoreType.DMA((4, len(pieces_of(width)))),
            pltpu.SemaphoreType.DMA((3 + n_table,)),
        ],
        compiler_params=params(60),
        cost_estimate=pl.CostEstimate(
            flops=8 * tokens * rank * width, bytes_accessed=4 * (tokens + rank) * width, transcendentals=0
        ),
    )(table_index, rep_index, owners, act, cot, down, up, bias, ids, lengths)


def bias_terms(value):
    high = value.astype(BF16).astype(F32)
    return high, (value - high).astype(BF16).astype(F32)


def put_bias(ref, width, high, low):
    if ref.shape[0] >= 2 * BIAS_ROWS:
        both = jnp.concatenate([high, low], axis=0).astype(BF16)
        ref[: 2 * BIAS_ROWS, width : width + EMBED_WIDTH] = both
    else:
        ref[:BIAS_ROWS, width : width + EMBED_WIDTH] = high.astype(BF16)
        ref[:BIAS_ROWS, width + EMBED_WIDTH : width + 2 * EMBED_WIDTH] = low.astype(BF16)


def get_bias(ref, width):
    if ref.shape[0] >= 2 * BIAS_ROWS:
        both = ref[: 2 * BIAS_ROWS, width : width + EMBED_WIDTH].astype(F32)
        return both[:BIAS_ROWS] + both[BIAS_ROWS:]
    high = ref[:BIAS_ROWS, width : width + EMBED_WIDTH].astype(F32)
    return high + ref[:BIAS_ROWS, width + EMBED_WIDTH : width + 2 * EMBED_WIDTH].astype(F32)


def extra_columns(rows):
    return EMBED_WIDTH if rows >= 2 * BIAS_ROWS else 2 * EMBED_WIDTH


def terms_kernel(
    ride, keep_ref, other_ref, act, cot, act_other, cot_other,
    up_keep_ref, up_send_ref, down_keep_ref, down_send_ref, bias_ref,
):
    width = act.shape[1]
    hidden = jnp.concatenate([keep_ref[0], other_ref[0]], axis=1)
    back = jnp.concatenate([keep_ref[1], other_ref[1]], axis=1)
    blocks = 3
    keep = hidden.shape[0] // 2
    bias_ref[...] = jnp.zeros_like(bias_ref)
    for first in range(0, width // EMBED_WIDTH, blocks):
        part = slice(first * EMBED_WIDTH, (first + blocks) * EMBED_WIDTH)
        values = jnp.concatenate([act[:, part], act_other[:, part]], axis=0)
        grads = jnp.concatenate([cot[:, part], cot_other[:, part]], axis=0)
        scaled = grads.astype(F32) * values.astype(F32)
        sums = jnp.sum(scaled, axis=0, keepdims=True)
        for k in range(blocks):
            bias_ref[first + k : first + k + 1, :] = sums[:, k * EMBED_WIDTH : (k + 1) * EMBED_WIDTH]
        up_part = jnp.dot(hidden, scaled.astype(BF16), preferred_element_type=F32)
        up_keep_ref[:, part] = up_part[:keep]
        up_send_ref[:, part] = up_part[keep:].astype(BF16)
        down_part = jnp.dot(back, values, preferred_element_type=F32)
        down_keep_ref[:, part] = down_part[:keep]
        down_send_ref[:, part] = down_part[keep:].astype(BF16)
    if ride:
        high, low = bias_terms(bias_ref[...])
        put_bias(up_send_ref, width, high, low)
        bias_ref[...] = high + low


def terms_call(keep, other, act, cot, act_other, cot_other, ride):
    tokens, width = act.shape
    rows = keep.shape[1] // 2
    extra = extra_columns(rows) if ride else 0
    return pl.pallas_call(
        functools.partial(terms_kernel, ride),
        in_specs=[VMEM] * 6,
        out_specs=[VMEM] * 5,
        out_shape=[
            jax.ShapeDtypeStruct((rows, width), F32),
            jax.ShapeDtypeStruct((rows, width + extra), BF16),
            jax.ShapeDtypeStruct((rows, width), F32),
            jax.ShapeDtypeStruct((rows, width), BF16),
            jax.ShapeDtypeStruct((BIAS_ROWS, EMBED_WIDTH), F32),
        ],
        compiler_params=params(16),
        cost_estimate=pl.CostEstimate(
            flops=16 * tokens * rows * width, bytes_accessed=8 * tokens * width + 12 * rows * width, transcendentals=0
        ),
    )(keep, other, act, cot, act_other, cot_other)


def halve_kernel(
    up_keep_ref, up_in_ref, down_keep_ref, down_in_ref, bias_ref,
    up_out_ref, up_send_ref, down_out_ref, down_send_ref, bias_out_ref,
):
    rows, width = up_keep_ref.shape
    half = rows // 2
    up = up_keep_ref[...] + up_in_ref[:, :width].astype(F32)
    up_out_ref[...] = up[:half]
    up_send_ref[:, :width] = up[half:].astype(BF16)
    down = down_keep_ref[...] + down_in_ref[...].astype(F32)
    down_out_ref[...] = down[:half]
    down_send_ref[...] = down[half:].astype(BF16)
    high, low = bias_terms(bias_ref[...] + get_bias(up_in_ref, width))
    put_bias(up_send_ref, width, high, low)
    bias_out_ref[...] = high + low


def halve_call(up_keep, up_in, down_keep, down_in, bias_sum):
    rows, width = up_keep.shape
    half = rows // 2
    return pl.pallas_call(
        halve_kernel,
        in_specs=[VMEM] * 5,
        out_specs=[VMEM] * 5,
        out_shape=[
            jax.ShapeDtypeStruct((half, width), F32),
            jax.ShapeDtypeStruct((half, width + extra_columns(half)), BF16),
            jax.ShapeDtypeStruct((half, width), F32),
            jax.ShapeDtypeStruct((half, width), BF16),
            jax.ShapeDtypeStruct(bias_sum.shape, F32),
        ],
        compiler_params=params(16),
    )(up_keep, up_in, down_keep, down_in, bias_sum)


def split_kernel(
    ride, n_table, scale, table_ref, up_keep_ref, up_in_ref, down_keep_ref, down_in_ref, bias_ref,
    own_ref, bias_out_ref, *rest,
):
    sends, store = rest[: n_table - 1], rest[n_table - 1]
    columns = own_ref.shape[2]
    width = up_keep_ref.shape[1]
    pairs = ((up_keep_ref, up_in_ref), (down_keep_ref, down_in_ref))
    for which, (keep, arrived) in enumerate(pairs):
        total = (keep[...] + arrived[:, :width].astype(F32)) * scale
        for table in range(n_table):
            store[table, which] = total[:, table * columns : (table + 1) * columns]
    own_ref[...] = store[table_ref[0]]
    start = -(-columns // EMBED_WIDTH) * EMBED_WIDTH
    bias = bias_ref[...]
    if ride:
        high, low = bias_terms(bias + get_bias(up_in_ref, width))
        bias = high + low
    bias_out_ref[...] = bias
    for shift in range(1, n_table):
        value = store[lax.rem(table_ref[0] + shift, n_table)].astype(BF16)
        sends[shift - 1][:, :, :columns] = value
        if ride:
            sends[shift - 1][0, :BIAS_ROWS, start:] = high.astype(BF16)
            sends[shift - 1][1, :BIAS_ROWS, start:] = low.astype(BF16)


def split_call(table_index, up_keep, up_in, down_keep, down_in, bias_sum, n_table, scale, ride):
    rows, width = up_keep.shape
    columns = width // n_table
    sent = -(-columns // EMBED_WIDTH) * EMBED_WIDTH + EMBED_WIDTH if ride else columns
    return pl.pallas_call(
        functools.partial(split_kernel, ride, n_table, scale),
        in_specs=[SMEM] + [VMEM] * 5,
        out_specs=[VMEM] * (n_table + 1),
        out_shape=[
            jax.ShapeDtypeStruct((2, rows, columns), F32),
            jax.ShapeDtypeStruct(bias_sum.shape, F32),
        ]
        + [jax.ShapeDtypeStruct((2, rows, sent), BF16)] * (n_table - 1),
        scratch_shapes=[pltpu.VMEM((n_table, 2, rows, columns), F32)],
        compiler_params=params(16),
    )(table_index, up_keep, up_in, down_keep, down_in, bias_sum)


def finish_kernel(ride, n_table, scale, table_ref, own_ref, bias_ref, *rest):
    arrived = rest[: n_table - 1]
    up_ref, down_ref, bias_out_ref, store = rest[n_table - 1 :]
    columns = own_ref.shape[2]
    start = -(-columns // EMBED_WIDTH) * EMBED_WIDTH
    up, down = own_ref[0], own_ref[1]
    store[table_ref[0]] = bias_ref[...]
    for shift in range(1, n_table):
        value = arrived[shift - 1]
        up = up + value[0, :, :columns].astype(F32)
        down = down + value[1, :, :columns].astype(F32)
        if ride:
            source = lax.rem(table_ref[0] + n_table - shift, n_table)
            high = value[0, :BIAS_ROWS, start:].astype(F32)
            store[source] = high + value[1, :BIAS_ROWS, start:].astype(F32)
    up_ref[...] = up
    down_ref[...] = down
    total = bias_ref[...]
    if ride:
        total = store[0]
        for table in range(1, n_table):
            total = total + store[table]
    bias_out_ref[...] = total[: bias_out_ref.shape[0]] * scale


def finish_call(table_index, own, bias_sum, arrived, scale, ride):
    n_table = len(arrived) + 1
    _, rows, columns = own.shape
    return pl.pallas_call(
        functools.partial(finish_kernel, ride, n_table, scale),
        in_specs=[SMEM] + [VMEM] * (n_table + 1),
        out_specs=[VMEM] * 3,
        out_shape=[
            jax.ShapeDtypeStruct((rows, columns), F32),
            jax.ShapeDtypeStruct((rows, columns), F32),
            jax.ShapeDtypeStruct((columns * n_table // EMBED_WIDTH, EMBED_WIDTH), F32),
        ],
        scratch_shapes=[pltpu.VMEM((n_table,) + bias_sum.shape, F32)],
        compiler_params=params(16),
    )(table_index, own, bias_sum, *arrived)


def rows_kernel(n_table, slots, *refs):
    parts, out_ref = refs[:n_table], refs[n_table]
    id_store = refs[n_table + 1]
    tokens = (parts[0].shape[0] - id_store.shape[1]) // slots
    slot = pl.program_id(0)

    @pl.when(slot == 0)
    def _():
        for source in range(n_table):
            ids = parts[source][slots * tokens :, :].astype(F32).astype(jnp.int32)
            id_store[source] = ids + EMPTY

    rows = lax.broadcasted_iota(jnp.int32, (TABLE_REACH_ROWS, tokens), 0)
    counts, grads = [], []
    for source in range(n_table):
        count = jnp.zeros((TABLE_REACH_ROWS, tokens), F32)
        for entry in range(BAG):
            ids = id_store[source, pl.ds(slot * BAG + entry, 1), :]
            count = count + jnp.where(ids == rows, 1.0, 0.0)
        counts.append(count.astype(BF16))
        grads.append(parts[source][pl.ds(pl.multiple_of(slot * tokens, tokens), tokens), :])
    count = jnp.concatenate(counts, axis=1)
    grad = jnp.concatenate(grads, axis=0)
    out_ref[0, 0] = jnp.dot(count, grad, preferred_element_type=F32)


def rows_call(parts, slots):
    n_table = len(parts)
    id_rows = -(-slots * BAG // 16) * 16
    tokens = (parts[0].shape[0] - id_rows) // slots
    whole = pl.BlockSpec(parts[0].shape, lambda i: (0, 0))
    return pl.pallas_call(
        functools.partial(rows_kernel, n_table, slots),
        grid=(slots,),
        in_specs=[whole] * n_table,
        out_specs=pl.BlockSpec((1, 1, TABLE_REACH_ROWS, EMBED_WIDTH), lambda i: (0, i, 0, 0)),
        out_shape=jax.ShapeDtypeStruct((1, slots, TABLE_REACH_ROWS, EMBED_WIDTH), F32),
        scratch_shapes=[pltpu.VMEM((n_table, id_rows, tokens), jnp.int32)],
        compiler_params=params(16),
        cost_estimate=pl.CostEstimate(
            flops=2 * slots * n_table * tokens * TABLE_REACH_ROWS * EMBED_WIDTH,
            bytes_accessed=4 * slots * TABLE_REACH_ROWS * EMBED_WIDTH,
            transcendentals=0,
        ),
    )(*parts)


def body(
    activations, cotangent, down_weight, up_weight, bias, bag_ids, bag_lengths, feature_table_slot
):
    tokens, width = activations.shape
    rank = down_weight.shape[0]
    n_table = lax.axis_size("table")
    n_rep = lax.axis_size("rep")
    slots = (SPARSE_FEATURES + n_table - 1) // n_table
    scale = 1.0 / math.sqrt(tokens * n_table * n_rep)
    table_index = lax.axis_index("table").astype(jnp.int32).reshape(1)
    rep_index = lax.axis_index("rep").astype(jnp.int32).reshape(1)
    far_bits = [1 << k for k in range(1, n_rep.bit_length() - 1)]
    up_bits, down_bits = [1] + far_bits, [1] + far_bits[::-1]
    ride = rank // n_rep >= BIAS_ROWS

    def swap(value, axis, bit):
        size = n_rep if axis == "rep" else n_table
        return lax.ppermute(value, axis, [(k, k ^ bit) for k in range(size)])

    def shifted(value, shift):
        return lax.ppermute(value, "table", [(k, (k + shift) % n_table) for k in range(n_table)])

    act_other = swap(activations, "rep", 1)
    cot_other = swap(cotangent, "rep", 1)
    keep, send, dense_grad, *parts = input_call(
        table_index, rep_index, feature_table_slot, activations, cotangent, down_weight, up_weight,
        bias.reshape(-1, EMBED_WIDTH), jnp.transpose(bag_ids, (1, 2, 0)), jnp.transpose(bag_lengths, (1, 0)),
        n_table, slots, up_bits, down_bits,
    )
    other = swap(send, "rep", 1)
    parts = [parts[0]] + [shifted(parts[k], k) for k in range(1, n_table)]
    up_keep, up_send, down_keep, down_send, bias_sum = terms_call(
        keep, other, activations, cotangent, act_other, cot_other, ride
    )
    for place, (up_bit, down_bit) in enumerate(zip(up_bits[1:], down_bits[1:])):
        up_in = swap(up_send, "rep", up_bit)
        down_in = swap(down_send, "rep", down_bit)
        if not ride:
            bias_sum = bias_sum + swap(bias_sum, "rep", up_bit)
        if place == len(far_bits) - 1:
            break
        if ride:
            up_keep, up_send, down_keep, down_send, bias_sum = halve_call(
                up_keep, up_in, down_keep, down_in, bias_sum
            )
        else:
            half = up_keep.shape[0] // 2
            up = up_keep + up_in.astype(F32)
            down = down_keep + down_in.astype(F32)
            up_keep, up_send = up[:half], up[half:].astype(BF16)
            down_keep, down_send = down[:half], down[half:].astype(BF16)
    if not ride:
        for bit in [1 << k for k in range(n_table.bit_length() - 1)]:
            bias_sum = bias_sum + swap(bias_sum, "table", bit)
    (up_in, down_in), parts = lax.optimization_barrier(((up_in, down_in), parts))
    own, bias_sum, *sends = split_call(
        table_index, up_keep, up_in, down_keep, down_in, bias_sum, n_table, scale, ride
    )
    arrived = [shifted(value, k + 1) for k, value in enumerate(sends)]
    up_grad, down_grad, bias_grad = finish_call(table_index, own, bias_sum, arrived, scale, ride)
    parts, _ = lax.optimization_barrier((parts, own))
    row_grad = rows_call(parts, slots)
    bias_grad = bias_grad.reshape(width)
    return (dense_grad, up_grad, down_grad, bias_grad, row_grad)


def solution(mesh):
    placed = (
        P(("table", "rep"), None),
        P(("table", "rep"), None),
        P(),
        P(),
        P(),
        P(("table", "rep"), None, None),
        P(("table", "rep"), None),
        P(),
    )
    return jax.shard_map(
        body,
        mesh=mesh,
        in_specs=placed,
        out_specs=(
            P(("table", "rep"), None),
            P("rep", "table"),
            P("rep", "table"),
            P(),
            P("rep", "table", None, None),
        ),
        check_vma=False,
    )
```

```python
import functools
import math

import jax
import jax.numpy as jnp
from jax import lax
from jax.experimental import pallas as pl
from jax.experimental.pallas import tpu as pltpu
from jax.sharding import PartitionSpec as P

EMBED_WIDTH = 128
SPARSE_FEATURES = 26
BAG = 4
TABLE_REACH_ROWS = 512
EMPTY = TABLE_REACH_ROWS // 2
BIAS_ROWS = 32
F32 = jnp.float32
BF16 = jnp.bfloat16
MIB = 1024 * 1024
NT = (((1,), (1,)), ((), ()))
ANY = pl.BlockSpec(memory_space=pl.ANY)
VMEM = pl.BlockSpec(memory_space=pltpu.VMEM)
SMEM = pl.BlockSpec(memory_space=pltpu.SMEM)


def params(mib):
    return pltpu.CompilerParams(vmem_limit_bytes=mib * MIB)


def pieces_of(width):
    blocks = width // EMBED_WIDTH
    parts = max(p for p in (9, 3, 1) if blocks % p == 0)
    step = width // parts
    return [(k * step, step) for k in range(parts)]


def order_matrix(rep_index, size, block, bits):
    out_row = lax.broadcasted_iota(jnp.int32, (size, size), 0)
    in_row = lax.broadcasted_iota(jnp.int32, (size, size), 1)
    source = lax.rem(out_row, block)
    position = lax.div(out_row, block)
    for place, bit in enumerate(bits):
        flag = lax.rem(lax.div(position, 1 << (len(bits) - 1 - place)), 2)
        own = lax.rem(lax.div(rep_index, bit), 2)
        source = source + jnp.where(flag == own, 0, bit) * block
    return (source == in_row).astype(F32).astype(BF16)


def input_kernel(
    n_table, slots, up_bits, down_bits, table_ref, rep_ref, owner_ref,
    act_hbm, cot_hbm, down_hbm, up_hbm, bias_ref, ids_ref, length_ref,
    keep_hbm, send_hbm, dense_hbm, *rest,
):
    outs = rest[:n_table]
    act, cot, down, up, keep, send, store, message, id_store, feature_ref, in_sems, out_sems = rest[n_table:]
    tokens, width = act.shape
    rank = down.shape[0]
    half = rank // 2
    pieces = pieces_of(width)
    arrays = ((act_hbm, act), (down_hbm, down), (cot_hbm, cot), (up_hbm, up))
    fetched = []
    for place, (start, size) in enumerate(pieces):
        part = pl.ds(start, size)
        fetched.append(
            [
                pltpu.make_async_copy(source.at[:, part], target.at[:, part], in_sems.at[which, place])
                for which, (source, target) in enumerate(arrays)
            ]
        )
        for copy in fetched[-1]:
            copy.start()
    block = rank >> len(up_bits)
    up_order = order_matrix(rep_ref[0], rank, block, up_bits)
    down_order = order_matrix(rep_ref[0], rank, block, down_bits)
    for place in range(n_table * slots):
        feature_ref[place] = SPARSE_FEATURES
    for feature in range(SPARSE_FEATURES):
        slot = owner_ref[feature]
        shift = lax.rem(lax.div(slot, slots) + n_table - table_ref[0], n_table)
        feature_ref[shift * slots + lax.rem(slot, slots)] = feature
    store[SPARSE_FEATURES + 1] = jnp.zeros(store.shape[1:], BF16)
    id_store[...] = jnp.full(id_store.shape, EMPTY, F32)
    entries = lax.broadcasted_iota(jnp.int32, (BAG, tokens), 0)
    for shift in range(n_table):
        for slot in range(slots):
            feature = feature_ref[shift * slots + slot]
            at = jnp.minimum(feature, SPARSE_FEATURES - 1)
            length = jnp.where(feature < SPARSE_FEATURES, length_ref[pl.ds(at, 1), :], 0)
            ids = jnp.where(entries < length, ids_ref[at] - EMPTY, EMPTY)
            id_store[shift, slot * BAG : (slot + 1) * BAG, :] = ids.astype(F32)
        message[shift, slots * tokens :, :] = id_store[shift].astype(BF16)
    hidden = back = None
    for (start, size), copies in zip(pieces, fetched):
        part = slice(start, start + size)
        for copy in copies:
            copy.wait()
        value = act[:, part]
        term = lax.dot_general(value, down[:, part], NT, preferred_element_type=F32)
        hidden = term if hidden is None else hidden + term
        scaled_b = (cot[:, part].astype(F32) * value.astype(F32)).astype(BF16)
        term = lax.dot_general(scaled_b, up[:, part], NT, preferred_element_type=F32)
        back = term if back is None else back + term
    hidden, back = hidden.astype(BF16), back.astype(BF16)
    rows = lax.dot_general(up_order, hidden, NT, preferred_element_type=F32).astype(BF16)
    keep[0], send[0] = rows[:half], rows[half:]
    rows = lax.dot_general(down_order, back, NT, preferred_element_type=F32).astype(BF16)
    keep[1], send[1] = rows[:half], rows[half:]
    written = [
        pltpu.make_async_copy(send, send_hbm, out_sems.at[0]),
        pltpu.make_async_copy(keep, keep_hbm, out_sems.at[1]),
    ]
    for copy in written:
        copy.start()
    blocks = 3
    for first in range(0, width // EMBED_WIDTH, blocks):
        part = slice(first * EMBED_WIDTH, (first + blocks) * EMBED_WIDTH)
        mixed = jnp.dot(hidden, up[:, part], preferred_element_type=F32)
        tail = jnp.dot(back, down[:, part], preferred_element_type=F32)
        for k in range(blocks):
            place = first + k
            mine = slice(k * EMBED_WIDTH, (k + 1) * EMBED_WIDTH)
            cols = slice(place * EMBED_WIDTH, (place + 1) * EMBED_WIDTH)
            bias = bias_ref[place : place + 1, :]
            grad = cot[:, cols].astype(F32) * (1.0 + (mixed[:, mine] + bias)) + tail[:, mine]
            store[place] = grad.astype(BF16)
    written.append(pltpu.make_async_copy(store.at[0], dense_hbm, out_sems.at[2]))
    written[-1].start()
    for shift in range(n_table):
        for slot in range(slots):
            rows = slice(slot * tokens, (slot + 1) * tokens)
            message[shift, rows, :] = store[feature_ref[shift * slots + slot] + 1]
        written.append(pltpu.make_async_copy(message.at[shift], outs[shift], out_sems.at[3 + shift]))
        written[-1].start()
    for copy in written:
        copy.wait()


def input_call(
    table_index, rep_index, owners, act, cot, down, up, bias, ids, lengths, n_table, slots, up_bits, down_bits
):
    tokens, width = act.shape
    rank = down.shape[0]
    id_rows = -(-slots * BAG // 16) * 16
    sent = slots * tokens + id_rows
    return pl.pallas_call(
        functools.partial(input_kernel, n_table, slots, up_bits, down_bits),
        in_specs=[SMEM, SMEM, SMEM, ANY, ANY, ANY, ANY, VMEM, VMEM, VMEM],
        out_specs=[ANY] * (3 + n_table),
        out_shape=[
            jax.ShapeDtypeStruct((2, rank // 2, tokens), BF16),
            jax.ShapeDtypeStruct((2, rank // 2, tokens), BF16),
            jax.ShapeDtypeStruct((tokens, EMBED_WIDTH), BF16),
        ]
        + [jax.ShapeDtypeStruct((sent, EMBED_WIDTH), BF16)] * n_table,
        scratch_shapes=[
            pltpu.VMEM((tokens, width), BF16),
            pltpu.VMEM((tokens, width), BF16),
            pltpu.VMEM((rank, width), BF16),
            pltpu.VMEM((rank, width), BF16),
            pltpu.VMEM((2, rank // 2, tokens), BF16),
            pltpu.VMEM((2, rank // 2, tokens), BF16),
            pltpu.VMEM((SPARSE_FEATURES + 2, tokens, EMBED_WIDTH), BF16),
            pltpu.VMEM((n_table, sent, EMBED_WIDTH), BF16),
            pltpu.VMEM((n_table, id_rows, EMBED_WIDTH), F32),
            pltpu.SMEM((n_table * slots,), jnp.int32),
            pltpu.SemaphoreType.DMA((4, len(pieces_of(width)))),
            pltpu.SemaphoreType.DMA((3 + n_table,)),
        ],
        compiler_params=params(60),
        cost_estimate=pl.CostEstimate(
            flops=8 * tokens * rank * width, bytes_accessed=4 * (tokens + rank) * width, transcendentals=0
        ),
    )(table_index, rep_index, owners, act, cot, down, up, bias, ids, lengths)


def bias_terms(value):
    high = value.astype(BF16).astype(F32)
    return high, (value - high).astype(BF16).astype(F32)


def put_bias(ref, width, high, low):
    if ref.shape[0] >= 2 * BIAS_ROWS:
        both = jnp.concatenate([high, low], axis=0).astype(BF16)
        ref[: 2 * BIAS_ROWS, width : width + EMBED_WIDTH] = both
    else:
        ref[:BIAS_ROWS, width : width + EMBED_WIDTH] = high.astype(BF16)
        ref[:BIAS_ROWS, width + EMBED_WIDTH : width + 2 * EMBED_WIDTH] = low.astype(BF16)


def get_bias(ref, width):
    if ref.shape[0] >= 2 * BIAS_ROWS:
        both = ref[: 2 * BIAS_ROWS, width : width + EMBED_WIDTH].astype(F32)
        return both[:BIAS_ROWS] + both[BIAS_ROWS:]
    high = ref[:BIAS_ROWS, width : width + EMBED_WIDTH].astype(F32)
    return high + ref[:BIAS_ROWS, width + EMBED_WIDTH : width + 2 * EMBED_WIDTH].astype(F32)


def extra_columns(rows):
    return EMBED_WIDTH if rows >= 2 * BIAS_ROWS else 2 * EMBED_WIDTH


def terms_kernel(
    ride, keep_ref, other_ref, act, cot, act_other, cot_other,
    up_keep_ref, up_send_ref, down_keep_ref, down_send_ref, bias_ref,
):
    width = act.shape[1]
    hidden = jnp.concatenate([keep_ref[0], other_ref[0]], axis=1)
    back = jnp.concatenate([keep_ref[1], other_ref[1]], axis=1)
    blocks = 3
    keep = hidden.shape[0] // 2
    bias_ref[...] = jnp.zeros_like(bias_ref)
    for first in range(0, width // EMBED_WIDTH, blocks):
        part = slice(first * EMBED_WIDTH, (first + blocks) * EMBED_WIDTH)
        values = jnp.concatenate([act[:, part], act_other[:, part]], axis=0)
        grads = jnp.concatenate([cot[:, part], cot_other[:, part]], axis=0)
        scaled = grads.astype(F32) * values.astype(F32)
        sums = jnp.sum(scaled, axis=0, keepdims=True)
        for k in range(blocks):
            bias_ref[first + k : first + k + 1, :] = sums[:, k * EMBED_WIDTH : (k + 1) * EMBED_WIDTH]
        up_part = jnp.dot(hidden, scaled.astype(BF16), preferred_element_type=F32)
        up_keep_ref[:, part] = up_part[:keep]
        up_send_ref[:, part] = up_part[keep:].astype(BF16)
        down_part = jnp.dot(back, values, preferred_element_type=F32)
        down_keep_ref[:, part] = down_part[:keep]
        down_send_ref[:, part] = down_part[keep:].astype(BF16)
    if ride:
        high, low = bias_terms(bias_ref[...])
        put_bias(up_send_ref, width, high, low)
        bias_ref[...] = high + low


def terms_call(keep, other, act, cot, act_other, cot_other, ride):
    tokens, width = act.shape
    rows = keep.shape[1] // 2
    extra = extra_columns(rows) if ride else 0
    return pl.pallas_call(
        functools.partial(terms_kernel, ride),
        in_specs=[VMEM] * 6,
        out_specs=[VMEM] * 5,
        out_shape=[
            jax.ShapeDtypeStruct((rows, width), F32),
            jax.ShapeDtypeStruct((rows, width + extra), BF16),
            jax.ShapeDtypeStruct((rows, width), F32),
            jax.ShapeDtypeStruct((rows, width), BF16),
            jax.ShapeDtypeStruct((BIAS_ROWS, EMBED_WIDTH), F32),
        ],
        compiler_params=params(16),
        cost_estimate=pl.CostEstimate(
            flops=16 * tokens * rows * width, bytes_accessed=8 * tokens * width + 12 * rows * width, transcendentals=0
        ),
    )(keep, other, act, cot, act_other, cot_other)


def halve_kernel(
    up_keep_ref, up_in_ref, down_keep_ref, down_in_ref, bias_ref,
    up_out_ref, up_send_ref, down_out_ref, down_send_ref, bias_out_ref,
):
    rows, width = up_keep_ref.shape
    half = rows // 2
    up = up_keep_ref[...] + up_in_ref[:, :width].astype(F32)
    up_out_ref[...] = up[:half]
    up_send_ref[:, :width] = up[half:].astype(BF16)
    down = down_keep_ref[...] + down_in_ref[...].astype(F32)
    down_out_ref[...] = down[:half]
    down_send_ref[...] = down[half:].astype(BF16)
    high, low = bias_terms(bias_ref[...] + get_bias(up_in_ref, width))
    put_bias(up_send_ref, width, high, low)
    bias_out_ref[...] = high + low


def halve_call(up_keep, up_in, down_keep, down_in, bias_sum):
    rows, width = up_keep.shape
    half = rows // 2
    return pl.pallas_call(
        halve_kernel,
        in_specs=[VMEM] * 5,
        out_specs=[VMEM] * 5,
        out_shape=[
            jax.ShapeDtypeStruct((half, width), F32),
            jax.ShapeDtypeStruct((half, width + extra_columns(half)), BF16),
            jax.ShapeDtypeStruct((half, width), F32),
            jax.ShapeDtypeStruct((half, width), BF16),
            jax.ShapeDtypeStruct(bias_sum.shape, F32),
        ],
        compiler_params=params(16),
    )(up_keep, up_in, down_keep, down_in, bias_sum)


def split_kernel(
    ride, n_table, scale, table_ref, up_keep_ref, up_in_ref, down_keep_ref, down_in_ref, bias_ref,
    own_ref, bias_out_ref, *rest,
):
    sends, store = rest[: n_table - 1], rest[n_table - 1]
    columns = own_ref.shape[2]
    width = up_keep_ref.shape[1]
    pairs = ((up_keep_ref, up_in_ref), (down_keep_ref, down_in_ref))
    for which, (keep, arrived) in enumerate(pairs):
        total = (keep[...] + arrived[:, :width].astype(F32)) * scale
        for table in range(n_table):
            store[table, which] = total[:, table * columns : (table + 1) * columns]
    own_ref[...] = store[table_ref[0]]
    start = -(-columns // EMBED_WIDTH) * EMBED_WIDTH
    bias = bias_ref[...]
    if ride:
        high, low = bias_terms(bias + get_bias(up_in_ref, width))
        bias = high + low
    bias_out_ref[...] = bias
    for shift in range(1, n_table):
        value = store[lax.rem(table_ref[0] + shift, n_table)].astype(BF16)
        sends[shift - 1][:, :, :columns] = value
        if ride:
            sends[shift - 1][0, :BIAS_ROWS, start:] = high.astype(BF16)
            sends[shift - 1][1, :BIAS_ROWS, start:] = low.astype(BF16)


def split_call(table_index, up_keep, up_in, down_keep, down_in, bias_sum, n_table, scale, ride):
    rows, width = up_keep.shape
    columns = width // n_table
    sent = -(-columns // EMBED_WIDTH) * EMBED_WIDTH + EMBED_WIDTH if ride else columns
    return pl.pallas_call(
        functools.partial(split_kernel, ride, n_table, scale),
        in_specs=[SMEM] + [VMEM] * 5,
        out_specs=[VMEM] * (n_table + 1),
        out_shape=[
            jax.ShapeDtypeStruct((2, rows, columns), F32),
            jax.ShapeDtypeStruct(bias_sum.shape, F32),
        ]
        + [jax.ShapeDtypeStruct((2, rows, sent), BF16)] * (n_table - 1),
        scratch_shapes=[pltpu.VMEM((n_table, 2, rows, columns), F32)],
        compiler_params=params(16),
    )(table_index, up_keep, up_in, down_keep, down_in, bias_sum)


def finish_kernel(ride, n_table, scale, table_ref, own_ref, bias_ref, *rest):
    arrived = rest[: n_table - 1]
    up_ref, down_ref, bias_out_ref, store = rest[n_table - 1 :]
    columns = own_ref.shape[2]
    start = -(-columns // EMBED_WIDTH) * EMBED_WIDTH
    up, down = own_ref[0], own_ref[1]
    store[table_ref[0]] = bias_ref[...]
    for shift in range(1, n_table):
        value = arrived[shift - 1]
        up = up + value[0, :, :columns].astype(F32)
        down = down + value[1, :, :columns].astype(F32)
        if ride:
            source = lax.rem(table_ref[0] + n_table - shift, n_table)
            high = value[0, :BIAS_ROWS, start:].astype(F32)
            store[source] = high + value[1, :BIAS_ROWS, start:].astype(F32)
    up_ref[...] = up
    down_ref[...] = down
    total = bias_ref[...]
    if ride:
        total = store[0]
        for table in range(1, n_table):
            total = total + store[table]
    bias_out_ref[...] = total[: bias_out_ref.shape[0]] * scale


def finish_call(table_index, own, bias_sum, arrived, scale, ride):
    n_table = len(arrived) + 1
    _, rows, columns = own.shape
    return pl.pallas_call(
        functools.partial(finish_kernel, ride, n_table, scale),
        in_specs=[SMEM] + [VMEM] * (n_table + 1),
        out_specs=[VMEM] * 3,
        out_shape=[
            jax.ShapeDtypeStruct((rows, columns), F32),
            jax.ShapeDtypeStruct((rows, columns), F32),
            jax.ShapeDtypeStruct((columns * n_table // EMBED_WIDTH, EMBED_WIDTH), F32),
        ],
        scratch_shapes=[pltpu.VMEM((n_table,) + bias_sum.shape, F32)],
        compiler_params=params(16),
    )(table_index, own, bias_sum, *arrived)


def rows_kernel(n_table, slots, *refs):
    parts, out_ref = refs[:n_table], refs[n_table]
    id_store = refs[n_table + 1]
    tokens = (parts[0].shape[0] - id_store.shape[1]) // slots
    slot = pl.program_id(0)

    @pl.when(slot == 0)
    def _():
        for source in range(n_table):
            ids = parts[source][slots * tokens :, :].astype(F32).astype(jnp.int32)
            id_store[source] = ids + EMPTY

    rows = lax.broadcasted_iota(jnp.int32, (TABLE_REACH_ROWS, tokens), 0)
    counts, grads = [], []
    for source in range(n_table):
        count = jnp.zeros((TABLE_REACH_ROWS, tokens), F32)
        for entry in range(BAG):
            ids = id_store[source, pl.ds(slot * BAG + entry, 1), :]
            count = count + jnp.where(ids == rows, 1.0, 0.0)
        counts.append(count.astype(BF16))
        grads.append(parts[source][pl.ds(pl.multiple_of(slot * tokens, tokens), tokens), :])
    count = jnp.concatenate(counts, axis=1)
    grad = jnp.concatenate(grads, axis=0)
    out_ref[0, 0] = jnp.dot(count, grad, preferred_element_type=F32)


def rows_call(parts, slots):
    n_table = len(parts)
    id_rows = -(-slots * BAG // 16) * 16
    tokens = (parts[0].shape[0] - id_rows) // slots
    whole = pl.BlockSpec(parts[0].shape, lambda i: (0, 0))
    return pl.pallas_call(
        functools.partial(rows_kernel, n_table, slots),
        grid=(slots,),
        in_specs=[whole] * n_table,
        out_specs=pl.BlockSpec((1, 1, TABLE_REACH_ROWS, EMBED_WIDTH), lambda i: (0, i, 0, 0)),
        out_shape=jax.ShapeDtypeStruct((1, slots, TABLE_REACH_ROWS, EMBED_WIDTH), F32),
        scratch_shapes=[pltpu.VMEM((n_table, id_rows, tokens), jnp.int32)],
        compiler_params=params(16),
        cost_estimate=pl.CostEstimate(
            flops=2 * slots * n_table * tokens * TABLE_REACH_ROWS * EMBED_WIDTH,
            bytes_accessed=4 * slots * TABLE_REACH_ROWS * EMBED_WIDTH,
            transcendentals=0,
        ),
    )(*parts)


def body(
    activations, cotangent, down_weight, up_weight, bias, bag_ids, bag_lengths, feature_table_slot
):
    tokens, width = activations.shape
    rank = down_weight.shape[0]
    n_table = lax.axis_size("table")
    n_rep = lax.axis_size("rep")
    slots = (SPARSE_FEATURES + n_table - 1) // n_table
    scale = 1.0 / math.sqrt(tokens * n_table * n_rep)
    table_index = lax.axis_index("table").astype(jnp.int32).reshape(1)
    rep_index = lax.axis_index("rep").astype(jnp.int32).reshape(1)
    far_bits = [1 << k for k in range(1, n_rep.bit_length() - 1)]
    up_bits, down_bits = [1] + far_bits, [1] + far_bits[::-1]
    ride = rank // n_rep >= BIAS_ROWS

    def swap(value, axis, bit):
        size = n_rep if axis == "rep" else n_table
        return lax.ppermute(value, axis, [(k, k ^ bit) for k in range(size)])

    def shifted(value, shift):
        return lax.ppermute(value, "table", [(k, (k + shift) % n_table) for k in range(n_table)])

    act_other = swap(activations, "rep", 1)
    cot_other = swap(cotangent, "rep", 1)
    keep, send, dense_grad, *parts = input_call(
        table_index, rep_index, feature_table_slot, activations, cotangent, down_weight, up_weight,
        bias.reshape(-1, EMBED_WIDTH), jnp.transpose(bag_ids, (1, 2, 0)), jnp.transpose(bag_lengths, (1, 0)),
        n_table, slots, up_bits, down_bits,
    )
    other = swap(send, "rep", 1)
    middle = n_table // 2
    parts[middle] = shifted(parts[middle], middle)
    near = [k for k in range(1, n_table) if k != middle]
    terms = terms_call(keep, other, activations, cotangent, act_other, cot_other, ride)

    def chain(sent, up_keep, up_send, down_keep, down_send, bias_sum):
        sent = [shifted(value, k) for value, k in zip(sent, near)]
        for place, (up_bit, down_bit) in enumerate(zip(up_bits[1:], down_bits[1:])):
            up_in = swap(up_send, "rep", up_bit)
            down_in = swap(down_send, "rep", down_bit)
            if not ride:
                bias_sum = bias_sum + swap(bias_sum, "rep", up_bit)
            if place == len(far_bits) - 1:
                break
            if ride:
                up_keep, up_send, down_keep, down_send, bias_sum = halve_call(
                    up_keep, up_in, down_keep, down_in, bias_sum
                )
            else:
                half = up_keep.shape[0] // 2
                up = up_keep + up_in.astype(F32)
                down = down_keep + down_in.astype(F32)
                up_keep, up_send = up[:half], up[half:].astype(BF16)
                down_keep, down_send = down[:half], down[half:].astype(BF16)
        if not ride:
            for bit in [1 << k for k in range(n_table.bit_length() - 1)]:
                bias_sum = bias_sum + swap(bias_sum, "table", bit)
        (up_in, down_in), sent = lax.optimization_barrier(((up_in, down_in), sent))
        own, total, *sends = split_call(
            table_index, up_keep, up_in, down_keep, down_in, bias_sum, n_table, scale, ride
        )
        return sent, own, total, sends

    operands = ([parts[k] for k in near], *terms)
    shapes = jax.eval_shape(chain, *operands)
    came, own, bias_sum, sends = lax.cond(
        feature_table_slot[0] >= 0,
        chain,
        lambda *_: jax.tree.map(lambda x: jnp.zeros(x.shape, x.dtype), shapes),
        *operands,
    )
    for value, k in zip(came, near):
        parts[k] = value
    arrived = [shifted(value, k + 1) for k, value in enumerate(sends)]
    up_grad, down_grad, bias_grad = finish_call(table_index, own, bias_sum, arrived, scale, ride)
    parts, _ = lax.optimization_barrier((parts, own))
    row_grad = rows_call(parts, slots)
    bias_grad = bias_grad.reshape(width)
    return (dense_grad, up_grad, down_grad, bias_grad, row_grad)


def solution(mesh):
    placed = (
        P(("table", "rep"), None),
        P(("table", "rep"), None),
        P(),
        P(),
        P(),
        P(("table", "rep"), None, None),
        P(("table", "rep"), None),
        P(),
    )
    return jax.shard_map(
        body,
        mesh=mesh,
        in_specs=placed,
        out_specs=(
            P(("table", "rep"), None),
            P("rep", "table"),
            P("rep", "table"),
            P(),
            P("rep", "table", None, None),
        ),
        check_vma=False,
    )
```

```python
import functools
import math

import jax
import jax.numpy as jnp
from jax import lax
from jax.experimental import pallas as pl
from jax.experimental.pallas import tpu as pltpu
from jax.sharding import PartitionSpec as P

EMBED_WIDTH = 128
SPARSE_FEATURES = 26
BAG = 4
TABLE_REACH_ROWS = 512
EMPTY = TABLE_REACH_ROWS // 2
BIAS_ROWS = 32
F32 = jnp.float32
BF16 = jnp.bfloat16
MIB = 1024 * 1024
NT = (((1,), (1,)), ((), ()))
ANY = pl.BlockSpec(memory_space=pl.ANY)
VMEM = pl.BlockSpec(memory_space=pltpu.VMEM)
SMEM = pl.BlockSpec(memory_space=pltpu.SMEM)


def params(mib):
    return pltpu.CompilerParams(vmem_limit_bytes=mib * MIB)


def pieces_of(width):
    blocks = width // EMBED_WIDTH
    parts = max(p for p in (9, 3, 1) if blocks % p == 0)
    step = width // parts
    return [(k * step, step) for k in range(parts)]


def order_matrix(rep_index, size, block, bits):
    out_row = lax.broadcasted_iota(jnp.int32, (size, size), 0)
    in_row = lax.broadcasted_iota(jnp.int32, (size, size), 1)
    source = lax.rem(out_row, block)
    position = lax.div(out_row, block)
    for place, bit in enumerate(bits):
        flag = lax.rem(lax.div(position, 1 << (len(bits) - 1 - place)), 2)
        own = lax.rem(lax.div(rep_index, bit), 2)
        source = source + jnp.where(flag == own, 0, bit) * block
    return (source == in_row).astype(F32).astype(BF16)


def input_kernel(
    n_table, slots, up_bits, down_bits, table_ref, rep_ref, owner_ref,
    act_hbm, cot_hbm, down_hbm, up_hbm, bias_ref, ids_ref, length_ref,
    keep_hbm, send_hbm, dense_hbm, *rest,
):
    outs = rest[:n_table]
    act, cot, down, up, keep, send, store, message, id_store, feature_ref, in_sems, out_sems = rest[n_table:]
    tokens, width = act.shape
    rank = down.shape[0]
    half = rank // 2
    pieces = pieces_of(width)
    arrays = ((act_hbm, act), (down_hbm, down), (cot_hbm, cot), (up_hbm, up))
    fetched = []
    for place, (start, size) in enumerate(pieces):
        part = pl.ds(start, size)
        fetched.append(
            [
                pltpu.make_async_copy(source.at[:, part], target.at[:, part], in_sems.at[which, place])
                for which, (source, target) in enumerate(arrays)
            ]
        )
        for copy in fetched[-1]:
            copy.start()
    block = rank >> len(up_bits)
    up_order = order_matrix(rep_ref[0], rank, block, up_bits)
    down_order = order_matrix(rep_ref[0], rank, block, down_bits)
    for place in range(n_table * slots):
        feature_ref[place] = SPARSE_FEATURES
    for feature in range(SPARSE_FEATURES):
        slot = owner_ref[feature]
        shift = lax.rem(lax.div(slot, slots) + n_table - table_ref[0], n_table)
        feature_ref[shift * slots + lax.rem(slot, slots)] = feature
    store[SPARSE_FEATURES + 1] = jnp.zeros(store.shape[1:], BF16)
    id_store[...] = jnp.full(id_store.shape, EMPTY, F32)
    entries = lax.broadcasted_iota(jnp.int32, (BAG, tokens), 0)
    for shift in range(n_table):
        for slot in range(slots):
            feature = feature_ref[shift * slots + slot]
            at = jnp.minimum(feature, SPARSE_FEATURES - 1)
            length = jnp.where(feature < SPARSE_FEATURES, length_ref[pl.ds(at, 1), :], 0)
            ids = jnp.where(entries < length, ids_ref[at] - EMPTY, EMPTY)
            id_store[shift, slot * BAG : (slot + 1) * BAG, :] = ids.astype(F32)
        message[shift, slots * tokens :, :] = id_store[shift].astype(BF16)
    hidden = back = None
    for (start, size), copies in zip(pieces, fetched):
        part = slice(start, start + size)
        for copy in copies:
            copy.wait()
        value = act[:, part]
        term = lax.dot_general(value, down[:, part], NT, preferred_element_type=F32)
        hidden = term if hidden is None else hidden + term
        scaled_b = (cot[:, part].astype(F32) * value.astype(F32)).astype(BF16)
        term = lax.dot_general(scaled_b, up[:, part], NT, preferred_element_type=F32)
        back = term if back is None else back + term
    hidden, back = hidden.astype(BF16), back.astype(BF16)
    rows = lax.dot_general(up_order, hidden, NT, preferred_element_type=F32).astype(BF16)
    keep[0], send[0] = rows[:half], rows[half:]
    rows = lax.dot_general(down_order, back, NT, preferred_element_type=F32).astype(BF16)
    keep[1], send[1] = rows[:half], rows[half:]
    written = [
        pltpu.make_async_copy(send, send_hbm, out_sems.at[0]),
        pltpu.make_async_copy(keep, keep_hbm, out_sems.at[1]),
    ]
    for copy in written:
        copy.start()
    blocks = 3
    for first in range(0, width // EMBED_WIDTH, blocks):
        part = slice(first * EMBED_WIDTH, (first + blocks) * EMBED_WIDTH)
        mixed = jnp.dot(hidden, up[:, part], preferred_element_type=F32)
        tail = jnp.dot(back, down[:, part], preferred_element_type=F32)
        for k in range(blocks):
            place = first + k
            mine = slice(k * EMBED_WIDTH, (k + 1) * EMBED_WIDTH)
            cols = slice(place * EMBED_WIDTH, (place + 1) * EMBED_WIDTH)
            bias = bias_ref[place : place + 1, :]
            grad = cot[:, cols].astype(F32) * (1.0 + (mixed[:, mine] + bias)) + tail[:, mine]
            store[place] = grad.astype(BF16)
    written.append(pltpu.make_async_copy(store.at[0], dense_hbm, out_sems.at[2]))
    written[-1].start()
    for shift in range(n_table):
        for slot in range(slots):
            rows = slice(slot * tokens, (slot + 1) * tokens)
            message[shift, rows, :] = store[feature_ref[shift * slots + slot] + 1]
        written.append(pltpu.make_async_copy(message.at[shift], outs[shift], out_sems.at[3 + shift]))
        written[-1].start()
    for copy in written:
        copy.wait()


def input_call(
    table_index, rep_index, owners, act, cot, down, up, bias, ids, lengths, n_table, slots, up_bits, down_bits
):
    tokens, width = act.shape
    rank = down.shape[0]
    id_rows = -(-slots * BAG // 16) * 16
    sent = slots * tokens + id_rows
    return pl.pallas_call(
        functools.partial(input_kernel, n_table, slots, up_bits, down_bits),
        in_specs=[SMEM, SMEM, SMEM, ANY, ANY, ANY, ANY, VMEM, VMEM, VMEM],
        out_specs=[ANY] * (3 + n_table),
        out_shape=[
            jax.ShapeDtypeStruct((2, rank // 2, tokens), BF16),
            jax.ShapeDtypeStruct((2, rank // 2, tokens), BF16),
            jax.ShapeDtypeStruct((tokens, EMBED_WIDTH), BF16),
        ]
        + [jax.ShapeDtypeStruct((sent, EMBED_WIDTH), BF16)] * n_table,
        scratch_shapes=[
            pltpu.VMEM((tokens, width), BF16),
            pltpu.VMEM((tokens, width), BF16),
            pltpu.VMEM((rank, width), BF16),
            pltpu.VMEM((rank, width), BF16),
            pltpu.VMEM((2, rank // 2, tokens), BF16),
            pltpu.VMEM((2, rank // 2, tokens), BF16),
            pltpu.VMEM((SPARSE_FEATURES + 2, tokens, EMBED_WIDTH), BF16),
            pltpu.VMEM((n_table, sent, EMBED_WIDTH), BF16),
            pltpu.VMEM((n_table, id_rows, EMBED_WIDTH), F32),
            pltpu.SMEM((n_table * slots,), jnp.int32),
            pltpu.SemaphoreType.DMA((4, len(pieces_of(width)))),
            pltpu.SemaphoreType.DMA((3 + n_table,)),
        ],
        compiler_params=params(60),
        cost_estimate=pl.CostEstimate(
            flops=8 * tokens * rank * width, bytes_accessed=4 * (tokens + rank) * width, transcendentals=0
        ),
    )(table_index, rep_index, owners, act, cot, down, up, bias, ids, lengths)


def bias_terms(value):
    high = value.astype(BF16).astype(F32)
    return high, (value - high).astype(BF16).astype(F32)


def put_bias(ref, width, high, low):
    if ref.shape[0] >= 2 * BIAS_ROWS:
        both = jnp.concatenate([high, low], axis=0).astype(BF16)
        ref[: 2 * BIAS_ROWS, width : width + EMBED_WIDTH] = both
    else:
        ref[:BIAS_ROWS, width : width + EMBED_WIDTH] = high.astype(BF16)
        ref[:BIAS_ROWS, width + EMBED_WIDTH : width + 2 * EMBED_WIDTH] = low.astype(BF16)


def get_bias(ref, width):
    if ref.shape[0] >= 2 * BIAS_ROWS:
        both = ref[: 2 * BIAS_ROWS, width : width + EMBED_WIDTH].astype(F32)
        return both[:BIAS_ROWS] + both[BIAS_ROWS:]
    high = ref[:BIAS_ROWS, width : width + EMBED_WIDTH].astype(F32)
    return high + ref[:BIAS_ROWS, width + EMBED_WIDTH : width + 2 * EMBED_WIDTH].astype(F32)


def extra_columns(rows):
    return EMBED_WIDTH if rows >= 2 * BIAS_ROWS else 2 * EMBED_WIDTH


def terms_kernel(
    ride, keep_ref, other_ref, act, cot, act_other, cot_other,
    up_keep_ref, up_send_ref, down_keep_ref, down_send_ref, bias_ref,
):
    width = act.shape[1]
    hidden = jnp.concatenate([keep_ref[0], other_ref[0]], axis=1)
    back = jnp.concatenate([keep_ref[1], other_ref[1]], axis=1)
    blocks = 3
    keep = hidden.shape[0] // 2
    bias_ref[...] = jnp.zeros_like(bias_ref)
    for first in range(0, width // EMBED_WIDTH, blocks):
        part = slice(first * EMBED_WIDTH, (first + blocks) * EMBED_WIDTH)
        values = jnp.concatenate([act[:, part], act_other[:, part]], axis=0)
        grads = jnp.concatenate([cot[:, part], cot_other[:, part]], axis=0)
        scaled = grads.astype(F32) * values.astype(F32)
        sums = jnp.sum(scaled, axis=0, keepdims=True)
        for k in range(blocks):
            bias_ref[first + k : first + k + 1, :] = sums[:, k * EMBED_WIDTH : (k + 1) * EMBED_WIDTH]
        up_part = jnp.dot(hidden, scaled.astype(BF16), preferred_element_type=F32)
        up_keep_ref[:, part] = up_part[:keep]
        up_send_ref[:, part] = up_part[keep:].astype(BF16)
        down_part = jnp.dot(back, values, preferred_element_type=F32)
        down_keep_ref[:, part] = down_part[:keep]
        down_send_ref[:, part] = down_part[keep:].astype(BF16)
    if ride:
        high, low = bias_terms(bias_ref[...])
        put_bias(up_send_ref, width, high, low)
        bias_ref[...] = high + low


def terms_call(keep, other, act, cot, act_other, cot_other, ride):
    tokens, width = act.shape
    rows = keep.shape[1] // 2
    extra = extra_columns(rows) if ride else 0
    return pl.pallas_call(
        functools.partial(terms_kernel, ride),
        in_specs=[VMEM] * 6,
        out_specs=[VMEM] * 5,
        out_shape=[
            jax.ShapeDtypeStruct((rows, width), F32),
            jax.ShapeDtypeStruct((rows, width + extra), BF16),
            jax.ShapeDtypeStruct((rows, width), F32),
            jax.ShapeDtypeStruct((rows, width), BF16),
            jax.ShapeDtypeStruct((BIAS_ROWS, EMBED_WIDTH), F32),
        ],
        compiler_params=params(16),
        cost_estimate=pl.CostEstimate(
            flops=16 * tokens * rows * width, bytes_accessed=8 * tokens * width + 12 * rows * width, transcendentals=0
        ),
    )(keep, other, act, cot, act_other, cot_other)


def halve_kernel(
    up_keep_ref, up_in_ref, down_keep_ref, down_in_ref, bias_ref,
    up_out_ref, up_send_ref, down_out_ref, down_send_ref, bias_out_ref,
):
    rows, width = up_keep_ref.shape
    half = rows // 2
    up = up_keep_ref[...] + up_in_ref[:, :width].astype(F32)
    up_out_ref[...] = up[:half]
    up_send_ref[:, :width] = up[half:].astype(BF16)
    down = down_keep_ref[...] + down_in_ref[...].astype(F32)
    down_out_ref[...] = down[:half]
    down_send_ref[...] = down[half:].astype(BF16)
    high, low = bias_terms(bias_ref[...] + get_bias(up_in_ref, width))
    put_bias(up_send_ref, width, high, low)
    bias_out_ref[...] = high + low


def halve_call(up_keep, up_in, down_keep, down_in, bias_sum):
    rows, width = up_keep.shape
    half = rows // 2
    return pl.pallas_call(
        halve_kernel,
        in_specs=[VMEM] * 5,
        out_specs=[VMEM] * 5,
        out_shape=[
            jax.ShapeDtypeStruct((half, width), F32),
            jax.ShapeDtypeStruct((half, width + extra_columns(half)), BF16),
            jax.ShapeDtypeStruct((half, width), F32),
            jax.ShapeDtypeStruct((half, width), BF16),
            jax.ShapeDtypeStruct(bias_sum.shape, F32),
        ],
        compiler_params=params(16),
    )(up_keep, up_in, down_keep, down_in, bias_sum)


def split_kernel(
    ride, n_table, scale, table_ref, up_keep_ref, up_in_ref, down_keep_ref, down_in_ref, bias_ref,
    own_ref, bias_out_ref, *rest,
):
    sends, store = rest[: n_table - 1], rest[n_table - 1]
    columns = own_ref.shape[2]
    width = up_keep_ref.shape[1]
    pairs = ((up_keep_ref, up_in_ref), (down_keep_ref, down_in_ref))
    for which, (keep, arrived) in enumerate(pairs):
        total = (keep[...] + arrived[:, :width].astype(F32)) * scale
        for table in range(n_table):
            store[table, which] = total[:, table * columns : (table + 1) * columns]
    own_ref[...] = store[table_ref[0]]
    start = -(-columns // EMBED_WIDTH) * EMBED_WIDTH
    bias = bias_ref[...]
    if ride:
        high, low = bias_terms(bias + get_bias(up_in_ref, width))
        bias = high + low
    bias_out_ref[...] = bias
    for shift in range(1, n_table):
        value = store[lax.rem(table_ref[0] + shift, n_table)].astype(BF16)
        sends[shift - 1][:, :, :columns] = value
        if ride:
            sends[shift - 1][0, :BIAS_ROWS, start:] = high.astype(BF16)
            sends[shift - 1][1, :BIAS_ROWS, start:] = low.astype(BF16)


def split_call(table_index, up_keep, up_in, down_keep, down_in, bias_sum, n_table, scale, ride):
    rows, width = up_keep.shape
    columns = width // n_table
    sent = -(-columns // EMBED_WIDTH) * EMBED_WIDTH + EMBED_WIDTH if ride else columns
    return pl.pallas_call(
        functools.partial(split_kernel, ride, n_table, scale),
        in_specs=[SMEM] + [VMEM] * 5,
        out_specs=[VMEM] * (n_table + 1),
        out_shape=[
            jax.ShapeDtypeStruct((2, rows, columns), F32),
            jax.ShapeDtypeStruct(bias_sum.shape, F32),
        ]
        + [jax.ShapeDtypeStruct((2, rows, sent), BF16)] * (n_table - 1),
        scratch_shapes=[pltpu.VMEM((n_table, 2, rows, columns), F32)],
        compiler_params=params(16),
    )(table_index, up_keep, up_in, down_keep, down_in, bias_sum)


def finish_kernel(ride, n_table, scale, table_ref, own_ref, bias_ref, *rest):
    arrived = rest[: n_table - 1]
    up_ref, down_ref, bias_out_ref, store = rest[n_table - 1 :]
    columns = own_ref.shape[2]
    start = -(-columns // EMBED_WIDTH) * EMBED_WIDTH
    up, down = own_ref[0], own_ref[1]
    store[table_ref[0]] = bias_ref[...]
    for shift in range(1, n_table):
        value = arrived[shift - 1]
        up = up + value[0, :, :columns].astype(F32)
        down = down + value[1, :, :columns].astype(F32)
        if ride:
            source = lax.rem(table_ref[0] + n_table - shift, n_table)
            high = value[0, :BIAS_ROWS, start:].astype(F32)
            store[source] = high + value[1, :BIAS_ROWS, start:].astype(F32)
    up_ref[...] = up
    down_ref[...] = down
    total = bias_ref[...]
    if ride:
        total = store[0]
        for table in range(1, n_table):
            total = total + store[table]
    bias_out_ref[...] = total[: bias_out_ref.shape[0]] * scale


def finish_call(table_index, own, bias_sum, arrived, scale, ride):
    n_table = len(arrived) + 1
    _, rows, columns = own.shape
    return pl.pallas_call(
        functools.partial(finish_kernel, ride, n_table, scale),
        in_specs=[SMEM] + [VMEM] * (n_table + 1),
        out_specs=[VMEM] * 3,
        out_shape=[
            jax.ShapeDtypeStruct((rows, columns), F32),
            jax.ShapeDtypeStruct((rows, columns), F32),
            jax.ShapeDtypeStruct((columns * n_table // EMBED_WIDTH, EMBED_WIDTH), F32),
        ],
        scratch_shapes=[pltpu.VMEM((n_table,) + bias_sum.shape, F32)],
        compiler_params=params(16),
    )(table_index, own, bias_sum, *arrived)


def put_rows(ref, high, low):
    wide = ref.shape[1] // EMBED_WIDTH
    first = ref.shape[0] - 8
    ref[first:, :] = jnp.zeros((8, ref.shape[1]), BF16)
    rows = []
    for value in (high, low):
        for row in range(4):
            pieces = [
                value[min(row * wide + k, BIAS_ROWS - 1) : min(row * wide + k, BIAS_ROWS - 1) + 1, :]
                for k in range(wide)
            ]
            rows.append(jnp.concatenate(pieces, axis=1))
    ref[first:, :] = jnp.concatenate(rows, axis=0).astype(BF16)


def get_rows(ref, store):
    wide = ref.shape[1] // EMBED_WIDTH
    value = ref[ref.shape[0] - 8 :, :].astype(F32)
    value = value[:4] + value[4:]
    for place in range(min(4 * wide, BIAS_ROWS)):
        row, k = divmod(place, wide)
        store[place : place + 1, :] = value[row : row + 1, k * EMBED_WIDTH : (k + 1) * EMBED_WIDTH]
    return store[...]


def padded(columns):
    return -(-columns // EMBED_WIDTH) * EMBED_WIDTH


def first_kernel(
    n_table, scale, table_ref, up_keep_ref, up_in_ref, down_keep_ref, down_in_ref, bias_ref,
    keep_ref, send_ref, bias_out_ref, store,
):
    _, _, rows, columns = keep_ref.shape
    width = up_keep_ref.shape[1]
    pairs = ((up_keep_ref, up_in_ref), (down_keep_ref, down_in_ref))
    for which, (keep, arrived) in enumerate(pairs):
        total = (keep[...] + arrived[:, :width].astype(F32)) * scale
        for table in range(n_table):
            store[table, which] = total[:, table * columns : (table + 1) * columns]
    for place in range(n_table // 2):
        keep_ref[place] = store[table_ref[0] ^ (2 * place)]
        for which in range(2):
            first = (2 * place + which) * rows
            value = store[table_ref[0] ^ (2 * place + 1), which]
            send_ref[first : first + rows, :columns] = value.astype(BF16)
    high, low = bias_terms(bias_ref[...] + get_bias(up_in_ref, width))
    put_rows(send_ref, high, low)
    bias_out_ref[...] = high + low


def first_call(table_index, up_keep, up_in, down_keep, down_in, bias_sum, n_table, scale):
    rows, width = up_keep.shape
    columns = width // n_table
    return pl.pallas_call(
        functools.partial(first_kernel, n_table, scale),
        in_specs=[SMEM] + [VMEM] * 5,
        out_specs=[VMEM] * 3,
        out_shape=[
            jax.ShapeDtypeStruct((n_table // 2, 2, rows, columns), F32),
            jax.ShapeDtypeStruct((n_table * rows + 8, padded(columns)), BF16),
            jax.ShapeDtypeStruct(bias_sum.shape, F32),
        ],
        scratch_shapes=[pltpu.VMEM((n_table, 2, rows, columns), F32)],
        compiler_params=params(16),
    )(table_index, up_keep, up_in, down_keep, down_in, bias_sum)


def next_kernel(keep_ref, in_ref, bias_ref, out_ref, send_ref, bias_out_ref, store):
    count, _, rows, columns = keep_ref.shape
    for place in range(count):
        for which in range(2):
            first = (2 * place + which) * rows
            total = keep_ref[place, which] + in_ref[first : first + rows, :columns].astype(F32)
            if place % 2 == 0:
                out_ref[place // 2, which] = total
            else:
                first = (place - 1 + which) * rows
                send_ref[first : first + rows, :columns] = total.astype(BF16)
    store[...] = jnp.zeros_like(store)
    high, low = bias_terms(bias_ref[...] + get_rows(in_ref, store))
    put_rows(send_ref, high, low)
    bias_out_ref[...] = high + low


def next_call(keep, arrived, bias_sum):
    count, _, rows, columns = keep.shape
    return pl.pallas_call(
        next_kernel,
        in_specs=[VMEM] * 3,
        out_specs=[VMEM] * 3,
        out_shape=[
            jax.ShapeDtypeStruct((count // 2, 2, rows, columns), F32),
            jax.ShapeDtypeStruct((count * rows + 8, padded(columns)), BF16),
            jax.ShapeDtypeStruct(bias_sum.shape, F32),
        ],
        scratch_shapes=[pltpu.VMEM(bias_sum.shape, F32)],
        compiler_params=params(16),
    )(keep, arrived, bias_sum)


def last_kernel(scale, keep_ref, in_ref, bias_ref, up_ref, down_ref, bias_out_ref, store):
    rows, columns = up_ref.shape
    up_ref[...] = keep_ref[0, 0] + in_ref[:rows, :columns].astype(F32)
    down_ref[...] = keep_ref[0, 1] + in_ref[rows : 2 * rows, :columns].astype(F32)
    store[...] = jnp.zeros_like(store)
    total = bias_ref[...] + get_rows(in_ref, store)
    bias_out_ref[...] = total[: bias_out_ref.shape[0]] * scale


def last_call(keep, arrived, bias_sum, n_table, scale):
    _, _, rows, columns = keep.shape
    return pl.pallas_call(
        functools.partial(last_kernel, scale),
        in_specs=[VMEM] * 3,
        out_specs=[VMEM] * 3,
        out_shape=[
            jax.ShapeDtypeStruct((rows, columns), F32),
            jax.ShapeDtypeStruct((rows, columns), F32),
            jax.ShapeDtypeStruct((columns * n_table // EMBED_WIDTH, EMBED_WIDTH), F32),
        ],
        scratch_shapes=[pltpu.VMEM(bias_sum.shape, F32)],
        compiler_params=params(16),
    )(keep, arrived, bias_sum)


def rows_kernel(n_table, slots, *refs):
    parts, out_ref = refs[:n_table], refs[n_table]
    id_store = refs[n_table + 1]
    tokens = (parts[0].shape[0] - id_store.shape[1]) // slots
    slot = pl.program_id(0)

    @pl.when(slot == 0)
    def _():
        for source in range(n_table):
            ids = parts[source][slots * tokens :, :].astype(F32).astype(jnp.int32)
            id_store[source] = ids + EMPTY

    rows = lax.broadcasted_iota(jnp.int32, (TABLE_REACH_ROWS, tokens), 0)
    counts, grads = [], []
    for source in range(n_table):
        count = jnp.zeros((TABLE_REACH_ROWS, tokens), F32)
        for entry in range(BAG):
            ids = id_store[source, pl.ds(slot * BAG + entry, 1), :]
            count = count + jnp.where(ids == rows, 1.0, 0.0)
        counts.append(count.astype(BF16))
        grads.append(parts[source][pl.ds(pl.multiple_of(slot * tokens, tokens), tokens), :])
    count = jnp.concatenate(counts, axis=1)
    grad = jnp.concatenate(grads, axis=0)
    out_ref[0, 0] = jnp.dot(count, grad, preferred_element_type=F32)


def rows_call(parts, slots):
    n_table = len(parts)
    id_rows = -(-slots * BAG // 16) * 16
    tokens = (parts[0].shape[0] - id_rows) // slots
    whole = pl.BlockSpec(parts[0].shape, lambda i: (0, 0))
    return pl.pallas_call(
        functools.partial(rows_kernel, n_table, slots),
        grid=(slots,),
        in_specs=[whole] * n_table,
        out_specs=pl.BlockSpec((1, 1, TABLE_REACH_ROWS, EMBED_WIDTH), lambda i: (0, i, 0, 0)),
        out_shape=jax.ShapeDtypeStruct((1, slots, TABLE_REACH_ROWS, EMBED_WIDTH), F32),
        scratch_shapes=[pltpu.VMEM((n_table, id_rows, tokens), jnp.int32)],
        compiler_params=params(16),
        cost_estimate=pl.CostEstimate(
            flops=2 * slots * n_table * tokens * TABLE_REACH_ROWS * EMBED_WIDTH,
            bytes_accessed=4 * slots * TABLE_REACH_ROWS * EMBED_WIDTH,
            transcendentals=0,
        ),
    )(*parts)


def body(
    activations, cotangent, down_weight, up_weight, bias, bag_ids, bag_lengths, feature_table_slot
):
    tokens, width = activations.shape
    rank = down_weight.shape[0]
    n_table = lax.axis_size("table")
    n_rep = lax.axis_size("rep")
    slots = (SPARSE_FEATURES + n_table - 1) // n_table
    scale = 1.0 / math.sqrt(tokens * n_table * n_rep)
    table_index = lax.axis_index("table").astype(jnp.int32).reshape(1)
    rep_index = lax.axis_index("rep").astype(jnp.int32).reshape(1)
    far_bits = [1 << k for k in range(1, n_rep.bit_length() - 1)]
    up_bits, down_bits = [1] + far_bits, [1] + far_bits[::-1]
    ride = rank // n_rep >= BIAS_ROWS

    def swap(value, axis, bit):
        size = n_rep if axis == "rep" else n_table
        return lax.ppermute(value, axis, [(k, k ^ bit) for k in range(size)])

    def shifted(value, shift):
        return lax.ppermute(value, "table", [(k, (k + shift) % n_table) for k in range(n_table)])

    act_other = swap(activations, "rep", 1)
    cot_other = swap(cotangent, "rep", 1)
    keep, send, dense_grad, *parts = input_call(
        table_index, rep_index, feature_table_slot, activations, cotangent, down_weight, up_weight,
        bias.reshape(-1, EMBED_WIDTH), jnp.transpose(bag_ids, (1, 2, 0)), jnp.transpose(bag_lengths, (1, 0)),
        n_table, slots, up_bits, down_bits,
    )
    other = swap(send, "rep", 1)
    parts = [parts[0]] + [shifted(parts[k], k) for k in range(1, n_table)]
    up_keep, up_send, down_keep, down_send, bias_sum = terms_call(
        keep, other, activations, cotangent, act_other, cot_other, ride
    )
    def exchange(place, up_send, down_send, bias_sum):
        up_in = swap(up_send, "rep", up_bits[place])
        down_in = swap(down_send, "rep", down_bits[place])
        if not ride:
            bias_sum = bias_sum + swap(bias_sum, "rep", up_bits[place])
        return up_in, down_in, bias_sum

    def halved(up_keep, up_in, down_keep, down_in, bias_sum):
        if ride:
            return halve_call(up_keep, up_in, down_keep, down_in, bias_sum)
        half = up_keep.shape[0] // 2
        up = up_keep + up_in.astype(F32)
        down = down_keep + down_in.astype(F32)
        return up[:half], up[half:].astype(BF16), down[:half], down[half:].astype(BF16), bias_sum

    def chain(up_keep, up_send, down_keep, down_send, bias_sum):
        for place in range(2, len(up_bits)):
            up_in, down_in, bias_sum = exchange(place, up_send, down_send, bias_sum)
            if place < len(up_bits) - 1:
                up_keep, up_send, down_keep, down_send, bias_sum = halved(
                    up_keep, up_in, down_keep, down_in, bias_sum
                )
        if not ride:
            for bit in [1 << k for k in range(n_table.bit_length() - 1)]:
                bias_sum = bias_sum + swap(bias_sum, "table", bit)
        if not ride:
            return split_call(
                table_index, up_keep, up_in, down_keep, down_in, bias_sum, n_table, scale, ride
            )
        own, message, bias_sum = first_call(
            table_index, up_keep, up_in, down_keep, down_in, bias_sum, n_table, scale
        )
        for bit in [1 << k for k in range(n_table.bit_length() - 2)]:
            message = swap(message, "table", bit)
            own, message, bias_sum = next_call(own, message, bias_sum)
        return [own, bias_sum, message]

    up_in, down_in, bias_sum = exchange(1, up_send, down_send, bias_sum)
    terms = halved(up_keep, up_in, down_keep, down_in, bias_sum)
    shapes = jax.eval_shape(chain, *terms)
    own, bias_sum, *sends = lax.cond(
        feature_table_slot[0] >= 0,
        chain,
        lambda *_: jax.tree.map(lambda x: jnp.zeros(x.shape, x.dtype), shapes),
        *terms,
    )
    if ride:
        message = swap(sends[0], "table", n_table // 2)
        up_grad, down_grad, bias_grad = last_call(own, message, bias_sum, n_table, scale)
    else:
        arrived = [shifted(value, k + 1) for k, value in enumerate(sends)]
        up_grad, down_grad, bias_grad = finish_call(table_index, own, bias_sum, arrived, scale, ride)
    parts, _ = lax.optimization_barrier((parts, own))
    row_grad = rows_call(parts, slots)
    bias_grad = bias_grad.reshape(width)
    return (dense_grad, up_grad, down_grad, bias_grad, row_grad)


def solution(mesh):
    placed = (
        P(("table", "rep"), None),
        P(("table", "rep"), None),
        P(),
        P(),
        P(),
        P(("table", "rep"), None, None),
        P(("table", "rep"), None),
        P(),
    )
    return jax.shard_map(
        body,
        mesh=mesh,
        in_specs=placed,
        out_specs=(
            P(("table", "rep"), None),
            P("rep", "table"),
            P("rep", "table"),
            P(),
            P("rep", "table", None, None),
        ),
        check_vma=False,
    )
```

```python
import functools
import math

import jax
import jax.numpy as jnp
from jax import lax
from jax.experimental import pallas as pl
from jax.experimental.pallas import tpu as pltpu
from jax.sharding import PartitionSpec as P

EMBED_WIDTH = 128
SPARSE_FEATURES = 26
BAG = 4
TABLE_REACH_ROWS = 512
EMPTY = TABLE_REACH_ROWS // 2
BIAS_ROWS = 32
F32 = jnp.float32
BF16 = jnp.bfloat16
MIB = 1024 * 1024
NT = (((1,), (1,)), ((), ()))
ANY = pl.BlockSpec(memory_space=pl.ANY)
VMEM = pl.BlockSpec(memory_space=pltpu.VMEM)
SMEM = pl.BlockSpec(memory_space=pltpu.SMEM)


def params(mib):
    return pltpu.CompilerParams(vmem_limit_bytes=mib * MIB)


def pieces_of(width):
    blocks = width // EMBED_WIDTH
    parts = max(p for p in (9, 3, 1) if blocks % p == 0)
    step = width // parts
    return [(k * step, step) for k in range(parts)]


def order_matrix(rep_index, size, block, bits):
    out_row = lax.broadcasted_iota(jnp.int32, (size, size), 0)
    in_row = lax.broadcasted_iota(jnp.int32, (size, size), 1)
    source = lax.rem(out_row, block)
    position = lax.div(out_row, block)
    for place, bit in enumerate(bits):
        flag = lax.rem(lax.div(position, 1 << (len(bits) - 1 - place)), 2)
        own = lax.rem(lax.div(rep_index, bit), 2)
        source = source + jnp.where(flag == own, 0, bit) * block
    return (source == in_row).astype(F32).astype(BF16)


def input_kernel(
    n_table, slots, up_bits, down_bits, table_ref, rep_ref, owner_ref,
    act_hbm, cot_hbm, down_hbm, up_hbm, bias_ref, ids_ref, length_ref,
    keep, send_hbm, dense_hbm, *rest,
):
    outs = rest[:n_table]
    act, cot, down, up, send, store, message, id_store, feature_ref, in_sems, out_sems = rest[n_table:]
    tokens, width = act.shape
    rank = down.shape[0]
    half = rank // 2
    pieces = pieces_of(width)
    arrays = ((act_hbm, act), (down_hbm, down), (cot_hbm, cot), (up_hbm, up))
    fetched = []
    for place, (start, size) in enumerate(pieces):
        part = pl.ds(start, size)
        fetched.append(
            [
                pltpu.make_async_copy(source.at[:, part], target.at[:, part], in_sems.at[which, place])
                for which, (source, target) in enumerate(arrays)
            ]
        )
        for copy in fetched[-1]:
            copy.start()
    block = rank >> len(up_bits)
    up_order = order_matrix(rep_ref[0], rank, block, up_bits)
    down_order = order_matrix(rep_ref[0], rank, block, down_bits)
    for place in range(n_table * slots):
        feature_ref[place] = SPARSE_FEATURES
    for feature in range(SPARSE_FEATURES):
        slot = owner_ref[feature]
        shift = lax.rem(lax.div(slot, slots) + n_table - table_ref[0], n_table)
        feature_ref[shift * slots + lax.rem(slot, slots)] = feature
    store[SPARSE_FEATURES + 1] = jnp.zeros(store.shape[1:], BF16)
    id_store[...] = jnp.full(id_store.shape, EMPTY, F32)
    entries = lax.broadcasted_iota(jnp.int32, (BAG, tokens), 0)
    for shift in range(n_table):
        for slot in range(slots):
            feature = feature_ref[shift * slots + slot]
            at = jnp.minimum(feature, SPARSE_FEATURES - 1)
            length = jnp.where(feature < SPARSE_FEATURES, length_ref[pl.ds(at, 1), :], 0)
            ids = jnp.where(entries < length, ids_ref[at] - EMPTY, EMPTY)
            id_store[shift, slot * BAG : (slot + 1) * BAG, :] = ids.astype(F32)
        message[shift, slots * tokens :, :] = id_store[shift].astype(BF16)
    hidden = back = None
    for (start, size), copies in zip(pieces, fetched):
        part = slice(start, start + size)
        for copy in copies:
            copy.wait()
        value = act[:, part]
        term = lax.dot_general(value, down[:, part], NT, preferred_element_type=F32)
        hidden = term if hidden is None else hidden + term
        scaled_b = (cot[:, part].astype(F32) * value.astype(F32)).astype(BF16)
        term = lax.dot_general(scaled_b, up[:, part], NT, preferred_element_type=F32)
        back = term if back is None else back + term
    hidden, back = hidden.astype(BF16), back.astype(BF16)
    rows = lax.dot_general(up_order, hidden, NT, preferred_element_type=F32).astype(BF16)
    keep[0], send[0] = rows[:half], rows[half:]
    rows = lax.dot_general(down_order, back, NT, preferred_element_type=F32).astype(BF16)
    keep[1], send[1] = rows[:half], rows[half:]
    written = [pltpu.make_async_copy(send, send_hbm, out_sems.at[0])]
    written[0].start()
    blocks = 3
    for first in range(0, width // EMBED_WIDTH, blocks):
        part = slice(first * EMBED_WIDTH, (first + blocks) * EMBED_WIDTH)
        mixed = jnp.dot(hidden, up[:, part], preferred_element_type=F32)
        tail = jnp.dot(back, down[:, part], preferred_element_type=F32)
        for k in range(blocks):
            place = first + k
            mine = slice(k * EMBED_WIDTH, (k + 1) * EMBED_WIDTH)
            cols = slice(place * EMBED_WIDTH, (place + 1) * EMBED_WIDTH)
            bias = bias_ref[place : place + 1, :]
            grad = cot[:, cols].astype(F32) * (1.0 + (mixed[:, mine] + bias)) + tail[:, mine]
            store[place] = grad.astype(BF16)
    written.append(pltpu.make_async_copy(store.at[0], dense_hbm, out_sems.at[2]))
    written[-1].start()
    for shift in range(n_table):
        for slot in range(slots):
            rows = slice(slot * tokens, (slot + 1) * tokens)
            message[shift, rows, :] = store[feature_ref[shift * slots + slot] + 1]
        written.append(pltpu.make_async_copy(message.at[shift], outs[shift], out_sems.at[3 + shift]))
        written[-1].start()
    for copy in written:
        copy.wait()


def input_call(
    table_index, rep_index, owners, act, cot, down, up, bias, ids, lengths, n_table, slots, up_bits, down_bits
):
    tokens, width = act.shape
    rank = down.shape[0]
    id_rows = -(-slots * BAG // 16) * 16
    sent = slots * tokens + id_rows
    return pl.pallas_call(
        functools.partial(input_kernel, n_table, slots, up_bits, down_bits),
        in_specs=[SMEM, SMEM, SMEM, ANY, ANY, ANY, ANY, VMEM, VMEM, VMEM],
        out_specs=[VMEM] + [ANY] * (2 + n_table),
        out_shape=[
            pltpu.VMEM((2, rank // 2, tokens), BF16),
            jax.ShapeDtypeStruct((2, rank // 2, tokens), BF16),
            jax.ShapeDtypeStruct((tokens, EMBED_WIDTH), BF16),
        ]
        + [jax.ShapeDtypeStruct((sent, EMBED_WIDTH), BF16)] * n_table,
        scratch_shapes=[
            pltpu.VMEM((tokens, width), BF16),
            pltpu.VMEM((tokens, width), BF16),
            pltpu.VMEM((rank, width), BF16),
            pltpu.VMEM((rank, width), BF16),
            pltpu.VMEM((2, rank // 2, tokens), BF16),
            pltpu.VMEM((SPARSE_FEATURES + 2, tokens, EMBED_WIDTH), BF16),
            pltpu.VMEM((n_table, sent, EMBED_WIDTH), BF16),
            pltpu.VMEM((n_table, id_rows, EMBED_WIDTH), F32),
            pltpu.SMEM((n_table * slots,), jnp.int32),
            pltpu.SemaphoreType.DMA((4, len(pieces_of(width)))),
            pltpu.SemaphoreType.DMA((3 + n_table,)),
        ],
        compiler_params=params(60),
        cost_estimate=pl.CostEstimate(
            flops=8 * tokens * rank * width, bytes_accessed=4 * (tokens + rank) * width, transcendentals=0
        ),
    )(table_index, rep_index, owners, act, cot, down, up, bias, ids, lengths)


def bias_terms(value):
    high = value.astype(BF16).astype(F32)
    return high, (value - high).astype(BF16).astype(F32)


def put_bias(ref, width, high, low):
    if ref.shape[0] >= 2 * BIAS_ROWS:
        both = jnp.concatenate([high, low], axis=0).astype(BF16)
        ref[: 2 * BIAS_ROWS, width : width + EMBED_WIDTH] = both
    else:
        ref[:BIAS_ROWS, width : width + EMBED_WIDTH] = high.astype(BF16)
        ref[:BIAS_ROWS, width + EMBED_WIDTH : width + 2 * EMBED_WIDTH] = low.astype(BF16)


def get_bias(ref, width):
    if ref.shape[0] >= 2 * BIAS_ROWS:
        both = ref[: 2 * BIAS_ROWS, width : width + EMBED_WIDTH].astype(F32)
        return both[:BIAS_ROWS] + both[BIAS_ROWS:]
    high = ref[:BIAS_ROWS, width : width + EMBED_WIDTH].astype(F32)
    return high + ref[:BIAS_ROWS, width + EMBED_WIDTH : width + 2 * EMBED_WIDTH].astype(F32)


def extra_columns(rows):
    return EMBED_WIDTH if rows >= 2 * BIAS_ROWS else 2 * EMBED_WIDTH


def terms_kernel(
    ride, keep_ref, other_ref, act, cot, act_other, cot_other,
    up_keep_ref, up_send_ref, down_keep_ref, down_send_ref, bias_ref,
):
    width = act.shape[1]
    hidden = jnp.concatenate([keep_ref[0], other_ref[0]], axis=1)
    back = jnp.concatenate([keep_ref[1], other_ref[1]], axis=1)
    blocks = 3
    keep = hidden.shape[0] // 2
    bias_ref[...] = jnp.zeros_like(bias_ref)
    for first in range(0, width // EMBED_WIDTH, blocks):
        part = slice(first * EMBED_WIDTH, (first + blocks) * EMBED_WIDTH)
        values = jnp.concatenate([act[:, part], act_other[:, part]], axis=0)
        grads = jnp.concatenate([cot[:, part], cot_other[:, part]], axis=0)
        scaled = grads.astype(F32) * values.astype(F32)
        sums = jnp.sum(scaled, axis=0, keepdims=True)
        for k in range(blocks):
            bias_ref[first + k : first + k + 1, :] = sums[:, k * EMBED_WIDTH : (k + 1) * EMBED_WIDTH]
        up_part = jnp.dot(hidden, scaled.astype(BF16), preferred_element_type=F32)
        up_keep_ref[:, part] = up_part[:keep]
        up_send_ref[:, part] = up_part[keep:].astype(BF16)
        down_part = jnp.dot(back, values, preferred_element_type=F32)
        down_keep_ref[:, part] = down_part[:keep]
        down_send_ref[:, part] = down_part[keep:].astype(BF16)
    if ride:
        high, low = bias_terms(bias_ref[...])
        put_bias(up_send_ref, width, high, low)
        bias_ref[...] = high + low


def terms_call(keep, other, act, cot, act_other, cot_other, ride):
    tokens, width = act.shape
    rows = keep.shape[1] // 2
    extra = extra_columns(rows) if ride else 0
    return pl.pallas_call(
        functools.partial(terms_kernel, ride),
        in_specs=[VMEM] * 6,
        out_specs=[VMEM] * 5,
        out_shape=[
            jax.ShapeDtypeStruct((rows, width), F32),
            jax.ShapeDtypeStruct((rows, width + extra), BF16),
            jax.ShapeDtypeStruct((rows, width), F32),
            jax.ShapeDtypeStruct((rows, width), BF16),
            jax.ShapeDtypeStruct((BIAS_ROWS, EMBED_WIDTH), F32),
        ],
        compiler_params=params(16),
        cost_estimate=pl.CostEstimate(
            flops=16 * tokens * rows * width, bytes_accessed=8 * tokens * width + 12 * rows * width, transcendentals=0
        ),
    )(keep, other, act, cot, act_other, cot_other)


def halve_kernel(
    up_keep_ref, up_in_ref, down_keep_ref, down_in_ref, bias_ref,
    up_out_ref, up_send_ref, down_out_ref, down_send_ref, bias_out_ref,
):
    rows, width = up_keep_ref.shape
    half = rows // 2
    up = up_keep_ref[...] + up_in_ref[:, :width].astype(F32)
    up_out_ref[...] = up[:half]
    up_send_ref[:, :width] = up[half:].astype(BF16)
    down = down_keep_ref[...] + down_in_ref[...].astype(F32)
    down_out_ref[...] = down[:half]
    down_send_ref[...] = down[half:].astype(BF16)
    high, low = bias_terms(bias_ref[...] + get_bias(up_in_ref, width))
    put_bias(up_send_ref, width, high, low)
    bias_out_ref[...] = high + low


def halve_call(up_keep, up_in, down_keep, down_in, bias_sum):
    rows, width = up_keep.shape
    half = rows // 2
    return pl.pallas_call(
        halve_kernel,
        in_specs=[VMEM] * 5,
        out_specs=[VMEM] * 5,
        out_shape=[
            jax.ShapeDtypeStruct((half, width), F32),
            jax.ShapeDtypeStruct((half, width + extra_columns(half)), BF16),
            jax.ShapeDtypeStruct((half, width), F32),
            jax.ShapeDtypeStruct((half, width), BF16),
            jax.ShapeDtypeStruct(bias_sum.shape, F32),
        ],
        compiler_params=params(16),
    )(up_keep, up_in, down_keep, down_in, bias_sum)


def split_kernel(
    ride, n_table, scale, table_ref, up_keep_ref, up_in_ref, down_keep_ref, down_in_ref, bias_ref,
    own_ref, bias_out_ref, *rest,
):
    sends, store = rest[: n_table - 1], rest[n_table - 1]
    columns = own_ref.shape[2]
    width = up_keep_ref.shape[1]
    pairs = ((up_keep_ref, up_in_ref), (down_keep_ref, down_in_ref))
    for which, (keep, arrived) in enumerate(pairs):
        total = (keep[...] + arrived[:, :width].astype(F32)) * scale
        for table in range(n_table):
            store[table, which] = total[:, table * columns : (table + 1) * columns]
    own_ref[...] = store[table_ref[0]]
    start = -(-columns // EMBED_WIDTH) * EMBED_WIDTH
    bias = bias_ref[...]
    if ride:
        high, low = bias_terms(bias + get_bias(up_in_ref, width))
        bias = high + low
    bias_out_ref[...] = bias
    for shift in range(1, n_table):
        value = store[lax.rem(table_ref[0] + shift, n_table)].astype(BF16)
        sends[shift - 1][:, :, :columns] = value
        if ride:
            sends[shift - 1][0, :BIAS_ROWS, start:] = high.astype(BF16)
            sends[shift - 1][1, :BIAS_ROWS, start:] = low.astype(BF16)


def split_call(table_index, up_keep, up_in, down_keep, down_in, bias_sum, n_table, scale, ride):
    rows, width = up_keep.shape
    columns = width // n_table
    sent = -(-columns // EMBED_WIDTH) * EMBED_WIDTH + EMBED_WIDTH if ride else columns
    return pl.pallas_call(
        functools.partial(split_kernel, ride, n_table, scale),
        in_specs=[SMEM] + [VMEM] * 5,
        out_specs=[VMEM] * (n_table + 1),
        out_shape=[
            jax.ShapeDtypeStruct((2, rows, columns), F32),
            jax.ShapeDtypeStruct(bias_sum.shape, F32),
        ]
        + [jax.ShapeDtypeStruct((2, rows, sent), BF16)] * (n_table - 1),
        scratch_shapes=[pltpu.VMEM((n_table, 2, rows, columns), F32)],
        compiler_params=params(16),
    )(table_index, up_keep, up_in, down_keep, down_in, bias_sum)


def finish_kernel(ride, n_table, scale, table_ref, own_ref, bias_ref, *rest):
    arrived = rest[: n_table - 1]
    up_ref, down_ref, bias_out_ref, store = rest[n_table - 1 :]
    columns = own_ref.shape[2]
    start = -(-columns // EMBED_WIDTH) * EMBED_WIDTH
    up, down = own_ref[0], own_ref[1]
    store[table_ref[0]] = bias_ref[...]
    for shift in range(1, n_table):
        value = arrived[shift - 1]
        up = up + value[0, :, :columns].astype(F32)
        down = down + value[1, :, :columns].astype(F32)
        if ride:
            source = lax.rem(table_ref[0] + n_table - shift, n_table)
            high = value[0, :BIAS_ROWS, start:].astype(F32)
            store[source] = high + value[1, :BIAS_ROWS, start:].astype(F32)
    up_ref[...] = up
    down_ref[...] = down
    total = bias_ref[...]
    if ride:
        total = store[0]
        for table in range(1, n_table):
            total = total + store[table]
    bias_out_ref[...] = total[: bias_out_ref.shape[0]] * scale


def finish_call(table_index, own, bias_sum, arrived, scale, ride):
    n_table = len(arrived) + 1
    _, rows, columns = own.shape
    return pl.pallas_call(
        functools.partial(finish_kernel, ride, n_table, scale),
        in_specs=[SMEM] + [VMEM] * (n_table + 1),
        out_specs=[VMEM] * 3,
        out_shape=[
            jax.ShapeDtypeStruct((rows, columns), F32),
            jax.ShapeDtypeStruct((rows, columns), F32),
            jax.ShapeDtypeStruct((columns * n_table // EMBED_WIDTH, EMBED_WIDTH), F32),
        ],
        scratch_shapes=[pltpu.VMEM((n_table,) + bias_sum.shape, F32)],
        compiler_params=params(16),
    )(table_index, own, bias_sum, *arrived)


def put_rows(ref, high, low):
    wide = ref.shape[1] // EMBED_WIDTH
    first = ref.shape[0] - 8
    ref[first:, :] = jnp.zeros((8, ref.shape[1]), BF16)
    rows = []
    for value in (high, low):
        for row in range(4):
            pieces = [
                value[min(row * wide + k, BIAS_ROWS - 1) : min(row * wide + k, BIAS_ROWS - 1) + 1, :]
                for k in range(wide)
            ]
            rows.append(jnp.concatenate(pieces, axis=1))
    ref[first:, :] = jnp.concatenate(rows, axis=0).astype(BF16)


def get_rows(ref, store):
    wide = ref.shape[1] // EMBED_WIDTH
    value = ref[ref.shape[0] - 8 :, :].astype(F32)
    value = value[:4] + value[4:]
    for place in range(min(4 * wide, BIAS_ROWS)):
        row, k = divmod(place, wide)
        store[place : place + 1, :] = value[row : row + 1, k * EMBED_WIDTH : (k + 1) * EMBED_WIDTH]
    return store[...]


def padded(columns):
    return -(-columns // EMBED_WIDTH) * EMBED_WIDTH


def first_kernel(
    n_table, scale, table_ref, up_keep_ref, up_in_ref, down_keep_ref, down_in_ref, bias_ref,
    keep_ref, send_ref, bias_out_ref, store,
):
    _, _, rows, columns = keep_ref.shape
    width = up_keep_ref.shape[1]
    pairs = ((up_keep_ref, up_in_ref), (down_keep_ref, down_in_ref))
    for which, (keep, arrived) in enumerate(pairs):
        total = (keep[...] + arrived[:, :width].astype(F32)) * scale
        for table in range(n_table):
            store[table, which] = total[:, table * columns : (table + 1) * columns]
    for place in range(n_table // 2):
        keep_ref[place] = store[table_ref[0] ^ (2 * place)]
        for which in range(2):
            first = (2 * place + which) * rows
            value = store[table_ref[0] ^ (2 * place + 1), which]
            send_ref[first : first + rows, :columns] = value.astype(BF16)
    high, low = bias_terms(bias_ref[...] + get_bias(up_in_ref, width))
    put_rows(send_ref, high, low)
    bias_out_ref[...] = high + low


def first_call(table_index, up_keep, up_in, down_keep, down_in, bias_sum, n_table, scale):
    rows, width = up_keep.shape
    columns = width // n_table
    return pl.pallas_call(
        functools.partial(first_kernel, n_table, scale),
        in_specs=[SMEM] + [VMEM] * 5,
        out_specs=[VMEM] * 3,
        out_shape=[
            jax.ShapeDtypeStruct((n_table // 2, 2, rows, columns), F32),
            jax.ShapeDtypeStruct((n_table * rows + 8, padded(columns)), BF16),
            jax.ShapeDtypeStruct(bias_sum.shape, F32),
        ],
        scratch_shapes=[pltpu.VMEM((n_table, 2, rows, columns), F32)],
        compiler_params=params(16),
    )(table_index, up_keep, up_in, down_keep, down_in, bias_sum)


def next_kernel(keep_ref, in_ref, bias_ref, out_ref, send_ref, bias_out_ref, store):
    count, _, rows, columns = keep_ref.shape
    for place in range(count):
        for which in range(2):
            first = (2 * place + which) * rows
            total = keep_ref[place, which] + in_ref[first : first + rows, :columns].astype(F32)
            if place % 2 == 0:
                out_ref[place // 2, which] = total
            else:
                first = (place - 1 + which) * rows
                send_ref[first : first + rows, :columns] = total.astype(BF16)
    store[...] = jnp.zeros_like(store)
    high, low = bias_terms(bias_ref[...] + get_rows(in_ref, store))
    put_rows(send_ref, high, low)
    bias_out_ref[...] = high + low


def next_call(keep, arrived, bias_sum):
    count, _, rows, columns = keep.shape
    return pl.pallas_call(
        next_kernel,
        in_specs=[VMEM] * 3,
        out_specs=[VMEM] * 3,
        out_shape=[
            jax.ShapeDtypeStruct((count // 2, 2, rows, columns), F32),
            jax.ShapeDtypeStruct((count * rows + 8, padded(columns)), BF16),
            jax.ShapeDtypeStruct(bias_sum.shape, F32),
        ],
        scratch_shapes=[pltpu.VMEM(bias_sum.shape, F32)],
        compiler_params=params(16),
    )(keep, arrived, bias_sum)


def last_kernel(scale, keep_ref, in_ref, bias_ref, up_ref, down_ref, bias_out_ref, store):
    rows, columns = up_ref.shape
    up_ref[...] = keep_ref[0, 0] + in_ref[:rows, :columns].astype(F32)
    down_ref[...] = keep_ref[0, 1] + in_ref[rows : 2 * rows, :columns].astype(F32)
    store[...] = jnp.zeros_like(store)
    total = bias_ref[...] + get_rows(in_ref, store)
    bias_out_ref[...] = total[: bias_out_ref.shape[0]] * scale


def last_call(keep, arrived, bias_sum, n_table, scale):
    _, _, rows, columns = keep.shape
    return pl.pallas_call(
        functools.partial(last_kernel, scale),
        in_specs=[VMEM] * 3,
        out_specs=[VMEM] * 3,
        out_shape=[
            jax.ShapeDtypeStruct((rows, columns), F32),
            jax.ShapeDtypeStruct((rows, columns), F32),
            jax.ShapeDtypeStruct((columns * n_table // EMBED_WIDTH, EMBED_WIDTH), F32),
        ],
        scratch_shapes=[pltpu.VMEM(bias_sum.shape, F32)],
        compiler_params=params(16),
    )(keep, arrived, bias_sum)


def rows_kernel(slots, *refs):
    *parts, out_hbm, id_store, row_store, out, sems = refs
    tokens = (parts[0].shape[0] - id_store.shape[1]) // slots
    numbers = lax.broadcasted_iota(jnp.int32, row_store.shape, 0) - EMPTY
    row_store[...] = numbers.astype(F32).astype(BF16)
    for source, part in enumerate(parts):
        id_store[source] = part[slots * tokens :, :].astype(F32)
    copies = []
    for slot in range(slots):
        rows = row_store[...].reshape(TABLE_REACH_ROWS // 16, 16, tokens)
        one, zero = jnp.ones(rows.shape, BF16), jnp.zeros(rows.shape, BF16)
        counts = []
        for source in range(len(parts)):
            count = None
            for entry in range(BAG):
                place = slot * BAG + entry
                ids = jnp.broadcast_to(id_store[source, place : place + 1, :], (16, tokens)).astype(BF16)
                found = jnp.where(rows == ids[None], one, zero)
                count = found if count is None else count + found
            counts.append(count.reshape(TABLE_REACH_ROWS, tokens))
        count = jnp.concatenate(counts, axis=1)
        grad = jnp.concatenate([part[slot * tokens : (slot + 1) * tokens, :] for part in parts], axis=0)
        out[slot] = jnp.dot(count, grad, preferred_element_type=F32)
        copies.append(pltpu.make_async_copy(out.at[slot], out_hbm.at[0, slot], sems.at[slot]))
        copies[-1].start()
    for copy in copies:
        copy.wait()


def rows_call(parts, slots):
    n_table = len(parts)
    id_rows = -(-slots * BAG // 16) * 16
    tokens = (parts[0].shape[0] - id_rows) // slots
    return pl.pallas_call(
        functools.partial(rows_kernel, slots),
        in_specs=[VMEM] * n_table,
        out_specs=ANY,
        out_shape=jax.ShapeDtypeStruct((1, slots, TABLE_REACH_ROWS, EMBED_WIDTH), F32),
        scratch_shapes=[
            pltpu.VMEM((n_table, id_rows, tokens), F32),
            pltpu.VMEM((TABLE_REACH_ROWS, tokens), BF16),
            pltpu.VMEM((slots, TABLE_REACH_ROWS, EMBED_WIDTH), F32),
            pltpu.SemaphoreType.DMA((slots,)),
        ],
        compiler_params=params(16),
        cost_estimate=pl.CostEstimate(
            flops=2 * slots * n_table * tokens * TABLE_REACH_ROWS * EMBED_WIDTH,
            bytes_accessed=4 * slots * TABLE_REACH_ROWS * EMBED_WIDTH,
            transcendentals=0,
        ),
    )(*parts)


def body(
    activations, cotangent, down_weight, up_weight, bias, bag_ids, bag_lengths, feature_table_slot
):
    tokens, width = activations.shape
    rank = down_weight.shape[0]
    n_table = lax.axis_size("table")
    n_rep = lax.axis_size("rep")
    slots = (SPARSE_FEATURES + n_table - 1) // n_table
    scale = 1.0 / math.sqrt(tokens * n_table * n_rep)
    table_index = lax.axis_index("table").astype(jnp.int32).reshape(1)
    rep_index = lax.axis_index("rep").astype(jnp.int32).reshape(1)
    far_bits = [1 << k for k in range(1, n_rep.bit_length() - 1)]
    up_bits, down_bits = [1] + far_bits, [1] + far_bits[::-1]
    ride = rank // n_rep >= BIAS_ROWS

    def swap(value, axis, bit):
        size = n_rep if axis == "rep" else n_table
        return lax.ppermute(value, axis, [(k, k ^ bit) for k in range(size)])

    def shifted(value, shift):
        return lax.ppermute(value, "table", [(k, (k + shift) % n_table) for k in range(n_table)])

    act_other = swap(activations, "rep", 1)
    cot_other = swap(cotangent, "rep", 1)
    keep, send, dense_grad, *parts = input_call(
        table_index, rep_index, feature_table_slot, activations, cotangent, down_weight, up_weight,
        bias.reshape(-1, EMBED_WIDTH), jnp.transpose(bag_ids, (1, 2, 0)), jnp.transpose(bag_lengths, (1, 0)),
        n_table, slots, up_bits, down_bits,
    )
    other = swap(send, "rep", 1)
    parts = [parts[0]] + [shifted(parts[k], k) for k in range(1, n_table)]
    up_keep, up_send, down_keep, down_send, bias_sum = terms_call(
        keep, other, activations, cotangent, act_other, cot_other, ride
    )
    def exchange(place, up_send, down_send, bias_sum):
        up_in = swap(up_send, "rep", up_bits[place])
        down_in = swap(down_send, "rep", down_bits[place])
        if not ride:
            bias_sum = bias_sum + swap(bias_sum, "rep", up_bits[place])
        return up_in, down_in, bias_sum

    def halved(up_keep, up_in, down_keep, down_in, bias_sum):
        if ride:
            return halve_call(up_keep, up_in, down_keep, down_in, bias_sum)
        half = up_keep.shape[0] // 2
        up = up_keep + up_in.astype(F32)
        down = down_keep + down_in.astype(F32)
        return up[:half], up[half:].astype(BF16), down[:half], down[half:].astype(BF16), bias_sum

    def chain(up_keep, up_send, down_keep, down_send, bias_sum):
        for place in range(2, len(up_bits)):
            up_in, down_in, bias_sum = exchange(place, up_send, down_send, bias_sum)
            if place < len(up_bits) - 1:
                up_keep, up_send, down_keep, down_send, bias_sum = halved(
                    up_keep, up_in, down_keep, down_in, bias_sum
                )
        if not ride:
            for bit in [1 << k for k in range(n_table.bit_length() - 1)]:
                bias_sum = bias_sum + swap(bias_sum, "table", bit)
        if not ride:
            return split_call(
                table_index, up_keep, up_in, down_keep, down_in, bias_sum, n_table, scale, ride
            )
        own, message, bias_sum = first_call(
            table_index, up_keep, up_in, down_keep, down_in, bias_sum, n_table, scale
        )
        for bit in [1 << k for k in range(n_table.bit_length() - 2)]:
            message = swap(message, "table", bit)
            own, message, bias_sum = next_call(own, message, bias_sum)
        return [own, bias_sum, message]

    up_in, down_in, bias_sum = exchange(1, up_send, down_send, bias_sum)
    terms = halved(up_keep, up_in, down_keep, down_in, bias_sum)
    shapes = jax.eval_shape(chain, *terms)
    own, bias_sum, *sends = lax.cond(
        feature_table_slot[0] >= 0,
        chain,
        lambda *_: jax.tree.map(lambda x: jnp.zeros(x.shape, x.dtype), shapes),
        *terms,
    )
    if ride:
        message = swap(sends[0], "table", n_table // 2)
        up_grad, down_grad, bias_grad = last_call(own, message, bias_sum, n_table, scale)
    else:
        arrived = [shifted(value, k + 1) for k, value in enumerate(sends)]
        up_grad, down_grad, bias_grad = finish_call(table_index, own, bias_sum, arrived, scale, ride)
    parts, _ = lax.optimization_barrier((parts, own))
    row_grad = rows_call(parts, slots)
    bias_grad = bias_grad.reshape(width)
    return (dense_grad, up_grad, down_grad, bias_grad, row_grad)


def solution(mesh):
    placed = (
        P(("table", "rep"), None),
        P(("table", "rep"), None),
        P(),
        P(),
        P(),
        P(("table", "rep"), None, None),
        P(("table", "rep"), None),
        P(),
    )
    return jax.shard_map(
        body,
        mesh=mesh,
        in_specs=placed,
        out_specs=(
            P(("table", "rep"), None),
            P("rep", "table"),
            P("rep", "table"),
            P(),
            P("rep", "table", None, None),
        ),
        check_vma=False,
    )
```

```python
import functools
import math

import jax
import jax.numpy as jnp
from jax import lax
from jax.experimental import pallas as pl
from jax.experimental.pallas import tpu as pltpu
from jax.sharding import PartitionSpec as P

EMBED_WIDTH = 128
SPARSE_FEATURES = 26
BAG = 4
TABLE_REACH_ROWS = 512
EMPTY = TABLE_REACH_ROWS // 2
BIAS_ROWS = 32
F32 = jnp.float32
BF16 = jnp.bfloat16
MIB = 1024 * 1024
NT = (((1,), (1,)), ((), ()))
ANY = pl.BlockSpec(memory_space=pl.ANY)
VMEM = pl.BlockSpec(memory_space=pltpu.VMEM)
SMEM = pl.BlockSpec(memory_space=pltpu.SMEM)


def params(mib):
    return pltpu.CompilerParams(vmem_limit_bytes=mib * MIB)


def pieces_of(width):
    blocks = width // EMBED_WIDTH
    parts = max(p for p in (9, 3, 1) if blocks % p == 0)
    step = width // parts
    return [(k * step, step) for k in range(parts)]


def order_matrix(rep_index, size, block, bits):
    out_row = lax.broadcasted_iota(jnp.int32, (size, 1), 0)
    in_row = lax.broadcasted_iota(jnp.int32, (size, size), 1)
    source = out_row & (block - 1)
    for place, bit in enumerate(bits):
        unit = size >> (place + 1)
        flag = (out_row >> (unit.bit_length() - 1)) & 1
        own = (rep_index >> (bit.bit_length() - 1)) & 1
        source = source + (flag ^ own) * (bit * block)
    return (source == in_row).astype(F32).astype(BF16)


def input_kernel(
    n_table, slots, up_bits, down_bits, table_ref, rep_ref, owner_ref,
    act_hbm, cot_hbm, down_hbm, up_hbm, bias_ref, ids_ref, length_ref,
    keep, send, dense_ref, *rest,
):
    outs = rest[:n_table]
    act, cot, down, up, store, id_store, feature_ref, in_sems = rest[n_table:]
    tokens, width = act.shape
    rank = down.shape[0]
    half = rank // 2
    pieces = pieces_of(width)
    arrays = ((act_hbm, act), (down_hbm, down), (cot_hbm, cot), (up_hbm, up))
    fetched = []
    for place, (start, size) in enumerate(pieces):
        part = pl.ds(start, size)
        fetched.append(
            [
                pltpu.make_async_copy(source.at[:, part], target.at[:, part], in_sems.at[which, place])
                for which, (source, target) in enumerate(arrays)
            ]
        )
        for copy in fetched[-1]:
            copy.start()
    block = rank >> len(up_bits)
    up_order = order_matrix(rep_ref[0], rank, block, up_bits)
    down_order = order_matrix(rep_ref[0], rank, block, down_bits)
    for place in range(n_table * slots):
        feature_ref[place] = SPARSE_FEATURES
    for feature in range(SPARSE_FEATURES):
        feature_ref[owner_ref[feature]] = feature
    firsts = []
    for shift in range(n_table):
        owner = table_ref[0] + shift
        firsts.append(jnp.where(owner >= n_table, owner - n_table, owner) * slots)
    store[SPARSE_FEATURES + 1] = jnp.zeros(store.shape[1:], BF16)
    id_store[...] = jnp.full(id_store.shape, EMPTY, F32)
    entries = lax.broadcasted_iota(jnp.int32, (BAG, tokens), 0)
    for shift in range(n_table):
        for slot in range(slots):
            feature = feature_ref[firsts[shift] + slot]
            at = jnp.minimum(feature, SPARSE_FEATURES - 1)
            length = jnp.where(feature < SPARSE_FEATURES, length_ref[pl.ds(at, 1), :], 0)
            ids = jnp.where(entries < length, ids_ref[at] - EMPTY, EMPTY)
            id_store[shift, slot * BAG : (slot + 1) * BAG, :] = ids.astype(F32)
        outs[shift][slots * tokens :, :] = id_store[shift].astype(BF16)
    hidden = back = None
    for (start, size), copies in zip(pieces, fetched):
        part = slice(start, start + size)
        for copy in copies:
            copy.wait()
        value = act[:, part]
        term = lax.dot_general(value, down[:, part], NT, preferred_element_type=F32)
        hidden = term if hidden is None else hidden + term
        scaled_b = (cot[:, part].astype(F32) * value.astype(F32)).astype(BF16)
        term = lax.dot_general(scaled_b, up[:, part], NT, preferred_element_type=F32)
        back = term if back is None else back + term
    hidden, back = hidden.astype(BF16), back.astype(BF16)
    rows = lax.dot_general(up_order, hidden, NT, preferred_element_type=F32).astype(BF16)
    keep[0], send[0] = rows[:half], rows[half:]
    rows = lax.dot_general(down_order, back, NT, preferred_element_type=F32).astype(BF16)
    keep[1], send[1] = rows[:half], rows[half:]
    blocks = 3
    for first in range(0, width // EMBED_WIDTH, blocks):
        part = slice(first * EMBED_WIDTH, (first + blocks) * EMBED_WIDTH)
        mixed = jnp.dot(hidden, up[:, part], preferred_element_type=F32)
        tail = jnp.dot(back, down[:, part], preferred_element_type=F32)
        for k in range(blocks):
            place = first + k
            mine = slice(k * EMBED_WIDTH, (k + 1) * EMBED_WIDTH)
            cols = slice(place * EMBED_WIDTH, (place + 1) * EMBED_WIDTH)
            bias = bias_ref[place : place + 1, :]
            grad = cot[:, cols].astype(F32) * (1.0 + (mixed[:, mine] + bias)) + tail[:, mine]
            store[place] = grad.astype(BF16)
    dense_ref[...] = store[0]
    for shift in range(n_table):
        for slot in range(slots):
            rows = slice(slot * tokens, (slot + 1) * tokens)
            outs[shift][rows, :] = store[feature_ref[firsts[shift] + slot] + 1]


def input_call(
    table_index, rep_index, owners, act, cot, down, up, bias, ids, lengths, n_table, slots, up_bits, down_bits
):
    tokens, width = act.shape
    rank = down.shape[0]
    id_rows = -(-slots * BAG // 16) * 16
    sent = slots * tokens + id_rows
    return pl.pallas_call(
        functools.partial(input_kernel, n_table, slots, up_bits, down_bits),
        in_specs=[SMEM, SMEM, SMEM, ANY, ANY, ANY, ANY, VMEM, VMEM, VMEM],
        out_specs=[VMEM] * (3 + n_table),
        out_shape=[
            pltpu.VMEM((2, rank // 2, tokens), BF16),
            pltpu.VMEM((2, rank // 2, tokens), BF16),
            jax.ShapeDtypeStruct((tokens, EMBED_WIDTH), BF16),
        ]
        + [pltpu.VMEM((sent, EMBED_WIDTH), BF16)] * n_table,
        scratch_shapes=[
            pltpu.VMEM((tokens, width), BF16),
            pltpu.VMEM((tokens, width), BF16),
            pltpu.VMEM((rank, width), BF16),
            pltpu.VMEM((rank, width), BF16),
            pltpu.VMEM((SPARSE_FEATURES + 2, tokens, EMBED_WIDTH), BF16),
            pltpu.VMEM((n_table, id_rows, EMBED_WIDTH), F32),
            pltpu.SMEM((n_table * slots,), jnp.int32),
            pltpu.SemaphoreType.DMA((4, len(pieces_of(width)))),
        ],
        compiler_params=params(58),
        cost_estimate=pl.CostEstimate(
            flops=8 * tokens * rank * width, bytes_accessed=4 * (tokens + rank) * width, transcendentals=0
        ),
    )(table_index, rep_index, owners, act, cot, down, up, bias, ids, lengths)


def bias_terms(value):
    high = value.astype(BF16).astype(F32)
    return high, (value - high).astype(BF16).astype(F32)


def put_bias(ref, width, high, low):
    if ref.shape[0] >= 2 * BIAS_ROWS:
        both = jnp.concatenate([high, low], axis=0).astype(BF16)
        ref[: 2 * BIAS_ROWS, width : width + EMBED_WIDTH] = both
    else:
        ref[:BIAS_ROWS, width : width + EMBED_WIDTH] = high.astype(BF16)
        ref[:BIAS_ROWS, width + EMBED_WIDTH : width + 2 * EMBED_WIDTH] = low.astype(BF16)


def get_bias(ref, width):
    if ref.shape[0] >= 2 * BIAS_ROWS:
        both = ref[: 2 * BIAS_ROWS, width : width + EMBED_WIDTH].astype(F32)
        return both[:BIAS_ROWS] + both[BIAS_ROWS:]
    high = ref[:BIAS_ROWS, width : width + EMBED_WIDTH].astype(F32)
    return high + ref[:BIAS_ROWS, width + EMBED_WIDTH : width + 2 * EMBED_WIDTH].astype(F32)


def extra_columns(rows):
    return EMBED_WIDTH if rows >= 2 * BIAS_ROWS else 2 * EMBED_WIDTH


def terms_kernel(
    ride, keep_ref, other_ref, act, cot, act_other, cot_other,
    up_keep_ref, up_send_ref, down_keep_ref, down_send_ref, bias_ref,
):
    width = act.shape[1]
    hidden = jnp.concatenate([keep_ref[0], other_ref[0]], axis=1)
    back = jnp.concatenate([keep_ref[1], other_ref[1]], axis=1)
    blocks = 3
    keep = hidden.shape[0] // 2
    bias_ref[...] = jnp.zeros_like(bias_ref)
    for first in range(0, width // EMBED_WIDTH, blocks):
        part = slice(first * EMBED_WIDTH, (first + blocks) * EMBED_WIDTH)
        values = jnp.concatenate([act[:, part], act_other[:, part]], axis=0)
        grads = jnp.concatenate([cot[:, part], cot_other[:, part]], axis=0)
        scaled = grads.astype(F32) * values.astype(F32)
        sums = jnp.sum(scaled, axis=0, keepdims=True)
        for k in range(blocks):
            bias_ref[first + k : first + k + 1, :] = sums[:, k * EMBED_WIDTH : (k + 1) * EMBED_WIDTH]
        up_part = jnp.dot(hidden, scaled.astype(BF16), preferred_element_type=F32)
        up_keep_ref[:, part] = up_part[:keep]
        up_send_ref[:, part] = up_part[keep:].astype(BF16)
        down_part = jnp.dot(back, values, preferred_element_type=F32)
        down_keep_ref[:, part] = down_part[:keep]
        down_send_ref[:, part] = down_part[keep:].astype(BF16)
    if ride:
        high, low = bias_terms(bias_ref[...])
        put_bias(up_send_ref, width, high, low)
        bias_ref[...] = high + low


def terms_call(keep, other, act, cot, act_other, cot_other, ride):
    tokens, width = act.shape
    rows = keep.shape[1] // 2
    extra = extra_columns(rows) if ride else 0
    return pl.pallas_call(
        functools.partial(terms_kernel, ride),
        in_specs=[VMEM] * 6,
        out_specs=[VMEM] * 5,
        out_shape=[
            jax.ShapeDtypeStruct((rows, width), F32),
            jax.ShapeDtypeStruct((rows, width + extra), BF16),
            jax.ShapeDtypeStruct((rows, width), F32),
            jax.ShapeDtypeStruct((rows, width), BF16),
            jax.ShapeDtypeStruct((BIAS_ROWS, EMBED_WIDTH), F32),
        ],
        compiler_params=params(16),
        cost_estimate=pl.CostEstimate(
            flops=16 * tokens * rows * width, bytes_accessed=8 * tokens * width + 12 * rows * width, transcendentals=0
        ),
    )(keep, other, act, cot, act_other, cot_other)


def halve_kernel(
    up_keep_ref, up_in_ref, down_keep_ref, down_in_ref, bias_ref,
    up_out_ref, up_send_ref, down_out_ref, down_send_ref, bias_out_ref,
):
    rows, width = up_keep_ref.shape
    half = rows // 2
    up = up_keep_ref[...] + up_in_ref[:, :width].astype(F32)
    up_out_ref[...] = up[:half]
    up_send_ref[:, :width] = up[half:].astype(BF16)
    down = down_keep_ref[...] + down_in_ref[...].astype(F32)
    down_out_ref[...] = down[:half]
    down_send_ref[...] = down[half:].astype(BF16)
    high, low = bias_terms(bias_ref[...] + get_bias(up_in_ref, width))
    put_bias(up_send_ref, width, high, low)
    bias_out_ref[...] = high + low


def halve_call(up_keep, up_in, down_keep, down_in, bias_sum):
    rows, width = up_keep.shape
    half = rows // 2
    return pl.pallas_call(
        halve_kernel,
        in_specs=[VMEM] * 5,
        out_specs=[VMEM] * 5,
        out_shape=[
            jax.ShapeDtypeStruct((half, width), F32),
            jax.ShapeDtypeStruct((half, width + extra_columns(half)), BF16),
            jax.ShapeDtypeStruct((half, width), F32),
            jax.ShapeDtypeStruct((half, width), BF16),
            jax.ShapeDtypeStruct(bias_sum.shape, F32),
        ],
        compiler_params=params(16),
    )(up_keep, up_in, down_keep, down_in, bias_sum)


def split_kernel(
    ride, n_table, scale, table_ref, up_keep_ref, up_in_ref, down_keep_ref, down_in_ref, bias_ref,
    own_ref, bias_out_ref, *rest,
):
    sends, store = rest[: n_table - 1], rest[n_table - 1]
    columns = own_ref.shape[2]
    width = up_keep_ref.shape[1]
    pairs = ((up_keep_ref, up_in_ref), (down_keep_ref, down_in_ref))
    for which, (keep, arrived) in enumerate(pairs):
        total = (keep[...] + arrived[:, :width].astype(F32)) * scale
        for table in range(n_table):
            store[table, which] = total[:, table * columns : (table + 1) * columns]
    own_ref[...] = store[table_ref[0]]
    start = -(-columns // EMBED_WIDTH) * EMBED_WIDTH
    bias = bias_ref[...]
    if ride:
        high, low = bias_terms(bias + get_bias(up_in_ref, width))
        bias = high + low
    bias_out_ref[...] = bias
    for shift in range(1, n_table):
        value = store[lax.rem(table_ref[0] + shift, n_table)].astype(BF16)
        sends[shift - 1][:, :, :columns] = value
        if ride:
            sends[shift - 1][0, :BIAS_ROWS, start:] = high.astype(BF16)
            sends[shift - 1][1, :BIAS_ROWS, start:] = low.astype(BF16)


def split_call(table_index, up_keep, up_in, down_keep, down_in, bias_sum, n_table, scale, ride):
    rows, width = up_keep.shape
    columns = width // n_table
    sent = -(-columns // EMBED_WIDTH) * EMBED_WIDTH + EMBED_WIDTH if ride else columns
    return pl.pallas_call(
        functools.partial(split_kernel, ride, n_table, scale),
        in_specs=[SMEM] + [VMEM] * 5,
        out_specs=[VMEM] * (n_table + 1),
        out_shape=[
            jax.ShapeDtypeStruct((2, rows, columns), F32),
            jax.ShapeDtypeStruct(bias_sum.shape, F32),
        ]
        + [jax.ShapeDtypeStruct((2, rows, sent), BF16)] * (n_table - 1),
        scratch_shapes=[pltpu.VMEM((n_table, 2, rows, columns), F32)],
        compiler_params=params(16),
    )(table_index, up_keep, up_in, down_keep, down_in, bias_sum)


def finish_kernel(ride, n_table, scale, table_ref, own_ref, bias_ref, *rest):
    arrived = rest[: n_table - 1]
    up_ref, down_ref, bias_out_ref, store = rest[n_table - 1 :]
    columns = own_ref.shape[2]
    start = -(-columns // EMBED_WIDTH) * EMBED_WIDTH
    up, down = own_ref[0], own_ref[1]
    store[table_ref[0]] = bias_ref[...]
    for shift in range(1, n_table):
        value = arrived[shift - 1]
        up = up + value[0, :, :columns].astype(F32)
        down = down + value[1, :, :columns].astype(F32)
        if ride:
            source = lax.rem(table_ref[0] + n_table - shift, n_table)
            high = value[0, :BIAS_ROWS, start:].astype(F32)
            store[source] = high + value[1, :BIAS_ROWS, start:].astype(F32)
    up_ref[...] = up
    down_ref[...] = down
    total = bias_ref[...]
    if ride:
        total = store[0]
        for table in range(1, n_table):
            total = total + store[table]
    bias_out_ref[...] = total[: bias_out_ref.shape[0]] * scale


def finish_call(table_index, own, bias_sum, arrived, scale, ride):
    n_table = len(arrived) + 1
    _, rows, columns = own.shape
    return pl.pallas_call(
        functools.partial(finish_kernel, ride, n_table, scale),
        in_specs=[SMEM] + [VMEM] * (n_table + 1),
        out_specs=[VMEM] * 3,
        out_shape=[
            jax.ShapeDtypeStruct((rows, columns), F32),
            jax.ShapeDtypeStruct((rows, columns), F32),
            jax.ShapeDtypeStruct((columns * n_table // EMBED_WIDTH, EMBED_WIDTH), F32),
        ],
        scratch_shapes=[pltpu.VMEM((n_table,) + bias_sum.shape, F32)],
        compiler_params=params(16),
    )(table_index, own, bias_sum, *arrived)


def put_rows(ref, high, low):
    wide = ref.shape[1] // EMBED_WIDTH
    first = ref.shape[0] - 8
    ref[first:, :] = jnp.zeros((8, ref.shape[1]), BF16)
    rows = []
    for value in (high, low):
        for row in range(4):
            pieces = [
                value[min(row * wide + k, BIAS_ROWS - 1) : min(row * wide + k, BIAS_ROWS - 1) + 1, :]
                for k in range(wide)
            ]
            rows.append(jnp.concatenate(pieces, axis=1))
    ref[first:, :] = jnp.concatenate(rows, axis=0).astype(BF16)


def get_rows(ref, store):
    wide = ref.shape[1] // EMBED_WIDTH
    value = ref[ref.shape[0] - 8 :, :].astype(F32)
    value = value[:4] + value[4:]
    for place in range(min(4 * wide, BIAS_ROWS)):
        row, k = divmod(place, wide)
        store[place : place + 1, :] = value[row : row + 1, k * EMBED_WIDTH : (k + 1) * EMBED_WIDTH]
    return store[...]


def padded(columns):
    return -(-columns // EMBED_WIDTH) * EMBED_WIDTH


def first_kernel(
    n_table, scale, table_ref, up_keep_ref, up_in_ref, down_keep_ref, down_in_ref, bias_ref,
    keep_ref, send_ref, bias_out_ref, store,
):
    _, _, rows, columns = keep_ref.shape
    width = up_keep_ref.shape[1]
    pairs = ((up_keep_ref, up_in_ref), (down_keep_ref, down_in_ref))
    for which, (keep, arrived) in enumerate(pairs):
        total = (keep[...] + arrived[:, :width].astype(F32)) * scale
        for table in range(n_table):
            store[table, which] = total[:, table * columns : (table + 1) * columns]
    for place in range(n_table // 2):
        keep_ref[place] = store[table_ref[0] ^ (2 * place)]
        for which in range(2):
            first = (2 * place + which) * rows
            value = store[table_ref[0] ^ (2 * place + 1), which]
            send_ref[first : first + rows, :columns] = value.astype(BF16)
    high, low = bias_terms(bias_ref[...] + get_bias(up_in_ref, width))
    put_rows(send_ref, high, low)
    bias_out_ref[...] = high + low


def first_call(table_index, up_keep, up_in, down_keep, down_in, bias_sum, n_table, scale):
    rows, width = up_keep.shape
    columns = width // n_table
    return pl.pallas_call(
        functools.partial(first_kernel, n_table, scale),
        in_specs=[SMEM] + [VMEM] * 5,
        out_specs=[VMEM] * 3,
        out_shape=[
            jax.ShapeDtypeStruct((n_table // 2, 2, rows, columns), F32),
            jax.ShapeDtypeStruct((n_table * rows + 8, padded(columns)), BF16),
            jax.ShapeDtypeStruct(bias_sum.shape, F32),
        ],
        scratch_shapes=[pltpu.VMEM((n_table, 2, rows, columns), F32)],
        compiler_params=params(16),
    )(table_index, up_keep, up_in, down_keep, down_in, bias_sum)


def next_kernel(keep_ref, in_ref, bias_ref, out_ref, send_ref, bias_out_ref, store):
    count, _, rows, columns = keep_ref.shape
    for place in range(count):
        for which in range(2):
            first = (2 * place + which) * rows
            total = keep_ref[place, which] + in_ref[first : first + rows, :columns].astype(F32)
            if place % 2 == 0:
                out_ref[place // 2, which] = total
            else:
                first = (place - 1 + which) * rows
                send_ref[first : first + rows, :columns] = total.astype(BF16)
    store[...] = jnp.zeros_like(store)
    high, low = bias_terms(bias_ref[...] + get_rows(in_ref, store))
    put_rows(send_ref, high, low)
    bias_out_ref[...] = high + low


def next_call(keep, arrived, bias_sum):
    count, _, rows, columns = keep.shape
    return pl.pallas_call(
        next_kernel,
        in_specs=[VMEM] * 3,
        out_specs=[VMEM] * 3,
        out_shape=[
            jax.ShapeDtypeStruct((count // 2, 2, rows, columns), F32),
            jax.ShapeDtypeStruct((count * rows + 8, padded(columns)), BF16),
            jax.ShapeDtypeStruct(bias_sum.shape, F32),
        ],
        scratch_shapes=[pltpu.VMEM(bias_sum.shape, F32)],
        compiler_params=params(16),
    )(keep, arrived, bias_sum)


def last_kernel(scale, keep_ref, in_ref, bias_ref, up_ref, down_ref, bias_out_ref, store):
    rows, columns = up_ref.shape
    up_ref[...] = keep_ref[0, 0] + in_ref[:rows, :columns].astype(F32)
    down_ref[...] = keep_ref[0, 1] + in_ref[rows : 2 * rows, :columns].astype(F32)
    store[...] = jnp.zeros_like(store)
    total = bias_ref[...] + get_rows(in_ref, store)
    bias_out_ref[...] = total[: bias_out_ref.shape[0]] * scale


def last_call(keep, arrived, bias_sum, n_table, scale):
    _, _, rows, columns = keep.shape
    return pl.pallas_call(
        functools.partial(last_kernel, scale),
        in_specs=[VMEM] * 3,
        out_specs=[VMEM] * 3,
        out_shape=[
            jax.ShapeDtypeStruct((rows, columns), F32),
            jax.ShapeDtypeStruct((rows, columns), F32),
            jax.ShapeDtypeStruct((columns * n_table // EMBED_WIDTH, EMBED_WIDTH), F32),
        ],
        scratch_shapes=[pltpu.VMEM(bias_sum.shape, F32)],
        compiler_params=params(16),
    )(keep, arrived, bias_sum)


def rows_kernel(slots, *refs):
    *parts, out_hbm, id_store, row_store, out, sems = refs
    tokens = (parts[0].shape[0] - id_store.shape[1]) // slots
    numbers = lax.broadcasted_iota(jnp.int32, row_store.shape, 0) - EMPTY
    row_store[...] = numbers.astype(F32).astype(BF16)
    for source, part in enumerate(parts):
        id_store[source] = part[slots * tokens :, :].astype(F32)
    copies = []
    for slot in range(slots):
        rows = row_store[...].reshape(TABLE_REACH_ROWS // 16, 16, tokens)
        one, zero = jnp.ones(rows.shape, BF16), jnp.zeros(rows.shape, BF16)
        counts = []
        for source in range(len(parts)):
            count = None
            for entry in range(BAG):
                place = slot * BAG + entry
                ids = jnp.broadcast_to(id_store[source, place : place + 1, :], (16, tokens)).astype(BF16)
                found = jnp.where(rows == ids[None], one, zero)
                count = found if count is None else count + found
            counts.append(count.reshape(TABLE_REACH_ROWS, tokens))
        count = jnp.concatenate(counts, axis=1)
        grad = jnp.concatenate([part[slot * tokens : (slot + 1) * tokens, :] for part in parts], axis=0)
        out[slot] = jnp.dot(count, grad, preferred_element_type=F32)
        copies.append(pltpu.make_async_copy(out.at[slot], out_hbm.at[0, slot], sems.at[slot]))
        copies[-1].start()
    for copy in copies:
        copy.wait()


def rows_call(parts, slots):
    n_table = len(parts)
    id_rows = -(-slots * BAG // 16) * 16
    tokens = (parts[0].shape[0] - id_rows) // slots
    return pl.pallas_call(
        functools.partial(rows_kernel, slots),
        in_specs=[VMEM] * n_table,
        out_specs=ANY,
        out_shape=jax.ShapeDtypeStruct((1, slots, TABLE_REACH_ROWS, EMBED_WIDTH), F32),
        scratch_shapes=[
            pltpu.VMEM((n_table, id_rows, tokens), F32),
            pltpu.VMEM((TABLE_REACH_ROWS, tokens), BF16),
            pltpu.VMEM((slots, TABLE_REACH_ROWS, EMBED_WIDTH), F32),
            pltpu.SemaphoreType.DMA((slots,)),
        ],
        compiler_params=params(16),
        cost_estimate=pl.CostEstimate(
            flops=2 * slots * n_table * tokens * TABLE_REACH_ROWS * EMBED_WIDTH,
            bytes_accessed=4 * slots * TABLE_REACH_ROWS * EMBED_WIDTH,
            transcendentals=0,
        ),
    )(*parts)


def body(
    activations, cotangent, down_weight, up_weight, bias, bag_ids, bag_lengths, feature_table_slot
):
    tokens, width = activations.shape
    rank = down_weight.shape[0]
    n_table = lax.axis_size("table")
    n_rep = lax.axis_size("rep")
    slots = (SPARSE_FEATURES + n_table - 1) // n_table
    scale = 1.0 / math.sqrt(tokens * n_table * n_rep)
    table_index = lax.axis_index("table").astype(jnp.int32).reshape(1)
    rep_index = lax.axis_index("rep").astype(jnp.int32).reshape(1)
    far_bits = [1 << k for k in range(1, n_rep.bit_length() - 1)]
    up_bits, down_bits = [1] + far_bits, [1] + far_bits[::-1]
    ride = rank // n_rep >= BIAS_ROWS

    def swap(value, axis, bit):
        size = n_rep if axis == "rep" else n_table
        return lax.ppermute(value, axis, [(k, k ^ bit) for k in range(size)])

    def shifted(value, shift):
        return lax.ppermute(value, "table", [(k, (k + shift) % n_table) for k in range(n_table)])

    act_other = swap(activations, "rep", 1)
    cot_other = swap(cotangent, "rep", 1)
    keep, send, dense_grad, *parts = input_call(
        table_index, rep_index, feature_table_slot, activations, cotangent, down_weight, up_weight,
        bias.reshape(-1, EMBED_WIDTH), jnp.transpose(bag_ids, (1, 2, 0)), jnp.transpose(bag_lengths, (1, 0)),
        n_table, slots, up_bits, down_bits,
    )
    other = swap(send, "rep", 1)
    parts = [parts[0]] + [shifted(parts[k], k) for k in range(1, n_table)]
    up_keep, up_send, down_keep, down_send, bias_sum = terms_call(
        keep, other, activations, cotangent, act_other, cot_other, ride
    )
    def exchange(place, up_send, down_send, bias_sum):
        up_in = swap(up_send, "rep", up_bits[place])
        down_in = swap(down_send, "rep", down_bits[place])
        if not ride:
            bias_sum = bias_sum + swap(bias_sum, "rep", up_bits[place])
        return up_in, down_in, bias_sum

    def halved(up_keep, up_in, down_keep, down_in, bias_sum):
        if ride:
            return halve_call(up_keep, up_in, down_keep, down_in, bias_sum)
        half = up_keep.shape[0] // 2
        up = up_keep + up_in.astype(F32)
        down = down_keep + down_in.astype(F32)
        return up[:half], up[half:].astype(BF16), down[:half], down[half:].astype(BF16), bias_sum

    def chain(up_keep, up_send, down_keep, down_send, bias_sum):
        for place in range(2, len(up_bits)):
            up_in, down_in, bias_sum = exchange(place, up_send, down_send, bias_sum)
            if place < len(up_bits) - 1:
                up_keep, up_send, down_keep, down_send, bias_sum = halved(
                    up_keep, up_in, down_keep, down_in, bias_sum
                )
        if not ride:
            for bit in [1 << k for k in range(n_table.bit_length() - 1)]:
                bias_sum = bias_sum + swap(bias_sum, "table", bit)
        if not ride:
            return split_call(
                table_index, up_keep, up_in, down_keep, down_in, bias_sum, n_table, scale, ride
            )
        own, message, bias_sum = first_call(
            table_index, up_keep, up_in, down_keep, down_in, bias_sum, n_table, scale
        )
        for bit in [1 << k for k in range(n_table.bit_length() - 2)]:
            message = swap(message, "table", bit)
            own, message, bias_sum = next_call(own, message, bias_sum)
        return [own, bias_sum, message]

    up_in, down_in, bias_sum = exchange(1, up_send, down_send, bias_sum)
    terms = halved(up_keep, up_in, down_keep, down_in, bias_sum)
    shapes = jax.eval_shape(chain, *terms)
    own, bias_sum, *sends = lax.cond(
        feature_table_slot[0] >= 0,
        chain,
        lambda *_: jax.tree.map(lambda x: jnp.zeros(x.shape, x.dtype), shapes),
        *terms,
    )
    if ride:
        message = swap(sends[0], "table", n_table // 2)
        up_grad, down_grad, bias_grad = last_call(own, message, bias_sum, n_table, scale)
    else:
        arrived = [shifted(value, k + 1) for k, value in enumerate(sends)]
        up_grad, down_grad, bias_grad = finish_call(table_index, own, bias_sum, arrived, scale, ride)
    parts, _ = lax.optimization_barrier((parts, own))
    row_grad = rows_call(parts, slots)
    bias_grad = bias_grad.reshape(width)
    return (dense_grad, up_grad, down_grad, bias_grad, row_grad)


def solution(mesh):
    placed = (
        P(("table", "rep"), None),
        P(("table", "rep"), None),
        P(),
        P(),
        P(),
        P(("table", "rep"), None, None),
        P(("table", "rep"), None),
        P(),
    )
    return jax.shard_map(
        body,
        mesh=mesh,
        in_specs=placed,
        out_specs=(
            P(("table", "rep"), None),
            P("rep", "table"),
            P("rep", "table"),
            P(),
            P("rep", "table", None, None),
        ),
        check_vma=False,
    )
```

```python
import functools
import math

import jax
import jax.numpy as jnp
from jax import lax
from jax.experimental import pallas as pl
from jax.experimental.pallas import tpu as pltpu
from jax.sharding import PartitionSpec as P

EMBED_WIDTH = 128
SPARSE_FEATURES = 26
BAG = 4
TABLE_REACH_ROWS = 512
EMPTY = TABLE_REACH_ROWS // 2
BIAS_ROWS = 32
F32 = jnp.float32
BF16 = jnp.bfloat16
MIB = 1024 * 1024
NT = (((1,), (1,)), ((), ()))
ANY = pl.BlockSpec(memory_space=pl.ANY)
VMEM = pl.BlockSpec(memory_space=pltpu.VMEM)
SMEM = pl.BlockSpec(memory_space=pltpu.SMEM)


def params(mib):
    return pltpu.CompilerParams(vmem_limit_bytes=mib * MIB)


def pieces_of(width):
    blocks = width // EMBED_WIDTH
    parts = max(p for p in (9, 3, 1) if blocks % p == 0)
    step = width // parts
    return [(k * step, step) for k in range(parts)]


def order_matrix(rep_index, size, block, bits):
    out_row = lax.broadcasted_iota(jnp.int32, (size, 1), 0)
    in_row = lax.broadcasted_iota(jnp.int32, (size, size), 1)
    source = out_row & (block - 1)
    for place, bit in enumerate(bits):
        unit = size >> (place + 1)
        flag = (out_row >> (unit.bit_length() - 1)) & 1
        own = (rep_index >> (bit.bit_length() - 1)) & 1
        source = source + (flag ^ own) * (bit * block)
    return (source == in_row).astype(F32).astype(BF16)


def input_kernel(
    n_table, slots, up_bits, down_bits, table_ref, rep_ref, owner_ref,
    act_hbm, cot_hbm, down_hbm, up_hbm, bias_ref, ids_ref, length_ref,
    act, cot, keep, send, dense_ref, *rest,
):
    outs = rest[:n_table]
    down, up, store, id_store, feature_ref, in_sems = rest[n_table:]
    tokens, width = act.shape
    rank = down.shape[0]
    half = rank // 2
    pieces = pieces_of(width)
    arrays = ((act_hbm, act), (down_hbm, down), (cot_hbm, cot), (up_hbm, up))
    fetched = []
    for place, (start, size) in enumerate(pieces):
        part = pl.ds(start, size)
        fetched.append(
            [
                pltpu.make_async_copy(source.at[:, part], target.at[:, part], in_sems.at[which, place])
                for which, (source, target) in enumerate(arrays)
            ]
        )
        for copy in fetched[-1]:
            copy.start()
    block = rank >> len(up_bits)
    up_order = order_matrix(rep_ref[0], rank, block, up_bits)
    down_order = order_matrix(rep_ref[0], rank, block, down_bits)
    for place in range(n_table * slots):
        feature_ref[place] = SPARSE_FEATURES
    for feature in range(SPARSE_FEATURES):
        feature_ref[owner_ref[feature]] = feature
    firsts = []
    for shift in range(n_table):
        owner = table_ref[0] + shift
        firsts.append(jnp.where(owner >= n_table, owner - n_table, owner) * slots)
    store[SPARSE_FEATURES + 1] = jnp.zeros(store.shape[1:], BF16)
    id_store[...] = jnp.full(id_store.shape, EMPTY, F32)
    entries = lax.broadcasted_iota(jnp.int32, (BAG, tokens), 0)
    for shift in range(n_table):
        for slot in range(slots):
            feature = feature_ref[firsts[shift] + slot]
            at = jnp.minimum(feature, SPARSE_FEATURES - 1)
            length = jnp.where(feature < SPARSE_FEATURES, length_ref[pl.ds(at, 1), :], 0)
            ids = jnp.where(entries < length, ids_ref[at] - EMPTY, EMPTY)
            id_store[shift, slot * BAG : (slot + 1) * BAG, :] = ids.astype(F32)
        outs[shift][slots * tokens :, :] = id_store[shift].astype(BF16)
    hidden = back = None
    for (start, size), copies in zip(pieces, fetched):
        part = slice(start, start + size)
        for copy in copies:
            copy.wait()
        value = act[:, part]
        term = lax.dot_general(value, down[:, part], NT, preferred_element_type=F32)
        hidden = term if hidden is None else hidden + term
        scaled_b = (cot[:, part].astype(F32) * value.astype(F32)).astype(BF16)
        term = lax.dot_general(scaled_b, up[:, part], NT, preferred_element_type=F32)
        back = term if back is None else back + term
    hidden, back = hidden.astype(BF16), back.astype(BF16)
    rows = lax.dot_general(up_order, hidden, NT, preferred_element_type=F32).astype(BF16)
    keep[0], send[0] = rows[:half], rows[half:]
    rows = lax.dot_general(down_order, back, NT, preferred_element_type=F32).astype(BF16)
    keep[1], send[1] = rows[:half], rows[half:]
    blocks = 3
    for first in range(0, width // EMBED_WIDTH, blocks):
        part = slice(first * EMBED_WIDTH, (first + blocks) * EMBED_WIDTH)
        mixed = jnp.dot(hidden, up[:, part], preferred_element_type=F32)
        tail = jnp.dot(back, down[:, part], preferred_element_type=F32)
        for k in range(blocks):
            place = first + k
            mine = slice(k * EMBED_WIDTH, (k + 1) * EMBED_WIDTH)
            cols = slice(place * EMBED_WIDTH, (place + 1) * EMBED_WIDTH)
            bias = bias_ref[place : place + 1, :]
            grad = cot[:, cols].astype(F32) * (1.0 + (mixed[:, mine] + bias)) + tail[:, mine]
            store[place] = grad.astype(BF16)
    dense_ref[...] = store[0]
    for shift in range(n_table):
        for slot in range(slots):
            rows = slice(slot * tokens, (slot + 1) * tokens)
            outs[shift][rows, :] = store[feature_ref[firsts[shift] + slot] + 1]


def input_call(
    table_index, rep_index, owners, act, cot, down, up, bias, ids, lengths, n_table, slots, up_bits, down_bits
):
    tokens, width = act.shape
    rank = down.shape[0]
    id_rows = -(-slots * BAG // 16) * 16
    sent = slots * tokens + id_rows
    return pl.pallas_call(
        functools.partial(input_kernel, n_table, slots, up_bits, down_bits),
        in_specs=[SMEM, SMEM, SMEM, ANY, ANY, ANY, ANY, VMEM, VMEM, VMEM],
        out_specs=[VMEM] * (5 + n_table),
        out_shape=[
            pltpu.VMEM((tokens, width), BF16),
            pltpu.VMEM((tokens, width), BF16),
            pltpu.VMEM((2, rank // 2, tokens), BF16),
            pltpu.VMEM((2, rank // 2, tokens), BF16),
            jax.ShapeDtypeStruct((tokens, EMBED_WIDTH), BF16),
        ]
        + [pltpu.VMEM((sent, EMBED_WIDTH), BF16)] * n_table,
        scratch_shapes=[
            pltpu.VMEM((rank, width), BF16),
            pltpu.VMEM((rank, width), BF16),
            pltpu.VMEM((SPARSE_FEATURES + 2, tokens, EMBED_WIDTH), BF16),
            pltpu.VMEM((n_table, id_rows, EMBED_WIDTH), F32),
            pltpu.SMEM((n_table * slots,), jnp.int32),
            pltpu.SemaphoreType.DMA((4, len(pieces_of(width)))),
        ],
        compiler_params=params(57),
        cost_estimate=pl.CostEstimate(
            flops=8 * tokens * rank * width, bytes_accessed=4 * (tokens + rank) * width, transcendentals=0
        ),
    )(table_index, rep_index, owners, act, cot, down, up, bias, ids, lengths)


def bias_terms(value):
    high = value.astype(BF16).astype(F32)
    return high, (value - high).astype(BF16).astype(F32)


def put_bias(ref, width, high, low):
    if ref.shape[0] >= 2 * BIAS_ROWS:
        both = jnp.concatenate([high, low], axis=0).astype(BF16)
        ref[: 2 * BIAS_ROWS, width : width + EMBED_WIDTH] = both
    else:
        ref[:BIAS_ROWS, width : width + EMBED_WIDTH] = high.astype(BF16)
        ref[:BIAS_ROWS, width + EMBED_WIDTH : width + 2 * EMBED_WIDTH] = low.astype(BF16)


def get_bias(ref, width):
    if ref.shape[0] >= 2 * BIAS_ROWS:
        both = ref[: 2 * BIAS_ROWS, width : width + EMBED_WIDTH].astype(F32)
        return both[:BIAS_ROWS] + both[BIAS_ROWS:]
    high = ref[:BIAS_ROWS, width : width + EMBED_WIDTH].astype(F32)
    return high + ref[:BIAS_ROWS, width + EMBED_WIDTH : width + 2 * EMBED_WIDTH].astype(F32)


def extra_columns(rows):
    return EMBED_WIDTH if rows >= 2 * BIAS_ROWS else 2 * EMBED_WIDTH


def terms_kernel(
    ride, keep_ref, other_ref, act, cot, act_other, cot_other,
    up_keep_ref, up_send_ref, down_keep_ref, down_send_ref, bias_ref,
):
    width = act.shape[1]
    hidden = jnp.concatenate([keep_ref[0], other_ref[0]], axis=1)
    back = jnp.concatenate([keep_ref[1], other_ref[1]], axis=1)
    blocks = 3
    keep = hidden.shape[0] // 2
    bias_ref[...] = jnp.zeros_like(bias_ref)
    for first in range(0, width // EMBED_WIDTH, blocks):
        part = slice(first * EMBED_WIDTH, (first + blocks) * EMBED_WIDTH)
        values = jnp.concatenate([act[:, part], act_other[:, part]], axis=0)
        grads = jnp.concatenate([cot[:, part], cot_other[:, part]], axis=0)
        scaled = grads.astype(F32) * values.astype(F32)
        sums = jnp.sum(scaled, axis=0, keepdims=True)
        for k in range(blocks):
            bias_ref[first + k : first + k + 1, :] = sums[:, k * EMBED_WIDTH : (k + 1) * EMBED_WIDTH]
        up_part = jnp.dot(hidden, scaled.astype(BF16), preferred_element_type=F32)
        up_keep_ref[:, part] = up_part[:keep]
        up_send_ref[:, part] = up_part[keep:].astype(BF16)
        down_part = jnp.dot(back, values, preferred_element_type=F32)
        down_keep_ref[:, part] = down_part[:keep]
        down_send_ref[:, part] = down_part[keep:].astype(BF16)
    if ride:
        high, low = bias_terms(bias_ref[...])
        put_bias(up_send_ref, width, high, low)
        bias_ref[...] = high + low


def terms_call(keep, other, act, cot, act_other, cot_other, ride):
    tokens, width = act.shape
    rows = keep.shape[1] // 2
    extra = extra_columns(rows) if ride else 0
    return pl.pallas_call(
        functools.partial(terms_kernel, ride),
        in_specs=[VMEM] * 6,
        out_specs=[VMEM] * 5,
        out_shape=[
            jax.ShapeDtypeStruct((rows, width), F32),
            jax.ShapeDtypeStruct((rows, width + extra), BF16),
            jax.ShapeDtypeStruct((rows, width), F32),
            jax.ShapeDtypeStruct((rows, width), BF16),
            jax.ShapeDtypeStruct((BIAS_ROWS, EMBED_WIDTH), F32),
        ],
        compiler_params=params(16),
        cost_estimate=pl.CostEstimate(
            flops=16 * tokens * rows * width, bytes_accessed=8 * tokens * width + 12 * rows * width, transcendentals=0
        ),
    )(keep, other, act, cot, act_other, cot_other)


def halve_kernel(
    up_keep_ref, up_in_ref, down_keep_ref, down_in_ref, bias_ref,
    up_out_ref, up_send_ref, down_out_ref, down_send_ref, bias_out_ref,
):
    rows, width = up_keep_ref.shape
    half = rows // 2
    up = up_keep_ref[...] + up_in_ref[:, :width].astype(F32)
    up_out_ref[...] = up[:half]
    up_send_ref[:, :width] = up[half:].astype(BF16)
    down = down_keep_ref[...] + down_in_ref[...].astype(F32)
    down_out_ref[...] = down[:half]
    down_send_ref[...] = down[half:].astype(BF16)
    high, low = bias_terms(bias_ref[...] + get_bias(up_in_ref, width))
    put_bias(up_send_ref, width, high, low)
    bias_out_ref[...] = high + low


def halve_call(up_keep, up_in, down_keep, down_in, bias_sum):
    rows, width = up_keep.shape
    half = rows // 2
    return pl.pallas_call(
        halve_kernel,
        in_specs=[VMEM] * 5,
        out_specs=[VMEM] * 5,
        out_shape=[
            jax.ShapeDtypeStruct((half, width), F32),
            jax.ShapeDtypeStruct((half, width + extra_columns(half)), BF16),
            jax.ShapeDtypeStruct((half, width), F32),
            jax.ShapeDtypeStruct((half, width), BF16),
            jax.ShapeDtypeStruct(bias_sum.shape, F32),
        ],
        compiler_params=params(16),
    )(up_keep, up_in, down_keep, down_in, bias_sum)


def split_kernel(
    ride, n_table, scale, table_ref, up_keep_ref, up_in_ref, down_keep_ref, down_in_ref, bias_ref,
    own_ref, bias_out_ref, *rest,
):
    sends, store = rest[: n_table - 1], rest[n_table - 1]
    columns = own_ref.shape[2]
    width = up_keep_ref.shape[1]
    pairs = ((up_keep_ref, up_in_ref), (down_keep_ref, down_in_ref))
    for which, (keep, arrived) in enumerate(pairs):
        total = (keep[...] + arrived[:, :width].astype(F32)) * scale
        for table in range(n_table):
            store[table, which] = total[:, table * columns : (table + 1) * columns]
    own_ref[...] = store[table_ref[0]]
    start = -(-columns // EMBED_WIDTH) * EMBED_WIDTH
    bias = bias_ref[...]
    if ride:
        high, low = bias_terms(bias + get_bias(up_in_ref, width))
        bias = high + low
    bias_out_ref[...] = bias
    for shift in range(1, n_table):
        value = store[lax.rem(table_ref[0] + shift, n_table)].astype(BF16)
        sends[shift - 1][:, :, :columns] = value
        if ride:
            sends[shift - 1][0, :BIAS_ROWS, start:] = high.astype(BF16)
            sends[shift - 1][1, :BIAS_ROWS, start:] = low.astype(BF16)


def split_call(table_index, up_keep, up_in, down_keep, down_in, bias_sum, n_table, scale, ride):
    rows, width = up_keep.shape
    columns = width // n_table
    sent = -(-columns // EMBED_WIDTH) * EMBED_WIDTH + EMBED_WIDTH if ride else columns
    return pl.pallas_call(
        functools.partial(split_kernel, ride, n_table, scale),
        in_specs=[SMEM] + [VMEM] * 5,
        out_specs=[VMEM] * (n_table + 1),
        out_shape=[
            jax.ShapeDtypeStruct((2, rows, columns), F32),
            jax.ShapeDtypeStruct(bias_sum.shape, F32),
        ]
        + [jax.ShapeDtypeStruct((2, rows, sent), BF16)] * (n_table - 1),
        scratch_shapes=[pltpu.VMEM((n_table, 2, rows, columns), F32)],
        compiler_params=params(16),
    )(table_index, up_keep, up_in, down_keep, down_in, bias_sum)


def finish_kernel(ride, n_table, scale, table_ref, own_ref, bias_ref, *rest):
    arrived = rest[: n_table - 1]
    up_ref, down_ref, bias_out_ref, store = rest[n_table - 1 :]
    columns = own_ref.shape[2]
    start = -(-columns // EMBED_WIDTH) * EMBED_WIDTH
    up, down = own_ref[0], own_ref[1]
    store[table_ref[0]] = bias_ref[...]
    for shift in range(1, n_table):
        value = arrived[shift - 1]
        up = up + value[0, :, :columns].astype(F32)
        down = down + value[1, :, :columns].astype(F32)
        if ride:
            source = lax.rem(table_ref[0] + n_table - shift, n_table)
            high = value[0, :BIAS_ROWS, start:].astype(F32)
            store[source] = high + value[1, :BIAS_ROWS, start:].astype(F32)
    up_ref[...] = up
    down_ref[...] = down
    total = bias_ref[...]
    if ride:
        total = store[0]
        for table in range(1, n_table):
            total = total + store[table]
    bias_out_ref[...] = total[: bias_out_ref.shape[0]] * scale


def finish_call(table_index, own, bias_sum, arrived, scale, ride):
    n_table = len(arrived) + 1
    _, rows, columns = own.shape
    return pl.pallas_call(
        functools.partial(finish_kernel, ride, n_table, scale),
        in_specs=[SMEM] + [VMEM] * (n_table + 1),
        out_specs=[VMEM] * 3,
        out_shape=[
            jax.ShapeDtypeStruct((rows, columns), F32),
            jax.ShapeDtypeStruct((rows, columns), F32),
            jax.ShapeDtypeStruct((columns * n_table // EMBED_WIDTH, EMBED_WIDTH), F32),
        ],
        scratch_shapes=[pltpu.VMEM((n_table,) + bias_sum.shape, F32)],
        compiler_params=params(16),
    )(table_index, own, bias_sum, *arrived)


def put_rows(ref, high, low):
    wide = ref.shape[1] // EMBED_WIDTH
    first = ref.shape[0] - 8
    ref[first:, :] = jnp.zeros((8, ref.shape[1]), BF16)
    rows = []
    for value in (high, low):
        for row in range(4):
            pieces = [
                value[min(row * wide + k, BIAS_ROWS - 1) : min(row * wide + k, BIAS_ROWS - 1) + 1, :]
                for k in range(wide)
            ]
            rows.append(jnp.concatenate(pieces, axis=1))
    ref[first:, :] = jnp.concatenate(rows, axis=0).astype(BF16)


def get_rows(ref, store):
    wide = ref.shape[1] // EMBED_WIDTH
    value = ref[ref.shape[0] - 8 :, :].astype(F32)
    value = value[:4] + value[4:]
    for place in range(min(4 * wide, BIAS_ROWS)):
        row, k = divmod(place, wide)
        store[place : place + 1, :] = value[row : row + 1, k * EMBED_WIDTH : (k + 1) * EMBED_WIDTH]
    return store[...]


def padded(columns):
    return -(-columns // EMBED_WIDTH) * EMBED_WIDTH


def first_kernel(
    n_table, scale, table_ref, up_keep_ref, up_in_ref, down_keep_ref, down_in_ref, bias_ref,
    keep_ref, send_ref, bias_out_ref, store,
):
    _, _, rows, columns = keep_ref.shape
    width = up_keep_ref.shape[1]
    pairs = ((up_keep_ref, up_in_ref), (down_keep_ref, down_in_ref))
    for which, (keep, arrived) in enumerate(pairs):
        total = (keep[...] + arrived[:, :width].astype(F32)) * scale
        for table in range(n_table):
            store[table, which] = total[:, table * columns : (table + 1) * columns]
    for place in range(n_table // 2):
        keep_ref[place] = store[table_ref[0] ^ (2 * place)]
        for which in range(2):
            first = (2 * place + which) * rows
            value = store[table_ref[0] ^ (2 * place + 1), which]
            send_ref[first : first + rows, :columns] = value.astype(BF16)
    high, low = bias_terms(bias_ref[...] + get_bias(up_in_ref, width))
    put_rows(send_ref, high, low)
    bias_out_ref[...] = high + low


def first_call(table_index, up_keep, up_in, down_keep, down_in, bias_sum, n_table, scale):
    rows, width = up_keep.shape
    columns = width // n_table
    return pl.pallas_call(
        functools.partial(first_kernel, n_table, scale),
        in_specs=[SMEM] + [VMEM] * 5,
        out_specs=[VMEM] * 3,
        out_shape=[
            jax.ShapeDtypeStruct((n_table // 2, 2, rows, columns), F32),
            jax.ShapeDtypeStruct((n_table * rows + 8, padded(columns)), BF16),
            jax.ShapeDtypeStruct(bias_sum.shape, F32),
        ],
        scratch_shapes=[pltpu.VMEM((n_table, 2, rows, columns), F32)],
        compiler_params=params(16),
    )(table_index, up_keep, up_in, down_keep, down_in, bias_sum)


def next_kernel(keep_ref, in_ref, bias_ref, out_ref, send_ref, bias_out_ref, store):
    count, _, rows, columns = keep_ref.shape
    for place in range(count):
        for which in range(2):
            first = (2 * place + which) * rows
            total = keep_ref[place, which] + in_ref[first : first + rows, :columns].astype(F32)
            if place % 2 == 0:
                out_ref[place // 2, which] = total
            else:
                first = (place - 1 + which) * rows
                send_ref[first : first + rows, :columns] = total.astype(BF16)
    store[...] = jnp.zeros_like(store)
    high, low = bias_terms(bias_ref[...] + get_rows(in_ref, store))
    put_rows(send_ref, high, low)
    bias_out_ref[...] = high + low


def next_call(keep, arrived, bias_sum):
    count, _, rows, columns = keep.shape
    return pl.pallas_call(
        next_kernel,
        in_specs=[VMEM] * 3,
        out_specs=[VMEM] * 3,
        out_shape=[
            jax.ShapeDtypeStruct((count // 2, 2, rows, columns), F32),
            jax.ShapeDtypeStruct((count * rows + 8, padded(columns)), BF16),
            jax.ShapeDtypeStruct(bias_sum.shape, F32),
        ],
        scratch_shapes=[pltpu.VMEM(bias_sum.shape, F32)],
        compiler_params=params(16),
    )(keep, arrived, bias_sum)


def last_kernel(scale, keep_ref, in_ref, bias_ref, up_ref, down_ref, bias_out_ref, store):
    rows, columns = up_ref.shape
    up_ref[...] = keep_ref[0, 0] + in_ref[:rows, :columns].astype(F32)
    down_ref[...] = keep_ref[0, 1] + in_ref[rows : 2 * rows, :columns].astype(F32)
    store[...] = jnp.zeros_like(store)
    total = bias_ref[...] + get_rows(in_ref, store)
    bias_out_ref[...] = total[: bias_out_ref.shape[0]] * scale


def last_call(keep, arrived, bias_sum, n_table, scale):
    _, _, rows, columns = keep.shape
    return pl.pallas_call(
        functools.partial(last_kernel, scale),
        in_specs=[VMEM] * 3,
        out_specs=[VMEM] * 3,
        out_shape=[
            jax.ShapeDtypeStruct((rows, columns), F32),
            jax.ShapeDtypeStruct((rows, columns), F32),
            jax.ShapeDtypeStruct((columns * n_table // EMBED_WIDTH, EMBED_WIDTH), F32),
        ],
        scratch_shapes=[pltpu.VMEM(bias_sum.shape, F32)],
        compiler_params=params(16),
    )(keep, arrived, bias_sum)


def rows_kernel(slots, *refs):
    *parts, out_hbm, id_store, row_store, out, sems = refs
    tokens = (parts[0].shape[0] - id_store.shape[1]) // slots
    numbers = lax.broadcasted_iota(jnp.int32, row_store.shape, 0) - EMPTY
    row_store[...] = numbers.astype(F32).astype(BF16)
    for source, part in enumerate(parts):
        id_store[source] = part[slots * tokens :, :].astype(F32)
    copies = []
    for slot in range(slots):
        rows = row_store[...].reshape(TABLE_REACH_ROWS // 16, 16, tokens)
        one, zero = jnp.ones(rows.shape, BF16), jnp.zeros(rows.shape, BF16)
        counts = []
        for source in range(len(parts)):
            count = None
            for entry in range(BAG):
                place = slot * BAG + entry
                ids = jnp.broadcast_to(id_store[source, place : place + 1, :], (16, tokens)).astype(BF16)
                found = jnp.where(rows == ids[None], one, zero)
                count = found if count is None else count + found
            counts.append(count.reshape(TABLE_REACH_ROWS, tokens))
        count = jnp.concatenate(counts, axis=1)
        grad = jnp.concatenate([part[slot * tokens : (slot + 1) * tokens, :] for part in parts], axis=0)
        out[slot] = jnp.dot(count, grad, preferred_element_type=F32)
        copies.append(pltpu.make_async_copy(out.at[slot], out_hbm.at[0, slot], sems.at[slot]))
        copies[-1].start()
    for copy in copies:
        copy.wait()


def rows_call(parts, slots):
    n_table = len(parts)
    id_rows = -(-slots * BAG // 16) * 16
    tokens = (parts[0].shape[0] - id_rows) // slots
    return pl.pallas_call(
        functools.partial(rows_kernel, slots),
        in_specs=[VMEM] * n_table,
        out_specs=ANY,
        out_shape=jax.ShapeDtypeStruct((1, slots, TABLE_REACH_ROWS, EMBED_WIDTH), F32),
        scratch_shapes=[
            pltpu.VMEM((n_table, id_rows, tokens), F32),
            pltpu.VMEM((TABLE_REACH_ROWS, tokens), BF16),
            pltpu.VMEM((slots, TABLE_REACH_ROWS, EMBED_WIDTH), F32),
            pltpu.SemaphoreType.DMA((slots,)),
        ],
        compiler_params=params(16),
        cost_estimate=pl.CostEstimate(
            flops=2 * slots * n_table * tokens * TABLE_REACH_ROWS * EMBED_WIDTH,
            bytes_accessed=4 * slots * TABLE_REACH_ROWS * EMBED_WIDTH,
            transcendentals=0,
        ),
    )(*parts)


def body(
    activations, cotangent, down_weight, up_weight, bias, bag_ids, bag_lengths, feature_table_slot
):
    tokens, width = activations.shape
    rank = down_weight.shape[0]
    n_table = lax.axis_size("table")
    n_rep = lax.axis_size("rep")
    slots = (SPARSE_FEATURES + n_table - 1) // n_table
    scale = 1.0 / math.sqrt(tokens * n_table * n_rep)
    table_index = lax.axis_index("table").astype(jnp.int32).reshape(1)
    rep_index = lax.axis_index("rep").astype(jnp.int32).reshape(1)
    far_bits = [1 << k for k in range(1, n_rep.bit_length() - 1)]
    up_bits, down_bits = [1] + far_bits, [1] + far_bits[::-1]
    ride = rank // n_rep >= BIAS_ROWS

    def swap(value, axis, bit):
        size = n_rep if axis == "rep" else n_table
        return lax.ppermute(value, axis, [(k, k ^ bit) for k in range(size)])

    def shifted(value, shift):
        return lax.ppermute(value, "table", [(k, (k + shift) % n_table) for k in range(n_table)])

    act_other = swap(activations, "rep", 1)
    cot_other = swap(cotangent, "rep", 1)
    act, cot, keep, send, dense_grad, *parts = input_call(
        table_index, rep_index, feature_table_slot, activations, cotangent, down_weight, up_weight,
        bias.reshape(-1, EMBED_WIDTH), jnp.transpose(bag_ids, (1, 2, 0)), jnp.transpose(bag_lengths, (1, 0)),
        n_table, slots, up_bits, down_bits,
    )
    other = swap(send, "rep", 1)
    parts = [parts[0]] + [shifted(parts[k], k) for k in range(1, n_table)]
    up_keep, up_send, down_keep, down_send, bias_sum = terms_call(
        keep, other, act, cot, act_other, cot_other, ride
    )
    def exchange(place, up_send, down_send, bias_sum):
        up_in = swap(up_send, "rep", up_bits[place])
        down_in = swap(down_send, "rep", down_bits[place])
        if not ride:
            bias_sum = bias_sum + swap(bias_sum, "rep", up_bits[place])
        return up_in, down_in, bias_sum

    def halved(up_keep, up_in, down_keep, down_in, bias_sum):
        if ride:
            return halve_call(up_keep, up_in, down_keep, down_in, bias_sum)
        half = up_keep.shape[0] // 2
        up = up_keep + up_in.astype(F32)
        down = down_keep + down_in.astype(F32)
        return up[:half], up[half:].astype(BF16), down[:half], down[half:].astype(BF16), bias_sum

    def chain(up_keep, up_send, down_keep, down_send, bias_sum):
        for place in range(2, len(up_bits)):
            up_in, down_in, bias_sum = exchange(place, up_send, down_send, bias_sum)
            if place < len(up_bits) - 1:
                up_keep, up_send, down_keep, down_send, bias_sum = halved(
                    up_keep, up_in, down_keep, down_in, bias_sum
                )
        if not ride:
            for bit in [1 << k for k in range(n_table.bit_length() - 1)]:
                bias_sum = bias_sum + swap(bias_sum, "table", bit)
        if not ride:
            return split_call(
                table_index, up_keep, up_in, down_keep, down_in, bias_sum, n_table, scale, ride
            )
        own, message, bias_sum = first_call(
            table_index, up_keep, up_in, down_keep, down_in, bias_sum, n_table, scale
        )
        for bit in [1 << k for k in range(n_table.bit_length() - 2)]:
            message = swap(message, "table", bit)
            own, message, bias_sum = next_call(own, message, bias_sum)
        return [own, bias_sum, message]

    up_in, down_in, bias_sum = exchange(1, up_send, down_send, bias_sum)
    terms = halved(up_keep, up_in, down_keep, down_in, bias_sum)
    shapes = jax.eval_shape(chain, *terms)
    own, bias_sum, *sends = lax.cond(
        feature_table_slot[0] >= 0,
        chain,
        lambda *_: jax.tree.map(lambda x: jnp.zeros(x.shape, x.dtype), shapes),
        *terms,
    )
    if ride:
        message = swap(sends[0], "table", n_table // 2)
        up_grad, down_grad, bias_grad = last_call(own, message, bias_sum, n_table, scale)
    else:
        arrived = [shifted(value, k + 1) for k, value in enumerate(sends)]
        up_grad, down_grad, bias_grad = finish_call(table_index, own, bias_sum, arrived, scale, ride)
    parts, _ = lax.optimization_barrier((parts, own))
    row_grad = rows_call(parts, slots)
    bias_grad = bias_grad.reshape(width)
    return (dense_grad, up_grad, down_grad, bias_grad, row_grad)


def solution(mesh):
    placed = (
        P(("table", "rep"), None),
        P(("table", "rep"), None),
        P(),
        P(),
        P(),
        P(("table", "rep"), None, None),
        P(("table", "rep"), None),
        P(),
    )
    return jax.shard_map(
        body,
        mesh=mesh,
        in_specs=placed,
        out_specs=(
            P(("table", "rep"), None),
            P("rep", "table"),
            P("rep", "table"),
            P(),
            P("rep", "table", None, None),
        ),
        check_vma=False,
    )
```

```python
import functools
import math

import jax
import jax.numpy as jnp
from jax import lax
from jax.experimental import pallas as pl
from jax.experimental.pallas import tpu as pltpu
from jax.sharding import PartitionSpec as P

EMBED_WIDTH = 128
SPARSE_FEATURES = 26
BAG = 4
TABLE_REACH_ROWS = 512
EMPTY = TABLE_REACH_ROWS // 2
BIAS_ROWS = 32
MESSAGE_ROWS = 16
F32 = jnp.float32
BF16 = jnp.bfloat16
MIB = 1024 * 1024
NT = (((1,), (1,)), ((), ()))
ANY = pl.BlockSpec(memory_space=pl.ANY)
VMEM = pl.BlockSpec(memory_space=pltpu.VMEM)
SMEM = pl.BlockSpec(memory_space=pltpu.SMEM)


def params(mib):
    return pltpu.CompilerParams(vmem_limit_bytes=mib * MIB)


def pieces_of(width):
    blocks = width // EMBED_WIDTH
    parts = max(p for p in (9, 3, 1) if blocks % p == 0)
    step = width // parts
    return [(k * step, step) for k in range(parts)]


def order_matrix(rep_index, size, block, bits):
    out_row = lax.broadcasted_iota(jnp.int32, (size, 1), 0)
    in_row = lax.broadcasted_iota(jnp.int32, (size, size), 1)
    source = out_row & (block - 1)
    for place, bit in enumerate(bits):
        unit = size >> (place + 1)
        flag = (out_row >> (unit.bit_length() - 1)) & 1
        own = (rep_index >> (bit.bit_length() - 1)) & 1
        source = source + (flag ^ own) * (bit * block)
    return (source == in_row).astype(F32).astype(BF16)


def input_kernel(
    n_table, slots, up_bits, down_bits, table_ref, rep_ref, owner_ref,
    act_hbm, cot_hbm, down_hbm, up_hbm, bias_ref, ids_ref, length_ref,
    act, cot, keep, send, dense_ref, *rest,
):
    outs = rest[:n_table]
    down, up, store, id_store, feature_ref, in_sems = rest[n_table:]
    tokens, width = act.shape
    rank = down.shape[0]
    half = rank // 2
    pieces = pieces_of(width)
    arrays = ((act_hbm, act), (down_hbm, down), (cot_hbm, cot), (up_hbm, up))
    fetched = []
    for place, (start, size) in enumerate(pieces):
        part = pl.ds(start, size)
        fetched.append(
            [
                pltpu.make_async_copy(source.at[:, part], target.at[:, part], in_sems.at[which, place])
                for which, (source, target) in enumerate(arrays)
            ]
        )
        for copy in fetched[-1]:
            copy.start()
    block = rank >> len(up_bits)
    up_order = order_matrix(rep_ref[0], rank, block, up_bits)
    down_order = order_matrix(rep_ref[0], rank, block, down_bits)
    for place in range(n_table * slots):
        feature_ref[place] = SPARSE_FEATURES
    for feature in range(SPARSE_FEATURES):
        feature_ref[owner_ref[feature]] = feature
    firsts = []
    for shift in range(n_table):
        owner = table_ref[0] + shift
        firsts.append(jnp.where(owner >= n_table, owner - n_table, owner) * slots)
    store[SPARSE_FEATURES + 1] = jnp.zeros(store.shape[1:], BF16)
    id_store[...] = jnp.full(id_store.shape, EMPTY, F32)
    entries = lax.broadcasted_iota(jnp.int32, (BAG, tokens), 0)
    for shift in range(n_table):
        for slot in range(slots):
            feature = feature_ref[firsts[shift] + slot]
            at = jnp.minimum(feature, SPARSE_FEATURES - 1)
            length = jnp.where(feature < SPARSE_FEATURES, length_ref[pl.ds(at, 1), :], 0)
            ids = jnp.where(entries < length, ids_ref[at] - EMPTY, EMPTY)
            id_store[shift, slot * BAG : (slot + 1) * BAG, :] = ids.astype(F32)
        outs[shift][slots * tokens :, :] = id_store[shift].astype(BF16)
    hidden = back = None
    for (start, size), copies in zip(pieces, fetched):
        part = slice(start, start + size)
        for copy in copies:
            copy.wait()
        value = act[:, part]
        term = lax.dot_general(value, down[:, part], NT, preferred_element_type=F32)
        hidden = term if hidden is None else hidden + term
        scaled_b = (cot[:, part].astype(F32) * value.astype(F32)).astype(BF16)
        term = lax.dot_general(scaled_b, up[:, part], NT, preferred_element_type=F32)
        back = term if back is None else back + term
    hidden, back = hidden.astype(BF16), back.astype(BF16)
    rows = lax.dot_general(up_order, hidden, NT, preferred_element_type=F32).astype(BF16)
    keep[0], send[0] = rows[:half], rows[half:]
    rows = lax.dot_general(down_order, back, NT, preferred_element_type=F32).astype(BF16)
    keep[1], send[1] = rows[:half], rows[half:]
    blocks = 3
    for first in range(0, width // EMBED_WIDTH, blocks):
        part = slice(first * EMBED_WIDTH, (first + blocks) * EMBED_WIDTH)
        mixed = jnp.dot(hidden, up[:, part], preferred_element_type=F32)
        tail = jnp.dot(back, down[:, part], preferred_element_type=F32)
        for k in range(blocks):
            place = first + k
            mine = slice(k * EMBED_WIDTH, (k + 1) * EMBED_WIDTH)
            cols = slice(place * EMBED_WIDTH, (place + 1) * EMBED_WIDTH)
            bias = bias_ref[place : place + 1, :]
            grad = cot[:, cols].astype(F32) * (1.0 + (mixed[:, mine] + bias)) + tail[:, mine]
            store[place] = grad.astype(BF16)
    dense_ref[...] = store[0]
    for shift in range(n_table):
        for slot in range(slots):
            rows = slice(slot * tokens, (slot + 1) * tokens)
            outs[shift][rows, :] = store[feature_ref[firsts[shift] + slot] + 1]


def input_call(
    table_index, rep_index, owners, act, cot, down, up, bias, ids, lengths, n_table, slots, up_bits, down_bits
):
    tokens, width = act.shape
    rank = down.shape[0]
    id_rows = -(-slots * BAG // 16) * 16
    sent = slots * tokens + id_rows
    return pl.pallas_call(
        functools.partial(input_kernel, n_table, slots, up_bits, down_bits),
        in_specs=[SMEM, SMEM, SMEM, ANY, ANY, ANY, ANY, VMEM, VMEM, VMEM],
        out_specs=[VMEM] * (5 + n_table),
        out_shape=[
            pltpu.VMEM((tokens, width), BF16),
            pltpu.VMEM((tokens, width), BF16),
            pltpu.VMEM((2, rank // 2, tokens), BF16),
            pltpu.VMEM((2, rank // 2, tokens), BF16),
            jax.ShapeDtypeStruct((tokens, EMBED_WIDTH), BF16),
        ]
        + [pltpu.VMEM((sent, EMBED_WIDTH), BF16)] * n_table,
        scratch_shapes=[
            pltpu.VMEM((rank, width), BF16),
            pltpu.VMEM((rank, width), BF16),
            pltpu.VMEM((SPARSE_FEATURES + 2, tokens, EMBED_WIDTH), BF16),
            pltpu.VMEM((n_table, id_rows, EMBED_WIDTH), F32),
            pltpu.SMEM((n_table * slots,), jnp.int32),
            pltpu.SemaphoreType.DMA((4, len(pieces_of(width)))),
        ],
        compiler_params=params(57),
        cost_estimate=pl.CostEstimate(
            flops=8 * tokens * rank * width, bytes_accessed=4 * (tokens + rank) * width, transcendentals=0
        ),
    )(table_index, rep_index, owners, act, cot, down, up, bias, ids, lengths)


def bias_terms(value):
    high = value.astype(BF16).astype(F32)
    return high, (value - high).astype(BF16).astype(F32)


def put_bias(ref, width, high, low):
    if ref.shape[0] >= 2 * BIAS_ROWS:
        both = jnp.concatenate([high, low], axis=0).astype(BF16)
        ref[: 2 * BIAS_ROWS, width : width + EMBED_WIDTH] = both
    else:
        ref[:BIAS_ROWS, width : width + EMBED_WIDTH] = high.astype(BF16)
        ref[:BIAS_ROWS, width + EMBED_WIDTH : width + 2 * EMBED_WIDTH] = low.astype(BF16)


def get_bias(ref, width):
    if ref.shape[0] >= 2 * BIAS_ROWS:
        both = ref[: 2 * BIAS_ROWS, width : width + EMBED_WIDTH].astype(F32)
        return both[:BIAS_ROWS] + both[BIAS_ROWS:]
    high = ref[:BIAS_ROWS, width : width + EMBED_WIDTH].astype(F32)
    return high + ref[:BIAS_ROWS, width + EMBED_WIDTH : width + 2 * EMBED_WIDTH].astype(F32)


def extra_columns(rows):
    return EMBED_WIDTH if rows >= 2 * BIAS_ROWS else 2 * EMBED_WIDTH


def terms_kernel(
    ride, keep_ref, other_ref, act, cot, act_other, cot_other,
    up_keep_ref, up_send_ref, down_keep_ref, down_send_ref, bias_ref,
):
    width = act.shape[1]
    hidden = jnp.concatenate([keep_ref[0], other_ref[0]], axis=1)
    back = jnp.concatenate([keep_ref[1], other_ref[1]], axis=1)
    blocks = 3
    keep = hidden.shape[0] // 2
    bias_ref[...] = jnp.zeros_like(bias_ref)
    for first in range(0, width // EMBED_WIDTH, blocks):
        part = slice(first * EMBED_WIDTH, (first + blocks) * EMBED_WIDTH)
        values = jnp.concatenate([act[:, part], act_other[:, part]], axis=0)
        grads = jnp.concatenate([cot[:, part], cot_other[:, part]], axis=0)
        scaled = grads.astype(F32) * values.astype(F32)
        sums = jnp.sum(scaled, axis=0, keepdims=True)
        for k in range(blocks):
            bias_ref[first + k : first + k + 1, :] = sums[:, k * EMBED_WIDTH : (k + 1) * EMBED_WIDTH]
        up_part = jnp.dot(hidden, scaled.astype(BF16), preferred_element_type=F32)
        up_keep_ref[:, part] = up_part[:keep]
        up_send_ref[:, part] = up_part[keep:].astype(BF16)
        down_part = jnp.dot(back, values, preferred_element_type=F32)
        down_keep_ref[:, part] = down_part[:keep]
        down_send_ref[:, part] = down_part[keep:].astype(BF16)
    if ride:
        high, low = bias_terms(bias_ref[...])
        put_bias(up_send_ref, width, high, low)
        bias_ref[...] = high + low


def terms_call(keep, other, act, cot, act_other, cot_other, ride):
    tokens, width = act.shape
    rows = keep.shape[1] // 2
    extra = extra_columns(rows) if ride else 0
    return pl.pallas_call(
        functools.partial(terms_kernel, ride),
        in_specs=[VMEM] * 6,
        out_specs=[VMEM] * 5,
        out_shape=[
            jax.ShapeDtypeStruct((rows, width), F32),
            jax.ShapeDtypeStruct((rows, width + extra), BF16),
            jax.ShapeDtypeStruct((rows, width), F32),
            jax.ShapeDtypeStruct((rows, width), BF16),
            jax.ShapeDtypeStruct((BIAS_ROWS, EMBED_WIDTH), F32),
        ],
        compiler_params=params(16),
        cost_estimate=pl.CostEstimate(
            flops=16 * tokens * rows * width, bytes_accessed=8 * tokens * width + 12 * rows * width, transcendentals=0
        ),
    )(keep, other, act, cot, act_other, cot_other)


def halve_kernel(
    up_keep_ref, up_in_ref, down_keep_ref, down_in_ref, bias_ref,
    up_out_ref, up_send_ref, down_out_ref, down_send_ref, bias_out_ref,
):
    rows, width = up_keep_ref.shape
    half = rows // 2
    up = up_keep_ref[...] + up_in_ref[:, :width].astype(F32)
    up_out_ref[...] = up[:half]
    up_send_ref[:, :width] = up[half:].astype(BF16)
    down = down_keep_ref[...] + down_in_ref[...].astype(F32)
    down_out_ref[...] = down[:half]
    down_send_ref[...] = down[half:].astype(BF16)
    high, low = bias_terms(bias_ref[...] + get_bias(up_in_ref, width))
    put_bias(up_send_ref, width, high, low)
    bias_out_ref[...] = high + low


def halve_call(up_keep, up_in, down_keep, down_in, bias_sum):
    rows, width = up_keep.shape
    half = rows // 2
    return pl.pallas_call(
        halve_kernel,
        in_specs=[VMEM] * 5,
        out_specs=[VMEM] * 5,
        out_shape=[
            jax.ShapeDtypeStruct((half, width), F32),
            jax.ShapeDtypeStruct((half, width + extra_columns(half)), BF16),
            jax.ShapeDtypeStruct((half, width), F32),
            jax.ShapeDtypeStruct((half, width), BF16),
            jax.ShapeDtypeStruct(bias_sum.shape, F32),
        ],
        compiler_params=params(16),
    )(up_keep, up_in, down_keep, down_in, bias_sum)


def split_kernel(
    ride, n_table, scale, table_ref, up_keep_ref, up_in_ref, down_keep_ref, down_in_ref, bias_ref,
    own_ref, bias_out_ref, *rest,
):
    sends, store = rest[: n_table - 1], rest[n_table - 1]
    columns = own_ref.shape[2]
    width = up_keep_ref.shape[1]
    pairs = ((up_keep_ref, up_in_ref), (down_keep_ref, down_in_ref))
    for which, (keep, arrived) in enumerate(pairs):
        total = (keep[...] + arrived[:, :width].astype(F32)) * scale
        for table in range(n_table):
            store[table, which] = total[:, table * columns : (table + 1) * columns]
    own_ref[...] = store[table_ref[0]]
    start = -(-columns // EMBED_WIDTH) * EMBED_WIDTH
    bias = bias_ref[...]
    if ride:
        high, low = bias_terms(bias + get_bias(up_in_ref, width))
        bias = high + low
    bias_out_ref[...] = bias
    for shift in range(1, n_table):
        value = store[lax.rem(table_ref[0] + shift, n_table)].astype(BF16)
        sends[shift - 1][:, :, :columns] = value
        if ride:
            sends[shift - 1][0, :BIAS_ROWS, start:] = high.astype(BF16)
            sends[shift - 1][1, :BIAS_ROWS, start:] = low.astype(BF16)


def split_call(table_index, up_keep, up_in, down_keep, down_in, bias_sum, n_table, scale, ride):
    rows, width = up_keep.shape
    columns = width // n_table
    sent = -(-columns // EMBED_WIDTH) * EMBED_WIDTH + EMBED_WIDTH if ride else columns
    return pl.pallas_call(
        functools.partial(split_kernel, ride, n_table, scale),
        in_specs=[SMEM] + [VMEM] * 5,
        out_specs=[VMEM] * (n_table + 1),
        out_shape=[
            jax.ShapeDtypeStruct((2, rows, columns), F32),
            jax.ShapeDtypeStruct(bias_sum.shape, F32),
        ]
        + [jax.ShapeDtypeStruct((2, rows, sent), BF16)] * (n_table - 1),
        scratch_shapes=[pltpu.VMEM((n_table, 2, rows, columns), F32)],
        compiler_params=params(16),
    )(table_index, up_keep, up_in, down_keep, down_in, bias_sum)


def finish_kernel(ride, n_table, scale, table_ref, own_ref, bias_ref, *rest):
    arrived = rest[: n_table - 1]
    up_ref, down_ref, bias_out_ref, store = rest[n_table - 1 :]
    columns = own_ref.shape[2]
    start = -(-columns // EMBED_WIDTH) * EMBED_WIDTH
    up, down = own_ref[0], own_ref[1]
    store[table_ref[0]] = bias_ref[...]
    for shift in range(1, n_table):
        value = arrived[shift - 1]
        up = up + value[0, :, :columns].astype(F32)
        down = down + value[1, :, :columns].astype(F32)
        if ride:
            source = lax.rem(table_ref[0] + n_table - shift, n_table)
            high = value[0, :BIAS_ROWS, start:].astype(F32)
            store[source] = high + value[1, :BIAS_ROWS, start:].astype(F32)
    up_ref[...] = up
    down_ref[...] = down
    total = bias_ref[...]
    if ride:
        total = store[0]
        for table in range(1, n_table):
            total = total + store[table]
    bias_out_ref[...] = total[: bias_out_ref.shape[0]] * scale


def finish_call(table_index, own, bias_sum, arrived, scale, ride):
    n_table = len(arrived) + 1
    _, rows, columns = own.shape
    return pl.pallas_call(
        functools.partial(finish_kernel, ride, n_table, scale),
        in_specs=[SMEM] + [VMEM] * (n_table + 1),
        out_specs=[VMEM] * 3,
        out_shape=[
            jax.ShapeDtypeStruct((rows, columns), F32),
            jax.ShapeDtypeStruct((rows, columns), F32),
            jax.ShapeDtypeStruct((columns * n_table // EMBED_WIDTH, EMBED_WIDTH), F32),
        ],
        scratch_shapes=[pltpu.VMEM((n_table,) + bias_sum.shape, F32)],
        compiler_params=params(16),
    )(table_index, own, bias_sum, *arrived)


def put_rows(ref, high, low):
    wide = ref.shape[1] // EMBED_WIDTH
    rows = []
    for value in (high, low):
        for row in range(4):
            places = [min(row * wide + k, BIAS_ROWS - 1) for k in range(wide)]
            rows.append(jnp.concatenate([value[place : place + 1, :] for place in places], axis=1))
    rows.append(jnp.zeros((MESSAGE_ROWS - 8, ref.shape[1]), F32))
    first = ref.shape[0] - MESSAGE_ROWS
    ref[first:, :] = jnp.concatenate(rows, axis=0).astype(BF16)


def get_rows(ref, store):
    wide = ref.shape[1] // EMBED_WIDTH
    value = ref[ref.shape[0] - MESSAGE_ROWS :, :].astype(F32)
    value = value[:4] + value[4:8]
    for place in range(min(4 * wide, BIAS_ROWS)):
        row, k = divmod(place, wide)
        store[place : place + 1, :] = value[row : row + 1, k * EMBED_WIDTH : (k + 1) * EMBED_WIDTH]
    return store[...]


def padded(columns):
    return -(-columns // EMBED_WIDTH) * EMBED_WIDTH


def first_kernel(
    n_table, scale, table_ref, up_keep_ref, up_in_ref, down_keep_ref, down_in_ref, bias_ref,
    keep_ref, send_ref, bias_out_ref, store,
):
    _, _, rows, columns = keep_ref.shape
    width = up_keep_ref.shape[1]
    pairs = ((up_keep_ref, up_in_ref), (down_keep_ref, down_in_ref))
    for which, (keep, arrived) in enumerate(pairs):
        total = (keep[...] + arrived[:, :width].astype(F32)) * scale
        for table in range(n_table):
            store[table, which] = total[:, table * columns : (table + 1) * columns]
    for place in range(n_table // 2):
        keep_ref[place] = store[table_ref[0] ^ (2 * place)]
        for which in range(2):
            first = (2 * place + which) * rows
            value = store[table_ref[0] ^ (2 * place + 1), which]
            send_ref[first : first + rows, :columns] = value.astype(BF16)
    high, low = bias_terms(bias_ref[...] + get_bias(up_in_ref, width))
    put_rows(send_ref, high, low)
    bias_out_ref[...] = high + low


def first_call(table_index, up_keep, up_in, down_keep, down_in, bias_sum, n_table, scale):
    rows, width = up_keep.shape
    columns = width // n_table
    return pl.pallas_call(
        functools.partial(first_kernel, n_table, scale),
        in_specs=[SMEM] + [VMEM] * 5,
        out_specs=[VMEM] * 3,
        out_shape=[
            jax.ShapeDtypeStruct((n_table // 2, 2, rows, columns), F32),
            jax.ShapeDtypeStruct((n_table * rows + MESSAGE_ROWS, padded(columns)), BF16),
            jax.ShapeDtypeStruct(bias_sum.shape, F32),
        ],
        scratch_shapes=[pltpu.VMEM((n_table, 2, rows, columns), F32)],
        compiler_params=params(16),
    )(table_index, up_keep, up_in, down_keep, down_in, bias_sum)


def next_kernel(keep_ref, in_ref, bias_ref, out_ref, send_ref, bias_out_ref, store):
    count, _, rows, columns = keep_ref.shape
    for place in range(count):
        for which in range(2):
            first = (2 * place + which) * rows
            total = keep_ref[place, which] + in_ref[first : first + rows, :columns].astype(F32)
            if place % 2 == 0:
                out_ref[place // 2, which] = total
            else:
                first = (place - 1 + which) * rows
                send_ref[first : first + rows, :columns] = total.astype(BF16)
    store[...] = jnp.zeros_like(store)
    high, low = bias_terms(bias_ref[...] + get_rows(in_ref, store))
    put_rows(send_ref, high, low)
    bias_out_ref[...] = high + low


def next_call(keep, arrived, bias_sum):
    count, _, rows, columns = keep.shape
    return pl.pallas_call(
        next_kernel,
        in_specs=[VMEM] * 3,
        out_specs=[VMEM] * 3,
        out_shape=[
            jax.ShapeDtypeStruct((count // 2, 2, rows, columns), F32),
            jax.ShapeDtypeStruct((count * rows + MESSAGE_ROWS, padded(columns)), BF16),
            jax.ShapeDtypeStruct(bias_sum.shape, F32),
        ],
        scratch_shapes=[pltpu.VMEM(bias_sum.shape, F32)],
        compiler_params=params(16),
    )(keep, arrived, bias_sum)


def last_kernel(scale, keep_ref, in_ref, bias_ref, up_ref, down_ref, bias_out_ref, store):
    rows, columns = up_ref.shape
    up_ref[...] = keep_ref[0, 0] + in_ref[:rows, :columns].astype(F32)
    down_ref[...] = keep_ref[0, 1] + in_ref[rows : 2 * rows, :columns].astype(F32)
    store[...] = jnp.zeros_like(store)
    total = bias_ref[...] + get_rows(in_ref, store)
    bias_out_ref[...] = total[: bias_out_ref.shape[0]] * scale


def last_call(keep, arrived, bias_sum, n_table, scale):
    _, _, rows, columns = keep.shape
    return pl.pallas_call(
        functools.partial(last_kernel, scale),
        in_specs=[VMEM] * 3,
        out_specs=[VMEM] * 3,
        out_shape=[
            jax.ShapeDtypeStruct((rows, columns), F32),
            jax.ShapeDtypeStruct((rows, columns), F32),
            jax.ShapeDtypeStruct((columns * n_table // EMBED_WIDTH, EMBED_WIDTH), F32),
        ],
        scratch_shapes=[pltpu.VMEM(bias_sum.shape, F32)],
        compiler_params=params(16),
    )(keep, arrived, bias_sum)


def rows_kernel(slots, *refs):
    *parts, out_hbm, id_store, row_store, out, sems = refs
    tokens = (parts[0].shape[0] - id_store.shape[1]) // slots
    numbers = lax.broadcasted_iota(jnp.int32, row_store.shape, 0) - EMPTY
    row_store[...] = numbers.astype(F32).astype(BF16)
    for source, part in enumerate(parts):
        id_store[source] = part[slots * tokens :, :].astype(F32)
    copies = []
    for slot in range(slots):
        rows = row_store[...].reshape(TABLE_REACH_ROWS // 16, 16, tokens)
        one, zero = jnp.ones(rows.shape, BF16), jnp.zeros(rows.shape, BF16)
        counts = []
        for source in range(len(parts)):
            count = None
            for entry in range(BAG):
                place = slot * BAG + entry
                ids = jnp.broadcast_to(id_store[source, place : place + 1, :], (16, tokens)).astype(BF16)
                found = jnp.where(rows == ids[None], one, zero)
                count = found if count is None else count + found
            counts.append(count.reshape(TABLE_REACH_ROWS, tokens))
        count = jnp.concatenate(counts, axis=1)
        grad = jnp.concatenate([part[slot * tokens : (slot + 1) * tokens, :] for part in parts], axis=0)
        out[slot] = jnp.dot(count, grad, preferred_element_type=F32)
        copies.append(pltpu.make_async_copy(out.at[slot], out_hbm.at[0, slot], sems.at[slot]))
        copies[-1].start()
    for copy in copies:
        copy.wait()


def rows_call(parts, slots):
    n_table = len(parts)
    id_rows = -(-slots * BAG // 16) * 16
    tokens = (parts[0].shape[0] - id_rows) // slots
    return pl.pallas_call(
        functools.partial(rows_kernel, slots),
        in_specs=[VMEM] * n_table,
        out_specs=ANY,
        out_shape=jax.ShapeDtypeStruct((1, slots, TABLE_REACH_ROWS, EMBED_WIDTH), F32),
        scratch_shapes=[
            pltpu.VMEM((n_table, id_rows, tokens), F32),
            pltpu.VMEM((TABLE_REACH_ROWS, tokens), BF16),
            pltpu.VMEM((slots, TABLE_REACH_ROWS, EMBED_WIDTH), F32),
            pltpu.SemaphoreType.DMA((slots,)),
        ],
        compiler_params=params(16),
        cost_estimate=pl.CostEstimate(
            flops=2 * slots * n_table * tokens * TABLE_REACH_ROWS * EMBED_WIDTH,
            bytes_accessed=4 * slots * TABLE_REACH_ROWS * EMBED_WIDTH,
            transcendentals=0,
        ),
    )(*parts)


def body(
    activations, cotangent, down_weight, up_weight, bias, bag_ids, bag_lengths, feature_table_slot
):
    tokens, width = activations.shape
    rank = down_weight.shape[0]
    n_table = lax.axis_size("table")
    n_rep = lax.axis_size("rep")
    slots = (SPARSE_FEATURES + n_table - 1) // n_table
    scale = 1.0 / math.sqrt(tokens * n_table * n_rep)
    table_index = lax.axis_index("table").astype(jnp.int32).reshape(1)
    rep_index = lax.axis_index("rep").astype(jnp.int32).reshape(1)
    far_bits = [1 << k for k in range(1, n_rep.bit_length() - 1)]
    up_bits, down_bits = [1] + far_bits, [1] + far_bits[::-1]
    ride = rank // n_rep >= BIAS_ROWS

    def swap(value, axis, bit):
        size = n_rep if axis == "rep" else n_table
        return lax.ppermute(value, axis, [(k, k ^ bit) for k in range(size)])

    def shifted(value, shift):
        return lax.ppermute(value, "table", [(k, (k + shift) % n_table) for k in range(n_table)])

    act_other = swap(activations, "rep", 1)
    cot_other = swap(cotangent, "rep", 1)
    act, cot, keep, send, dense_grad, *parts = input_call(
        table_index, rep_index, feature_table_slot, activations, cotangent, down_weight, up_weight,
        bias.reshape(-1, EMBED_WIDTH), jnp.transpose(bag_ids, (1, 2, 0)), jnp.transpose(bag_lengths, (1, 0)),
        n_table, slots, up_bits, down_bits,
    )
    other = swap(send, "rep", 1)
    parts = [parts[0]] + [shifted(parts[k], k) for k in range(1, n_table)]
    up_keep, up_send, down_keep, down_send, bias_sum = terms_call(
        keep, other, act, cot, act_other, cot_other, ride
    )
    def exchange(place, up_send, down_send, bias_sum):
        up_in = swap(up_send, "rep", up_bits[place])
        down_in = swap(down_send, "rep", down_bits[place])
        if not ride:
            bias_sum = bias_sum + swap(bias_sum, "rep", up_bits[place])
        return up_in, down_in, bias_sum

    def halved(up_keep, up_in, down_keep, down_in, bias_sum):
        if ride:
            return halve_call(up_keep, up_in, down_keep, down_in, bias_sum)
        half = up_keep.shape[0] // 2
        up = up_keep + up_in.astype(F32)
        down = down_keep + down_in.astype(F32)
        return up[:half], up[half:].astype(BF16), down[:half], down[half:].astype(BF16), bias_sum

    def chain(up_keep, up_send, down_keep, down_send, bias_sum):
        for place in range(2, len(up_bits)):
            up_in, down_in, bias_sum = exchange(place, up_send, down_send, bias_sum)
            if place < len(up_bits) - 1:
                up_keep, up_send, down_keep, down_send, bias_sum = halved(
                    up_keep, up_in, down_keep, down_in, bias_sum
                )
        if not ride:
            for bit in [1 << k for k in range(n_table.bit_length() - 1)]:
                bias_sum = bias_sum + swap(bias_sum, "table", bit)
        if not ride:
            return split_call(
                table_index, up_keep, up_in, down_keep, down_in, bias_sum, n_table, scale, ride
            )
        own, message, bias_sum = first_call(
            table_index, up_keep, up_in, down_keep, down_in, bias_sum, n_table, scale
        )
        for bit in [1 << k for k in range(n_table.bit_length() - 2)]:
            message = swap(message, "table", bit)
            own, message, bias_sum = next_call(own, message, bias_sum)
        return [own, bias_sum, message]

    up_in, down_in, bias_sum = exchange(1, up_send, down_send, bias_sum)
    terms = halved(up_keep, up_in, down_keep, down_in, bias_sum)
    shapes = jax.eval_shape(chain, *terms)
    own, bias_sum, *sends = lax.cond(
        feature_table_slot[0] >= 0,
        chain,
        lambda *_: jax.tree.map(lambda x: jnp.zeros(x.shape, x.dtype), shapes),
        *terms,
    )
    if ride:
        message = swap(sends[0], "table", n_table // 2)
        up_grad, down_grad, bias_grad = last_call(own, message, bias_sum, n_table, scale)
    else:
        arrived = [shifted(value, k + 1) for k, value in enumerate(sends)]
        up_grad, down_grad, bias_grad = finish_call(table_index, own, bias_sum, arrived, scale, ride)
    parts, _ = lax.optimization_barrier((parts, own))
    row_grad = rows_call(parts, slots)
    bias_grad = bias_grad.reshape(width)
    return (dense_grad, up_grad, down_grad, bias_grad, row_grad)


def solution(mesh):
    placed = (
        P(("table", "rep"), None),
        P(("table", "rep"), None),
        P(),
        P(),
        P(),
        P(("table", "rep"), None, None),
        P(("table", "rep"), None),
        P(),
    )
    return jax.shard_map(
        body,
        mesh=mesh,
        in_specs=placed,
        out_specs=(
            P(("table", "rep"), None),
            P("rep", "table"),
            P("rep", "table"),
            P(),
            P("rep", "table", None, None),
        ),
        check_vma=False,
    )
```

```python
import functools
import math

import jax
import jax.numpy as jnp
from jax import lax
from jax.experimental import pallas as pl
from jax.experimental.pallas import tpu as pltpu
from jax.sharding import PartitionSpec as P

EMBED_WIDTH = 128
SPARSE_FEATURES = 26
BAG = 4
TABLE_REACH_ROWS = 512
EMPTY = TABLE_REACH_ROWS // 2
BIAS_ROWS = 32
F32 = jnp.float32
BF16 = jnp.bfloat16
MIB = 1024 * 1024
NT = (((1,), (1,)), ((), ()))
ANY = pl.BlockSpec(memory_space=pl.ANY)
VMEM = pl.BlockSpec(memory_space=pltpu.VMEM)
SMEM = pl.BlockSpec(memory_space=pltpu.SMEM)


def params(mib):
    return pltpu.CompilerParams(vmem_limit_bytes=mib * MIB)


def pieces_of(width):
    blocks = width // EMBED_WIDTH
    parts = max(p for p in (9, 3, 1) if blocks % p == 0)
    step = width // parts
    return [(k * step, step) for k in range(parts)]


def order_matrix(rep_index, size, block, bits):
    out_row = lax.broadcasted_iota(jnp.int32, (size, 1), 0)
    in_row = lax.broadcasted_iota(jnp.int32, (size, size), 1)
    source = out_row & (block - 1)
    for place, bit in enumerate(bits):
        unit = size >> (place + 1)
        flag = (out_row >> (unit.bit_length() - 1)) & 1
        own = (rep_index >> (bit.bit_length() - 1)) & 1
        source = source + (flag ^ own) * (bit * block)
    return (source == in_row).astype(F32).astype(BF16)


def input_kernel(
    n_table, slots, up_bits, down_bits, table_ref, rep_ref, owner_ref,
    act_hbm, cot_hbm, down_hbm, up_hbm, bias_ref, ids_ref, length_ref,
    act, cot, keep, send, dense_ref, *rest,
):
    outs = rest[:n_table]
    down, up, store, id_store, feature_ref, in_sems = rest[n_table:]
    tokens, width = act.shape
    rank = down.shape[0]
    half = rank // 2
    pieces = pieces_of(width)
    arrays = ((act_hbm, act), (down_hbm, down), (cot_hbm, cot), (up_hbm, up))
    fetched = []
    for place, (start, size) in enumerate(pieces):
        part = pl.ds(start, size)
        fetched.append(
            [
                pltpu.make_async_copy(source.at[:, part], target.at[:, part], in_sems.at[which, place])
                for which, (source, target) in enumerate(arrays)
            ]
        )
        for copy in fetched[-1]:
            copy.start()
    block = rank >> len(up_bits)
    up_order = order_matrix(rep_ref[0], rank, block, up_bits)
    down_order = order_matrix(rep_ref[0], rank, block, down_bits)
    for place in range(n_table * slots):
        feature_ref[place] = SPARSE_FEATURES
    for feature in range(SPARSE_FEATURES):
        feature_ref[owner_ref[feature]] = feature
    firsts = []
    for shift in range(n_table):
        owner = table_ref[0] + shift
        firsts.append(jnp.where(owner >= n_table, owner - n_table, owner) * slots)
    store[SPARSE_FEATURES + 1] = jnp.zeros(store.shape[1:], BF16)
    id_store[...] = jnp.full(id_store.shape, EMPTY, F32)
    entries = lax.broadcasted_iota(jnp.int32, (BAG, tokens), 0)
    for shift in range(n_table):
        for slot in range(slots):
            feature = feature_ref[firsts[shift] + slot]
            at = jnp.minimum(feature, SPARSE_FEATURES - 1)
            length = jnp.where(feature < SPARSE_FEATURES, length_ref[pl.ds(at, 1), :], 0)
            ids = jnp.where(entries < length, ids_ref[at] - EMPTY, EMPTY)
            id_store[shift, slot * BAG : (slot + 1) * BAG, :] = ids.astype(F32)
        outs[shift][slots * tokens :, :] = id_store[shift].astype(BF16)
    hidden = back = None
    for (start, size), copies in zip(pieces, fetched):
        part = slice(start, start + size)
        for copy in copies:
            copy.wait()
        value = act[:, part]
        term = lax.dot_general(value, down[:, part], NT, preferred_element_type=F32)
        hidden = term if hidden is None else hidden + term
        scaled_b = (cot[:, part].astype(F32) * value.astype(F32)).astype(BF16)
        term = lax.dot_general(scaled_b, up[:, part], NT, preferred_element_type=F32)
        back = term if back is None else back + term
    hidden, back = hidden.astype(BF16), back.astype(BF16)
    rows = lax.dot_general(up_order, hidden, NT, preferred_element_type=F32).astype(BF16)
    keep[0], send[0] = rows[:half], rows[half:]
    rows = lax.dot_general(down_order, back, NT, preferred_element_type=F32).astype(BF16)
    keep[1], send[1] = rows[:half], rows[half:]
    blocks = 3
    for first in range(0, width // EMBED_WIDTH, blocks):
        part = slice(first * EMBED_WIDTH, (first + blocks) * EMBED_WIDTH)
        mixed = jnp.dot(hidden, up[:, part], preferred_element_type=F32)
        tail = jnp.dot(back, down[:, part], preferred_element_type=F32)
        for k in range(blocks):
            place = first + k
            mine = slice(k * EMBED_WIDTH, (k + 1) * EMBED_WIDTH)
            cols = slice(place * EMBED_WIDTH, (place + 1) * EMBED_WIDTH)
            bias = bias_ref[place : place + 1, :]
            grad = cot[:, cols].astype(F32) * (1.0 + (mixed[:, mine] + bias)) + tail[:, mine]
            store[place] = grad.astype(BF16)
    dense_ref[...] = store[0]
    for shift in range(n_table):
        for slot in range(slots):
            rows = slice(slot * tokens, (slot + 1) * tokens)
            outs[shift][rows, :] = store[feature_ref[firsts[shift] + slot] + 1]


def input_call(
    table_index, rep_index, owners, act, cot, down, up, bias, ids, lengths, n_table, slots, up_bits, down_bits
):
    tokens, width = act.shape
    rank = down.shape[0]
    id_rows = -(-slots * BAG // 16) * 16
    sent = slots * tokens + id_rows
    return pl.pallas_call(
        functools.partial(input_kernel, n_table, slots, up_bits, down_bits),
        in_specs=[SMEM, SMEM, SMEM, ANY, ANY, ANY, ANY, VMEM, VMEM, VMEM],
        out_specs=[VMEM] * (5 + n_table),
        out_shape=[
            pltpu.VMEM((tokens, width), BF16),
            pltpu.VMEM((tokens, width), BF16),
            pltpu.VMEM((2, rank // 2, tokens), BF16),
            pltpu.VMEM((2, rank // 2, tokens), BF16),
            jax.ShapeDtypeStruct((tokens, EMBED_WIDTH), BF16),
        ]
        + [pltpu.VMEM((sent, EMBED_WIDTH), BF16)] * n_table,
        scratch_shapes=[
            pltpu.VMEM((rank, width), BF16),
            pltpu.VMEM((rank, width), BF16),
            pltpu.VMEM((SPARSE_FEATURES + 2, tokens, EMBED_WIDTH), BF16),
            pltpu.VMEM((n_table, id_rows, EMBED_WIDTH), F32),
            pltpu.SMEM((n_table * slots,), jnp.int32),
            pltpu.SemaphoreType.DMA((4, len(pieces_of(width)))),
        ],
        compiler_params=params(57),
        cost_estimate=pl.CostEstimate(
            flops=8 * tokens * rank * width, bytes_accessed=4 * (tokens + rank) * width, transcendentals=0
        ),
    )(table_index, rep_index, owners, act, cot, down, up, bias, ids, lengths)


def bias_terms(value):
    high = value.astype(BF16).astype(F32)
    return high, (value - high).astype(BF16).astype(F32)


def put_bias(ref, width, high, low):
    if ref.shape[0] >= 2 * BIAS_ROWS:
        both = jnp.concatenate([high, low], axis=0).astype(BF16)
        ref[: 2 * BIAS_ROWS, width : width + EMBED_WIDTH] = both
    else:
        ref[:BIAS_ROWS, width : width + EMBED_WIDTH] = high.astype(BF16)
        ref[:BIAS_ROWS, width + EMBED_WIDTH : width + 2 * EMBED_WIDTH] = low.astype(BF16)


def get_bias(ref, width):
    if ref.shape[0] >= 2 * BIAS_ROWS:
        both = ref[: 2 * BIAS_ROWS, width : width + EMBED_WIDTH].astype(F32)
        return both[:BIAS_ROWS] + both[BIAS_ROWS:]
    high = ref[:BIAS_ROWS, width : width + EMBED_WIDTH].astype(F32)
    return high + ref[:BIAS_ROWS, width + EMBED_WIDTH : width + 2 * EMBED_WIDTH].astype(F32)


def extra_columns(rows):
    return EMBED_WIDTH if rows >= 2 * BIAS_ROWS else 2 * EMBED_WIDTH


def terms_kernel(
    ride, keep_ref, other_ref, act, cot, act_other, cot_other,
    up_keep_ref, up_send_ref, down_keep_ref, down_send_ref, bias_ref,
):
    width = act.shape[1]
    hidden = jnp.concatenate([keep_ref[0], other_ref[0]], axis=1)
    back = jnp.concatenate([keep_ref[1], other_ref[1]], axis=1)
    blocks = 3
    keep = hidden.shape[0] // 2
    bias_ref[...] = jnp.zeros_like(bias_ref)
    for first in range(0, width // EMBED_WIDTH, blocks):
        part = slice(first * EMBED_WIDTH, (first + blocks) * EMBED_WIDTH)
        values = jnp.concatenate([act[:, part], act_other[:, part]], axis=0)
        grads = jnp.concatenate([cot[:, part], cot_other[:, part]], axis=0)
        scaled = grads.astype(F32) * values.astype(F32)
        sums = jnp.sum(scaled, axis=0, keepdims=True)
        for k in range(blocks):
            bias_ref[first + k : first + k + 1, :] = sums[:, k * EMBED_WIDTH : (k + 1) * EMBED_WIDTH]
        up_part = jnp.dot(hidden, scaled.astype(BF16), preferred_element_type=F32)
        up_keep_ref[:, part] = up_part[:keep]
        up_send_ref[:, part] = up_part[keep:].astype(BF16)
        down_part = jnp.dot(back, values, preferred_element_type=F32)
        down_keep_ref[:, part] = down_part[:keep]
        down_send_ref[:, part] = down_part[keep:].astype(BF16)
    if ride:
        high, low = bias_terms(bias_ref[...])
        put_bias(up_send_ref, width, high, low)
        bias_ref[...] = high + low


def terms_call(keep, other, act, cot, act_other, cot_other, ride):
    tokens, width = act.shape
    rows = keep.shape[1] // 2
    extra = extra_columns(rows) if ride else 0
    return pl.pallas_call(
        functools.partial(terms_kernel, ride),
        in_specs=[VMEM] * 6,
        out_specs=[VMEM] * 5,
        out_shape=[
            jax.ShapeDtypeStruct((rows, width), F32),
            jax.ShapeDtypeStruct((rows, width + extra), BF16),
            jax.ShapeDtypeStruct((rows, width), F32),
            jax.ShapeDtypeStruct((rows, width), BF16),
            jax.ShapeDtypeStruct((BIAS_ROWS, EMBED_WIDTH), F32),
        ],
        compiler_params=params(16),
        cost_estimate=pl.CostEstimate(
            flops=16 * tokens * rows * width, bytes_accessed=8 * tokens * width + 12 * rows * width, transcendentals=0
        ),
    )(keep, other, act, cot, act_other, cot_other)


def halve_kernel(
    up_keep_ref, up_in_ref, down_keep_ref, down_in_ref, bias_ref,
    up_out_ref, up_send_ref, down_out_ref, down_send_ref, bias_out_ref,
):
    rows, width = up_keep_ref.shape
    half = rows // 2
    up = up_keep_ref[...] + up_in_ref[:, :width].astype(F32)
    up_out_ref[...] = up[:half]
    up_send_ref[:, :width] = up[half:].astype(BF16)
    down = down_keep_ref[...] + down_in_ref[...].astype(F32)
    down_out_ref[...] = down[:half]
    down_send_ref[...] = down[half:].astype(BF16)
    high, low = bias_terms(bias_ref[...] + get_bias(up_in_ref, width))
    put_bias(up_send_ref, width, high, low)
    bias_out_ref[...] = high + low


def halve_call(up_keep, up_in, down_keep, down_in, bias_sum):
    rows, width = up_keep.shape
    half = rows // 2
    return pl.pallas_call(
        halve_kernel,
        in_specs=[VMEM] * 5,
        out_specs=[VMEM] * 5,
        out_shape=[
            jax.ShapeDtypeStruct((half, width), F32),
            jax.ShapeDtypeStruct((half, width + extra_columns(half)), BF16),
            jax.ShapeDtypeStruct((half, width), F32),
            jax.ShapeDtypeStruct((half, width), BF16),
            jax.ShapeDtypeStruct(bias_sum.shape, F32),
        ],
        compiler_params=params(16),
    )(up_keep, up_in, down_keep, down_in, bias_sum)


def split_kernel(
    ride, n_table, scale, table_ref, up_keep_ref, up_in_ref, down_keep_ref, down_in_ref, bias_ref,
    own_ref, bias_out_ref, *rest,
):
    sends, store = rest[: n_table - 1], rest[n_table - 1]
    columns = own_ref.shape[2]
    width = up_keep_ref.shape[1]
    pairs = ((up_keep_ref, up_in_ref), (down_keep_ref, down_in_ref))
    for which, (keep, arrived) in enumerate(pairs):
        total = (keep[...] + arrived[:, :width].astype(F32)) * scale
        for table in range(n_table):
            store[table, which] = total[:, table * columns : (table + 1) * columns]
    own_ref[...] = store[table_ref[0]]
    start = -(-columns // EMBED_WIDTH) * EMBED_WIDTH
    bias = bias_ref[...]
    if ride:
        high, low = bias_terms(bias + get_bias(up_in_ref, width))
        bias = high + low
    bias_out_ref[...] = bias
    for shift in range(1, n_table):
        value = store[lax.rem(table_ref[0] + shift, n_table)].astype(BF16)
        sends[shift - 1][:, :, :columns] = value
        if ride:
            sends[shift - 1][0, :BIAS_ROWS, start:] = high.astype(BF16)
            sends[shift - 1][1, :BIAS_ROWS, start:] = low.astype(BF16)


def split_call(table_index, up_keep, up_in, down_keep, down_in, bias_sum, n_table, scale, ride):
    rows, width = up_keep.shape
    columns = width // n_table
    sent = -(-columns // EMBED_WIDTH) * EMBED_WIDTH + EMBED_WIDTH if ride else columns
    return pl.pallas_call(
        functools.partial(split_kernel, ride, n_table, scale),
        in_specs=[SMEM] + [VMEM] * 5,
        out_specs=[VMEM] * (n_table + 1),
        out_shape=[
            jax.ShapeDtypeStruct((2, rows, columns), F32),
            jax.ShapeDtypeStruct(bias_sum.shape, F32),
        ]
        + [jax.ShapeDtypeStruct((2, rows, sent), BF16)] * (n_table - 1),
        scratch_shapes=[pltpu.VMEM((n_table, 2, rows, columns), F32)],
        compiler_params=params(16),
    )(table_index, up_keep, up_in, down_keep, down_in, bias_sum)


def finish_kernel(ride, n_table, scale, table_ref, own_ref, bias_ref, *rest):
    arrived = rest[: n_table - 1]
    up_ref, down_ref, bias_out_ref, store = rest[n_table - 1 :]
    columns = own_ref.shape[2]
    start = -(-columns // EMBED_WIDTH) * EMBED_WIDTH
    up, down = own_ref[0], own_ref[1]
    store[table_ref[0]] = bias_ref[...]
    for shift in range(1, n_table):
        value = arrived[shift - 1]
        up = up + value[0, :, :columns].astype(F32)
        down = down + value[1, :, :columns].astype(F32)
        if ride:
            source = lax.rem(table_ref[0] + n_table - shift, n_table)
            high = value[0, :BIAS_ROWS, start:].astype(F32)
            store[source] = high + value[1, :BIAS_ROWS, start:].astype(F32)
    up_ref[...] = up
    down_ref[...] = down
    total = bias_ref[...]
    if ride:
        total = store[0]
        for table in range(1, n_table):
            total = total + store[table]
    bias_out_ref[...] = total[: bias_out_ref.shape[0]] * scale


def finish_call(table_index, own, bias_sum, arrived, scale, ride):
    n_table = len(arrived) + 1
    _, rows, columns = own.shape
    return pl.pallas_call(
        functools.partial(finish_kernel, ride, n_table, scale),
        in_specs=[SMEM] + [VMEM] * (n_table + 1),
        out_specs=[VMEM] * 3,
        out_shape=[
            jax.ShapeDtypeStruct((rows, columns), F32),
            jax.ShapeDtypeStruct((rows, columns), F32),
            jax.ShapeDtypeStruct((columns * n_table // EMBED_WIDTH, EMBED_WIDTH), F32),
        ],
        scratch_shapes=[pltpu.VMEM((n_table,) + bias_sum.shape, F32)],
        compiler_params=params(16),
    )(table_index, own, bias_sum, *arrived)


def padded(columns):
    return -(-columns // EMBED_WIDTH) * EMBED_WIDTH


def first_kernel(
    n_table, scale, table_ref, up_keep_ref, up_in_ref, down_keep_ref, down_in_ref, bias_ref,
    keep_ref, send_ref, bias_out_ref, store,
):
    _, _, rows, columns = keep_ref.shape
    width = up_keep_ref.shape[1]
    pairs = ((up_keep_ref, up_in_ref), (down_keep_ref, down_in_ref))
    for which, (keep, arrived) in enumerate(pairs):
        total = (keep[...] + arrived[:, :width].astype(F32)) * scale
        for table in range(n_table):
            store[table, which] = total[:, table * columns : (table + 1) * columns]
    for place in range(n_table // 2):
        keep_ref[place] = store[table_ref[0] ^ (2 * place)]
        for which in range(2):
            first = place * padded(columns)
            value = store[table_ref[0] ^ (2 * place + 1), which]
            send_ref[which * rows : (which + 1) * rows, first : first + columns] = value.astype(BF16)
    high, low = bias_terms(bias_ref[...] + get_bias(up_in_ref, width))
    put_bias(send_ref, n_table // 2 * padded(columns), high, low)
    bias_out_ref[...] = high + low


def message_shape(tables, rows, columns):
    return (2 * rows, tables * padded(columns) + extra_columns(2 * rows))


def first_call(table_index, up_keep, up_in, down_keep, down_in, bias_sum, n_table, scale):
    rows, width = up_keep.shape
    columns = width // n_table
    return pl.pallas_call(
        functools.partial(first_kernel, n_table, scale),
        in_specs=[SMEM] + [VMEM] * 5,
        out_specs=[VMEM] * 3,
        out_shape=[
            jax.ShapeDtypeStruct((n_table // 2, 2, rows, columns), F32),
            jax.ShapeDtypeStruct(message_shape(n_table // 2, rows, columns), BF16),
            jax.ShapeDtypeStruct(bias_sum.shape, F32),
        ],
        scratch_shapes=[pltpu.VMEM((n_table, 2, rows, columns), F32)],
        compiler_params=params(16),
    )(table_index, up_keep, up_in, down_keep, down_in, bias_sum)


def next_kernel(keep_ref, in_ref, bias_ref, out_ref, send_ref, bias_out_ref):
    count, _, rows, columns = keep_ref.shape
    for place in range(count):
        for which in range(2):
            part = slice(which * rows, (which + 1) * rows)
            first = place * padded(columns)
            total = keep_ref[place, which] + in_ref[part, first : first + columns].astype(F32)
            if place % 2 == 0:
                out_ref[place // 2, which] = total
            else:
                first = place // 2 * padded(columns)
                send_ref[part, first : first + columns] = total.astype(BF16)
    high, low = bias_terms(bias_ref[...] + get_bias(in_ref, count * padded(columns)))
    put_bias(send_ref, count // 2 * padded(columns), high, low)
    bias_out_ref[...] = high + low


def next_call(keep, arrived, bias_sum):
    count, _, rows, columns = keep.shape
    return pl.pallas_call(
        next_kernel,
        in_specs=[VMEM] * 3,
        out_specs=[VMEM] * 3,
        out_shape=[
            jax.ShapeDtypeStruct((count // 2, 2, rows, columns), F32),
            jax.ShapeDtypeStruct(message_shape(count // 2, rows, columns), BF16),
            jax.ShapeDtypeStruct(bias_sum.shape, F32),
        ],
        compiler_params=params(16),
    )(keep, arrived, bias_sum)


def last_kernel(scale, keep_ref, in_ref, bias_ref, up_ref, down_ref, bias_out_ref):
    rows, columns = up_ref.shape
    up_ref[...] = keep_ref[0, 0] + in_ref[:rows, :columns].astype(F32)
    down_ref[...] = keep_ref[0, 1] + in_ref[rows : 2 * rows, :columns].astype(F32)
    total = bias_ref[...] + get_bias(in_ref, padded(columns))
    bias_out_ref[...] = total[: bias_out_ref.shape[0]] * scale


def last_call(keep, arrived, bias_sum, n_table, scale):
    _, _, rows, columns = keep.shape
    return pl.pallas_call(
        functools.partial(last_kernel, scale),
        in_specs=[VMEM] * 3,
        out_specs=[VMEM] * 3,
        out_shape=[
            jax.ShapeDtypeStruct((rows, columns), F32),
            jax.ShapeDtypeStruct((rows, columns), F32),
            jax.ShapeDtypeStruct((columns * n_table // EMBED_WIDTH, EMBED_WIDTH), F32),
        ],
        compiler_params=params(16),
    )(keep, arrived, bias_sum)


def rows_kernel(slots, *refs):
    *parts, out_hbm, id_store, row_store, out, sems = refs
    tokens = (parts[0].shape[0] - id_store.shape[1]) // slots
    numbers = lax.broadcasted_iota(jnp.int32, row_store.shape, 0) - EMPTY
    row_store[...] = numbers.astype(F32).astype(BF16)
    for source, part in enumerate(parts):
        id_store[source] = part[slots * tokens :, :].astype(F32)
    copies = []
    for slot in range(slots):
        rows = row_store[...].reshape(TABLE_REACH_ROWS // 16, 16, tokens)
        one, zero = jnp.ones(rows.shape, BF16), jnp.zeros(rows.shape, BF16)
        counts = []
        for source in range(len(parts)):
            count = None
            for entry in range(BAG):
                place = slot * BAG + entry
                ids = jnp.broadcast_to(id_store[source, place : place + 1, :], (16, tokens)).astype(BF16)
                found = jnp.where(rows == ids[None], one, zero)
                count = found if count is None else count + found
            counts.append(count.reshape(TABLE_REACH_ROWS, tokens))
        count = jnp.concatenate(counts, axis=1)
        grad = jnp.concatenate([part[slot * tokens : (slot + 1) * tokens, :] for part in parts], axis=0)
        out[slot] = jnp.dot(count, grad, preferred_element_type=F32)
        copies.append(pltpu.make_async_copy(out.at[slot], out_hbm.at[0, slot], sems.at[slot]))
        copies[-1].start()
    for copy in copies:
        copy.wait()


def rows_call(parts, slots):
    n_table = len(parts)
    id_rows = -(-slots * BAG // 16) * 16
    tokens = (parts[0].shape[0] - id_rows) // slots
    return pl.pallas_call(
        functools.partial(rows_kernel, slots),
        in_specs=[VMEM] * n_table,
        out_specs=ANY,
        out_shape=jax.ShapeDtypeStruct((1, slots, TABLE_REACH_ROWS, EMBED_WIDTH), F32),
        scratch_shapes=[
            pltpu.VMEM((n_table, id_rows, tokens), F32),
            pltpu.VMEM((TABLE_REACH_ROWS, tokens), BF16),
            pltpu.VMEM((slots, TABLE_REACH_ROWS, EMBED_WIDTH), F32),
            pltpu.SemaphoreType.DMA((slots,)),
        ],
        compiler_params=params(16),
        cost_estimate=pl.CostEstimate(
            flops=2 * slots * n_table * tokens * TABLE_REACH_ROWS * EMBED_WIDTH,
            bytes_accessed=4 * slots * TABLE_REACH_ROWS * EMBED_WIDTH,
            transcendentals=0,
        ),
    )(*parts)


def body(
    activations, cotangent, down_weight, up_weight, bias, bag_ids, bag_lengths, feature_table_slot
):
    tokens, width = activations.shape
    rank = down_weight.shape[0]
    n_table = lax.axis_size("table")
    n_rep = lax.axis_size("rep")
    slots = (SPARSE_FEATURES + n_table - 1) // n_table
    scale = 1.0 / math.sqrt(tokens * n_table * n_rep)
    table_index = lax.axis_index("table").astype(jnp.int32).reshape(1)
    rep_index = lax.axis_index("rep").astype(jnp.int32).reshape(1)
    far_bits = [1 << k for k in range(1, n_rep.bit_length() - 1)]
    up_bits, down_bits = [1] + far_bits, [1] + far_bits[::-1]
    ride = rank // n_rep >= BIAS_ROWS

    def swap(value, axis, bit):
        size = n_rep if axis == "rep" else n_table
        return lax.ppermute(value, axis, [(k, k ^ bit) for k in range(size)])

    def shifted(value, shift):
        return lax.ppermute(value, "table", [(k, (k + shift) % n_table) for k in range(n_table)])

    act_other = swap(activations, "rep", 1)
    cot_other = swap(cotangent, "rep", 1)
    act, cot, keep, send, dense_grad, *parts = input_call(
        table_index, rep_index, feature_table_slot, activations, cotangent, down_weight, up_weight,
        bias.reshape(-1, EMBED_WIDTH), jnp.transpose(bag_ids, (1, 2, 0)), jnp.transpose(bag_lengths, (1, 0)),
        n_table, slots, up_bits, down_bits,
    )
    other = swap(send, "rep", 1)
    parts = [parts[0]] + [shifted(parts[k], k) for k in range(1, n_table)]
    up_keep, up_send, down_keep, down_send, bias_sum = terms_call(
        keep, other, act, cot, act_other, cot_other, ride
    )
    def exchange(place, up_send, down_send, bias_sum):
        up_in = swap(up_send, "rep", up_bits[place])
        down_in = swap(down_send, "rep", down_bits[place])
        if not ride:
            bias_sum = bias_sum + swap(bias_sum, "rep", up_bits[place])
        return up_in, down_in, bias_sum

    def halved(up_keep, up_in, down_keep, down_in, bias_sum):
        if ride:
            return halve_call(up_keep, up_in, down_keep, down_in, bias_sum)
        half = up_keep.shape[0] // 2
        up = up_keep + up_in.astype(F32)
        down = down_keep + down_in.astype(F32)
        return up[:half], up[half:].astype(BF16), down[:half], down[half:].astype(BF16), bias_sum

    def chain(up_keep, up_send, down_keep, down_send, bias_sum):
        for place in range(2, len(up_bits)):
            up_in, down_in, bias_sum = exchange(place, up_send, down_send, bias_sum)
            if place < len(up_bits) - 1:
                up_keep, up_send, down_keep, down_send, bias_sum = halved(
                    up_keep, up_in, down_keep, down_in, bias_sum
                )
        if not ride:
            for bit in [1 << k for k in range(n_table.bit_length() - 1)]:
                bias_sum = bias_sum + swap(bias_sum, "table", bit)
        if not ride:
            return split_call(
                table_index, up_keep, up_in, down_keep, down_in, bias_sum, n_table, scale, ride
            )
        own, message, bias_sum = first_call(
            table_index, up_keep, up_in, down_keep, down_in, bias_sum, n_table, scale
        )
        for bit in [1 << k for k in range(n_table.bit_length() - 2)]:
            message = swap(message, "table", bit)
            own, message, bias_sum = next_call(own, message, bias_sum)
        return [own, bias_sum, message]

    up_in, down_in, bias_sum = exchange(1, up_send, down_send, bias_sum)
    terms = halved(up_keep, up_in, down_keep, down_in, bias_sum)
    shapes = jax.eval_shape(chain, *terms)
    own, bias_sum, *sends = lax.cond(
        feature_table_slot[0] >= 0,
        chain,
        lambda *_: jax.tree.map(lambda x: jnp.zeros(x.shape, x.dtype), shapes),
        *terms,
    )
    if ride:
        message = swap(sends[0], "table", n_table // 2)
        up_grad, down_grad, bias_grad = last_call(own, message, bias_sum, n_table, scale)
    else:
        arrived = [shifted(value, k + 1) for k, value in enumerate(sends)]
        up_grad, down_grad, bias_grad = finish_call(table_index, own, bias_sum, arrived, scale, ride)
    parts, _ = lax.optimization_barrier((parts, own))
    row_grad = rows_call(parts, slots)
    bias_grad = bias_grad.reshape(width)
    return (dense_grad, up_grad, down_grad, bias_grad, row_grad)


def solution(mesh):
    placed = (
        P(("table", "rep"), None),
        P(("table", "rep"), None),
        P(),
        P(),
        P(),
        P(("table", "rep"), None, None),
        P(("table", "rep"), None),
        P(),
    )
    return jax.shard_map(
        body,
        mesh=mesh,
        in_specs=placed,
        out_specs=(
            P(("table", "rep"), None),
            P("rep", "table"),
            P("rep", "table"),
            P(),
            P("rep", "table", None, None),
        ),
        check_vma=False,
    )
```

```python
import functools
import math

import jax
import jax.numpy as jnp
from jax import lax
from jax.experimental import pallas as pl
from jax.experimental.pallas import tpu as pltpu
from jax.sharding import PartitionSpec as P

EMBED_WIDTH = 128
SPARSE_FEATURES = 26
BAG = 4
TABLE_REACH_ROWS = 512
EMPTY = TABLE_REACH_ROWS // 2
BIAS_ROWS = 32
F32 = jnp.float32
BF16 = jnp.bfloat16
MIB = 1024 * 1024
NT = (((1,), (1,)), ((), ()))
ANY = pl.BlockSpec(memory_space=pl.ANY)
VMEM = pl.BlockSpec(memory_space=pltpu.VMEM)
SMEM = pl.BlockSpec(memory_space=pltpu.SMEM)


def params(mib):
    return pltpu.CompilerParams(vmem_limit_bytes=mib * MIB)


def pieces_of(width):
    blocks = width // EMBED_WIDTH
    parts = max(p for p in (9, 3, 1) if blocks % p == 0)
    step = width // parts
    return [(k * step, step) for k in range(parts)]


def order_matrix(rep_index, size, block, bits):
    out_row = lax.broadcasted_iota(jnp.int32, (size, 1), 0)
    in_row = lax.broadcasted_iota(jnp.int32, (size, size), 1)
    source = out_row & (block - 1)
    for place, bit in enumerate(bits):
        unit = size >> (place + 1)
        flag = (out_row >> (unit.bit_length() - 1)) & 1
        own = (rep_index >> (bit.bit_length() - 1)) & 1
        source = source + (flag ^ own) * (bit * block)
    return (source == in_row).astype(F32).astype(BF16)


def input_kernel(
    n_table, slots, up_bits, down_bits, table_ref, rep_ref, owner_ref,
    act_hbm, cot_hbm, down_hbm, up_hbm, bias_hbm, ids_hbm, length_hbm,
    act, cot, keep, send, dense_ref, *rest,
):
    outs = rest[:n_table]
    down, up, bias_ref, ids_ref, length_ref, store, id_store, feature_ref, in_sems, small_sems = rest[n_table:]
    tokens, width = act.shape
    rank = down.shape[0]
    half = rank // 2
    pieces = pieces_of(width)
    arrays = ((act_hbm, act), (down_hbm, down), (cot_hbm, cot), (up_hbm, up))
    fetched = []
    for place, (start, size) in enumerate(pieces):
        part = pl.ds(start, size)
        fetched.append(
            [
                pltpu.make_async_copy(source.at[:, part], target.at[:, part], in_sems.at[which, place])
                for which, (source, target) in enumerate(arrays)
            ]
        )
        for copy in fetched[-1]:
            copy.start()
    small = [
        pltpu.make_async_copy(source, target, small_sems.at[which])
        for which, (source, target) in enumerate(
            ((bias_hbm, bias_ref), (ids_hbm, ids_ref), (length_hbm, length_ref))
        )
    ]
    for copy in small:
        copy.start()
    block = rank >> len(up_bits)
    up_order = order_matrix(rep_ref[0], rank, block, up_bits)
    down_order = order_matrix(rep_ref[0], rank, block, down_bits)
    hidden = back = None
    for (start, size), copies in zip(pieces, fetched):
        part = slice(start, start + size)
        for copy in copies:
            copy.wait()
        value = act[:, part]
        term = lax.dot_general(value, down[:, part], NT, preferred_element_type=F32)
        hidden = term if hidden is None else hidden + term
        scaled_b = (cot[:, part].astype(F32) * value.astype(F32)).astype(BF16)
        term = lax.dot_general(scaled_b, up[:, part], NT, preferred_element_type=F32)
        back = term if back is None else back + term
    for copy in small:
        copy.wait()
    for place in range(n_table * slots):
        feature_ref[place] = SPARSE_FEATURES
    for feature in range(SPARSE_FEATURES):
        feature_ref[owner_ref[feature]] = feature
    firsts = []
    for shift in range(n_table):
        owner = table_ref[0] + shift
        firsts.append(jnp.where(owner >= n_table, owner - n_table, owner) * slots)
    store[SPARSE_FEATURES + 1] = jnp.zeros(store.shape[1:], BF16)
    id_store[...] = jnp.full(id_store.shape, EMPTY, F32)
    entries = lax.broadcasted_iota(jnp.int32, (BAG, tokens), 0)
    for shift in range(n_table):
        for slot in range(slots):
            feature = feature_ref[firsts[shift] + slot]
            at = jnp.minimum(feature, SPARSE_FEATURES - 1)
            length = jnp.where(feature < SPARSE_FEATURES, length_ref[pl.ds(at, 1), :], 0)
            ids = jnp.where(entries < length, ids_ref[at] - EMPTY, EMPTY)
            id_store[shift, slot * BAG : (slot + 1) * BAG, :] = ids.astype(F32)
        outs[shift][slots * tokens :, :] = id_store[shift].astype(BF16)
    hidden, back = hidden.astype(BF16), back.astype(BF16)
    rows = lax.dot_general(up_order, hidden, NT, preferred_element_type=F32).astype(BF16)
    keep[0], send[0] = rows[:half], rows[half:]
    rows = lax.dot_general(down_order, back, NT, preferred_element_type=F32).astype(BF16)
    keep[1], send[1] = rows[:half], rows[half:]
    blocks = 3
    for first in range(0, width // EMBED_WIDTH, blocks):
        part = slice(first * EMBED_WIDTH, (first + blocks) * EMBED_WIDTH)
        mixed = jnp.dot(hidden, up[:, part], preferred_element_type=F32)
        tail = jnp.dot(back, down[:, part], preferred_element_type=F32)
        for k in range(blocks):
            place = first + k
            mine = slice(k * EMBED_WIDTH, (k + 1) * EMBED_WIDTH)
            cols = slice(place * EMBED_WIDTH, (place + 1) * EMBED_WIDTH)
            bias = bias_ref[place : place + 1, :]
            grad = cot[:, cols].astype(F32) * (1.0 + (mixed[:, mine] + bias)) + tail[:, mine]
            store[place] = grad.astype(BF16)
    dense_ref[...] = store[0]
    for shift in range(n_table):
        for slot in range(slots):
            rows = slice(slot * tokens, (slot + 1) * tokens)
            outs[shift][rows, :] = store[feature_ref[firsts[shift] + slot] + 1]


def input_call(
    table_index, rep_index, owners, act, cot, down, up, bias, ids, lengths, n_table, slots, up_bits, down_bits
):
    tokens, width = act.shape
    rank = down.shape[0]
    id_rows = -(-slots * BAG // 16) * 16
    sent = slots * tokens + id_rows
    return pl.pallas_call(
        functools.partial(input_kernel, n_table, slots, up_bits, down_bits),
        in_specs=[SMEM, SMEM, SMEM, ANY, ANY, ANY, ANY, ANY, ANY, ANY],
        out_specs=[VMEM] * (5 + n_table),
        out_shape=[
            pltpu.VMEM((tokens, width), BF16),
            pltpu.VMEM((tokens, width), BF16),
            pltpu.VMEM((2, rank // 2, tokens), BF16),
            pltpu.VMEM((2, rank // 2, tokens), BF16),
            jax.ShapeDtypeStruct((tokens, EMBED_WIDTH), BF16),
        ]
        + [pltpu.VMEM((sent, EMBED_WIDTH), BF16)] * n_table,
        scratch_shapes=[
            pltpu.VMEM((rank, width), BF16),
            pltpu.VMEM((rank, width), BF16),
            pltpu.VMEM(bias.shape, F32),
            pltpu.VMEM(ids.shape, jnp.int32),
            pltpu.VMEM(lengths.shape, jnp.int32),
            pltpu.VMEM((SPARSE_FEATURES + 2, tokens, EMBED_WIDTH), BF16),
            pltpu.VMEM((n_table, id_rows, EMBED_WIDTH), F32),
            pltpu.SMEM((n_table * slots,), jnp.int32),
            pltpu.SemaphoreType.DMA((4, len(pieces_of(width)))),
            pltpu.SemaphoreType.DMA((3,)),
        ],
        compiler_params=params(57),
        cost_estimate=pl.CostEstimate(
            flops=8 * tokens * rank * width, bytes_accessed=4 * (tokens + rank) * width, transcendentals=0
        ),
    )(table_index, rep_index, owners, act, cot, down, up, bias, ids, lengths)


def bias_terms(value):
    high = value.astype(BF16).astype(F32)
    return high, (value - high).astype(BF16).astype(F32)


def put_bias(ref, width, high, low):
    if ref.shape[0] >= 2 * BIAS_ROWS:
        both = jnp.concatenate([high, low], axis=0).astype(BF16)
        ref[: 2 * BIAS_ROWS, width : width + EMBED_WIDTH] = both
    else:
        ref[:BIAS_ROWS, width : width + EMBED_WIDTH] = high.astype(BF16)
        ref[:BIAS_ROWS, width + EMBED_WIDTH : width + 2 * EMBED_WIDTH] = low.astype(BF16)


def get_bias(ref, width):
    if ref.shape[0] >= 2 * BIAS_ROWS:
        both = ref[: 2 * BIAS_ROWS, width : width + EMBED_WIDTH].astype(F32)
        return both[:BIAS_ROWS] + both[BIAS_ROWS:]
    high = ref[:BIAS_ROWS, width : width + EMBED_WIDTH].astype(F32)
    return high + ref[:BIAS_ROWS, width + EMBED_WIDTH : width + 2 * EMBED_WIDTH].astype(F32)


def extra_columns(rows):
    return EMBED_WIDTH if rows >= 2 * BIAS_ROWS else 2 * EMBED_WIDTH


def terms_kernel(
    ride, keep_ref, other_ref, act, cot, act_other, cot_other,
    up_keep_ref, up_send_ref, down_keep_ref, down_send_ref, bias_ref,
):
    width = act.shape[1]
    hidden = jnp.concatenate([keep_ref[0], other_ref[0]], axis=1)
    back = jnp.concatenate([keep_ref[1], other_ref[1]], axis=1)
    blocks = 3
    keep = hidden.shape[0] // 2
    bias_ref[...] = jnp.zeros_like(bias_ref)
    for first in range(0, width // EMBED_WIDTH, blocks):
        part = slice(first * EMBED_WIDTH, (first + blocks) * EMBED_WIDTH)
        values = jnp.concatenate([act[:, part], act_other[:, part]], axis=0)
        grads = jnp.concatenate([cot[:, part], cot_other[:, part]], axis=0)
        scaled = grads.astype(F32) * values.astype(F32)
        sums = jnp.sum(scaled, axis=0, keepdims=True)
        for k in range(blocks):
            bias_ref[first + k : first + k + 1, :] = sums[:, k * EMBED_WIDTH : (k + 1) * EMBED_WIDTH]
        up_part = jnp.dot(hidden, scaled.astype(BF16), preferred_element_type=F32)
        up_keep_ref[:, part] = up_part[:keep]
        up_send_ref[:, part] = up_part[keep:].astype(BF16)
        down_part = jnp.dot(back, values, preferred_element_type=F32)
        down_keep_ref[:, part] = down_part[:keep]
        down_send_ref[:, part] = down_part[keep:].astype(BF16)
    if ride:
        high, low = bias_terms(bias_ref[...])
        put_bias(up_send_ref, width, high, low)
        bias_ref[...] = high + low


def terms_call(keep, other, act, cot, act_other, cot_other, ride):
    tokens, width = act.shape
    rows = keep.shape[1] // 2
    extra = extra_columns(rows) if ride else 0
    return pl.pallas_call(
        functools.partial(terms_kernel, ride),
        in_specs=[VMEM] * 6,
        out_specs=[VMEM] * 5,
        out_shape=[
            jax.ShapeDtypeStruct((rows, width), F32),
            jax.ShapeDtypeStruct((rows, width + extra), BF16),
            jax.ShapeDtypeStruct((rows, width), F32),
            jax.ShapeDtypeStruct((rows, width), BF16),
            jax.ShapeDtypeStruct((BIAS_ROWS, EMBED_WIDTH), F32),
        ],
        compiler_params=params(16),
        cost_estimate=pl.CostEstimate(
            flops=16 * tokens * rows * width, bytes_accessed=8 * tokens * width + 12 * rows * width, transcendentals=0
        ),
    )(keep, other, act, cot, act_other, cot_other)


def halve_kernel(
    up_keep_ref, up_in_ref, down_keep_ref, down_in_ref, bias_ref,
    up_out_ref, up_send_ref, down_out_ref, down_send_ref, bias_out_ref,
):
    rows, width = up_keep_ref.shape
    half = rows // 2
    up = up_keep_ref[...] + up_in_ref[:, :width].astype(F32)
    up_out_ref[...] = up[:half]
    up_send_ref[:, :width] = up[half:].astype(BF16)
    down = down_keep_ref[...] + down_in_ref[...].astype(F32)
    down_out_ref[...] = down[:half]
    down_send_ref[...] = down[half:].astype(BF16)
    high, low = bias_terms(bias_ref[...] + get_bias(up_in_ref, width))
    put_bias(up_send_ref, width, high, low)
    bias_out_ref[...] = high + low


def halve_call(up_keep, up_in, down_keep, down_in, bias_sum):
    rows, width = up_keep.shape
    half = rows // 2
    return pl.pallas_call(
        halve_kernel,
        in_specs=[VMEM] * 5,
        out_specs=[VMEM] * 5,
        out_shape=[
            jax.ShapeDtypeStruct((half, width), F32),
            jax.ShapeDtypeStruct((half, width + extra_columns(half)), BF16),
            jax.ShapeDtypeStruct((half, width), F32),
            jax.ShapeDtypeStruct((half, width), BF16),
            jax.ShapeDtypeStruct(bias_sum.shape, F32),
        ],
        compiler_params=params(16),
    )(up_keep, up_in, down_keep, down_in, bias_sum)


def split_kernel(
    ride, n_table, scale, table_ref, up_keep_ref, up_in_ref, down_keep_ref, down_in_ref, bias_ref,
    own_ref, bias_out_ref, *rest,
):
    sends, store = rest[: n_table - 1], rest[n_table - 1]
    columns = own_ref.shape[2]
    width = up_keep_ref.shape[1]
    pairs = ((up_keep_ref, up_in_ref), (down_keep_ref, down_in_ref))
    for which, (keep, arrived) in enumerate(pairs):
        total = (keep[...] + arrived[:, :width].astype(F32)) * scale
        for table in range(n_table):
            store[table, which] = total[:, table * columns : (table + 1) * columns]
    own_ref[...] = store[table_ref[0]]
    start = -(-columns // EMBED_WIDTH) * EMBED_WIDTH
    bias = bias_ref[...]
    if ride:
        high, low = bias_terms(bias + get_bias(up_in_ref, width))
        bias = high + low
    bias_out_ref[...] = bias
    for shift in range(1, n_table):
        value = store[lax.rem(table_ref[0] + shift, n_table)].astype(BF16)
        sends[shift - 1][:, :, :columns] = value
        if ride:
            sends[shift - 1][0, :BIAS_ROWS, start:] = high.astype(BF16)
            sends[shift - 1][1, :BIAS_ROWS, start:] = low.astype(BF16)


def split_call(table_index, up_keep, up_in, down_keep, down_in, bias_sum, n_table, scale, ride):
    rows, width = up_keep.shape
    columns = width // n_table
    sent = -(-columns // EMBED_WIDTH) * EMBED_WIDTH + EMBED_WIDTH if ride else columns
    return pl.pallas_call(
        functools.partial(split_kernel, ride, n_table, scale),
        in_specs=[SMEM] + [VMEM] * 5,
        out_specs=[VMEM] * (n_table + 1),
        out_shape=[
            jax.ShapeDtypeStruct((2, rows, columns), F32),
            jax.ShapeDtypeStruct(bias_sum.shape, F32),
        ]
        + [jax.ShapeDtypeStruct((2, rows, sent), BF16)] * (n_table - 1),
        scratch_shapes=[pltpu.VMEM((n_table, 2, rows, columns), F32)],
        compiler_params=params(16),
    )(table_index, up_keep, up_in, down_keep, down_in, bias_sum)


def finish_kernel(ride, n_table, scale, table_ref, own_ref, bias_ref, *rest):
    arrived = rest[: n_table - 1]
    up_ref, down_ref, bias_out_ref, store = rest[n_table - 1 :]
    columns = own_ref.shape[2]
    start = -(-columns // EMBED_WIDTH) * EMBED_WIDTH
    up, down = own_ref[0], own_ref[1]
    store[table_ref[0]] = bias_ref[...]
    for shift in range(1, n_table):
        value = arrived[shift - 1]
        up = up + value[0, :, :columns].astype(F32)
        down = down + value[1, :, :columns].astype(F32)
        if ride:
            source = lax.rem(table_ref[0] + n_table - shift, n_table)
            high = value[0, :BIAS_ROWS, start:].astype(F32)
            store[source] = high + value[1, :BIAS_ROWS, start:].astype(F32)
    up_ref[...] = up
    down_ref[...] = down
    total = bias_ref[...]
    if ride:
        total = store[0]
        for table in range(1, n_table):
            total = total + store[table]
    bias_out_ref[...] = total[: bias_out_ref.shape[0]] * scale


def finish_call(table_index, own, bias_sum, arrived, scale, ride):
    n_table = len(arrived) + 1
    _, rows, columns = own.shape
    return pl.pallas_call(
        functools.partial(finish_kernel, ride, n_table, scale),
        in_specs=[SMEM] + [VMEM] * (n_table + 1),
        out_specs=[VMEM] * 3,
        out_shape=[
            jax.ShapeDtypeStruct((rows, columns), F32),
            jax.ShapeDtypeStruct((rows, columns), F32),
            jax.ShapeDtypeStruct((columns * n_table // EMBED_WIDTH, EMBED_WIDTH), F32),
        ],
        scratch_shapes=[pltpu.VMEM((n_table,) + bias_sum.shape, F32)],
        compiler_params=params(16),
    )(table_index, own, bias_sum, *arrived)


def padded(columns):
    return -(-columns // EMBED_WIDTH) * EMBED_WIDTH


def first_kernel(
    n_table, scale, table_ref, up_keep_ref, up_in_ref, down_keep_ref, down_in_ref, bias_ref,
    keep_ref, send_ref, bias_out_ref, store,
):
    _, _, rows, columns = keep_ref.shape
    width = up_keep_ref.shape[1]
    pairs = ((up_keep_ref, up_in_ref), (down_keep_ref, down_in_ref))
    for which, (keep, arrived) in enumerate(pairs):
        total = (keep[...] + arrived[:, :width].astype(F32)) * scale
        for table in range(n_table):
            store[table, which] = total[:, table * columns : (table + 1) * columns]
    for place in range(n_table // 2):
        keep_ref[place] = store[table_ref[0] ^ (2 * place)]
        for which in range(2):
            first = place * padded(columns)
            value = store[table_ref[0] ^ (2 * place + 1), which]
            send_ref[which * rows : (which + 1) * rows, first : first + columns] = value.astype(BF16)
    high, low = bias_terms(bias_ref[...] + get_bias(up_in_ref, width))
    put_bias(send_ref, n_table // 2 * padded(columns), high, low)
    bias_out_ref[...] = high + low


def message_shape(tables, rows, columns):
    return (2 * rows, tables * padded(columns) + extra_columns(2 * rows))


def first_call(table_index, up_keep, up_in, down_keep, down_in, bias_sum, n_table, scale):
    rows, width = up_keep.shape
    columns = width // n_table
    return pl.pallas_call(
        functools.partial(first_kernel, n_table, scale),
        in_specs=[SMEM] + [VMEM] * 5,
        out_specs=[VMEM] * 3,
        out_shape=[
            jax.ShapeDtypeStruct((n_table // 2, 2, rows, columns), F32),
            jax.ShapeDtypeStruct(message_shape(n_table // 2, rows, columns), BF16),
            jax.ShapeDtypeStruct(bias_sum.shape, F32),
        ],
        scratch_shapes=[pltpu.VMEM((n_table, 2, rows, columns), F32)],
        compiler_params=params(16),
    )(table_index, up_keep, up_in, down_keep, down_in, bias_sum)


def next_kernel(keep_ref, in_ref, bias_ref, out_ref, send_ref, bias_out_ref):
    count, _, rows, columns = keep_ref.shape
    for place in range(count):
        for which in range(2):
            part = slice(which * rows, (which + 1) * rows)
            first = place * padded(columns)
            total = keep_ref[place, which] + in_ref[part, first : first + columns].astype(F32)
            if place % 2 == 0:
                out_ref[place // 2, which] = total
            else:
                first = place // 2 * padded(columns)
                send_ref[part, first : first + columns] = total.astype(BF16)
    high, low = bias_terms(bias_ref[...] + get_bias(in_ref, count * padded(columns)))
    put_bias(send_ref, count // 2 * padded(columns), high, low)
    bias_out_ref[...] = high + low


def next_call(keep, arrived, bias_sum):
    count, _, rows, columns = keep.shape
    return pl.pallas_call(
        next_kernel,
        in_specs=[VMEM] * 3,
        out_specs=[VMEM] * 3,
        out_shape=[
            jax.ShapeDtypeStruct((count // 2, 2, rows, columns), F32),
            jax.ShapeDtypeStruct(message_shape(count // 2, rows, columns), BF16),
            jax.ShapeDtypeStruct(bias_sum.shape, F32),
        ],
        compiler_params=params(16),
    )(keep, arrived, bias_sum)


def last_kernel(scale, keep_ref, in_ref, bias_ref, up_ref, down_ref, bias_out_ref):
    rows, columns = up_ref.shape
    up_ref[...] = keep_ref[0, 0] + in_ref[:rows, :columns].astype(F32)
    down_ref[...] = keep_ref[0, 1] + in_ref[rows : 2 * rows, :columns].astype(F32)
    total = bias_ref[...] + get_bias(in_ref, padded(columns))
    bias_out_ref[...] = total[: bias_out_ref.shape[0]] * scale


def last_call(keep, arrived, bias_sum, n_table, scale):
    _, _, rows, columns = keep.shape
    return pl.pallas_call(
        functools.partial(last_kernel, scale),
        in_specs=[VMEM] * 3,
        out_specs=[VMEM] * 3,
        out_shape=[
            jax.ShapeDtypeStruct((rows, columns), F32),
            jax.ShapeDtypeStruct((rows, columns), F32),
            jax.ShapeDtypeStruct((columns * n_table // EMBED_WIDTH, EMBED_WIDTH), F32),
        ],
        compiler_params=params(16),
    )(keep, arrived, bias_sum)


def rows_kernel(slots, *refs):
    *parts, out_hbm, id_store, row_store, out, sems = refs
    tokens = (parts[0].shape[0] - id_store.shape[1]) // slots
    numbers = lax.broadcasted_iota(jnp.int32, row_store.shape, 0) - EMPTY
    row_store[...] = numbers.astype(F32).astype(BF16)
    for source, part in enumerate(parts):
        id_store[source] = part[slots * tokens :, :].astype(F32)
    copies = []
    for slot in range(slots):
        rows = row_store[...].reshape(TABLE_REACH_ROWS // 16, 16, tokens)
        one, zero = jnp.ones(rows.shape, BF16), jnp.zeros(rows.shape, BF16)
        counts = []
        for source in range(len(parts)):
            count = None
            for entry in range(BAG):
                place = slot * BAG + entry
                ids = jnp.broadcast_to(id_store[source, place : place + 1, :], (16, tokens)).astype(BF16)
                found = jnp.where(rows == ids[None], one, zero)
                count = found if count is None else count + found
            counts.append(count.reshape(TABLE_REACH_ROWS, tokens))
        count = jnp.concatenate(counts, axis=1)
        grad = jnp.concatenate([part[slot * tokens : (slot + 1) * tokens, :] for part in parts], axis=0)
        out[slot] = jnp.dot(count, grad, preferred_element_type=F32)
        copies.append(pltpu.make_async_copy(out.at[slot], out_hbm.at[0, slot], sems.at[slot]))
        copies[-1].start()
    for copy in copies:
        copy.wait()


def rows_call(parts, slots):
    n_table = len(parts)
    id_rows = -(-slots * BAG // 16) * 16
    tokens = (parts[0].shape[0] - id_rows) // slots
    return pl.pallas_call(
        functools.partial(rows_kernel, slots),
        in_specs=[VMEM] * n_table,
        out_specs=ANY,
        out_shape=jax.ShapeDtypeStruct((1, slots, TABLE_REACH_ROWS, EMBED_WIDTH), F32),
        scratch_shapes=[
            pltpu.VMEM((n_table, id_rows, tokens), F32),
            pltpu.VMEM((TABLE_REACH_ROWS, tokens), BF16),
            pltpu.VMEM((slots, TABLE_REACH_ROWS, EMBED_WIDTH), F32),
            pltpu.SemaphoreType.DMA((slots,)),
        ],
        compiler_params=params(16),
        cost_estimate=pl.CostEstimate(
            flops=2 * slots * n_table * tokens * TABLE_REACH_ROWS * EMBED_WIDTH,
            bytes_accessed=4 * slots * TABLE_REACH_ROWS * EMBED_WIDTH,
            transcendentals=0,
        ),
    )(*parts)


def body(
    activations, cotangent, down_weight, up_weight, bias, bag_ids, bag_lengths, feature_table_slot
):
    tokens, width = activations.shape
    rank = down_weight.shape[0]
    n_table = lax.axis_size("table")
    n_rep = lax.axis_size("rep")
    slots = (SPARSE_FEATURES + n_table - 1) // n_table
    scale = 1.0 / math.sqrt(tokens * n_table * n_rep)
    table_index = lax.axis_index("table").astype(jnp.int32).reshape(1)
    rep_index = lax.axis_index("rep").astype(jnp.int32).reshape(1)
    far_bits = [1 << k for k in range(1, n_rep.bit_length() - 1)]
    up_bits, down_bits = [1] + far_bits, [1] + far_bits[::-1]
    ride = rank // n_rep >= BIAS_ROWS

    def swap(value, axis, bit):
        size = n_rep if axis == "rep" else n_table
        return lax.ppermute(value, axis, [(k, k ^ bit) for k in range(size)])

    def shifted(value, shift):
        return lax.ppermute(value, "table", [(k, (k + shift) % n_table) for k in range(n_table)])

    act_other = swap(activations, "rep", 1)
    cot_other = swap(cotangent, "rep", 1)
    act, cot, keep, send, dense_grad, *parts = input_call(
        table_index, rep_index, feature_table_slot, activations, cotangent, down_weight, up_weight,
        bias.reshape(-1, EMBED_WIDTH), jnp.transpose(bag_ids, (1, 2, 0)), jnp.transpose(bag_lengths, (1, 0)),
        n_table, slots, up_bits, down_bits,
    )
    other = swap(send, "rep", 1)
    parts = [parts[0]] + [shifted(parts[k], k) for k in range(1, n_table)]
    up_keep, up_send, down_keep, down_send, bias_sum = terms_call(
        keep, other, act, cot, act_other, cot_other, ride
    )
    def exchange(place, up_send, down_send, bias_sum):
        up_in = swap(up_send, "rep", up_bits[place])
        down_in = swap(down_send, "rep", down_bits[place])
        if not ride:
            bias_sum = bias_sum + swap(bias_sum, "rep", up_bits[place])
        return up_in, down_in, bias_sum

    def halved(up_keep, up_in, down_keep, down_in, bias_sum):
        if ride:
            return halve_call(up_keep, up_in, down_keep, down_in, bias_sum)
        half = up_keep.shape[0] // 2
        up = up_keep + up_in.astype(F32)
        down = down_keep + down_in.astype(F32)
        return up[:half], up[half:].astype(BF16), down[:half], down[half:].astype(BF16), bias_sum

    def chain(up_keep, up_send, down_keep, down_send, bias_sum):
        for place in range(2, len(up_bits)):
            up_in, down_in, bias_sum = exchange(place, up_send, down_send, bias_sum)
            if place < len(up_bits) - 1:
                up_keep, up_send, down_keep, down_send, bias_sum = halved(
                    up_keep, up_in, down_keep, down_in, bias_sum
                )
        if not ride:
            for bit in [1 << k for k in range(n_table.bit_length() - 1)]:
                bias_sum = bias_sum + swap(bias_sum, "table", bit)
        if not ride:
            return split_call(
                table_index, up_keep, up_in, down_keep, down_in, bias_sum, n_table, scale, ride
            )
        own, message, bias_sum = first_call(
            table_index, up_keep, up_in, down_keep, down_in, bias_sum, n_table, scale
        )
        for bit in [1 << k for k in range(n_table.bit_length() - 2)]:
            message = swap(message, "table", bit)
            own, message, bias_sum = next_call(own, message, bias_sum)
        return [own, bias_sum, message]

    up_in, down_in, bias_sum = exchange(1, up_send, down_send, bias_sum)
    terms = halved(up_keep, up_in, down_keep, down_in, bias_sum)
    shapes = jax.eval_shape(chain, *terms)
    own, bias_sum, *sends = lax.cond(
        feature_table_slot[0] >= 0,
        chain,
        lambda *_: jax.tree.map(lambda x: jnp.zeros(x.shape, x.dtype), shapes),
        *terms,
    )
    if ride:
        message = swap(sends[0], "table", n_table // 2)
        up_grad, down_grad, bias_grad = last_call(own, message, bias_sum, n_table, scale)
    else:
        arrived = [shifted(value, k + 1) for k, value in enumerate(sends)]
        up_grad, down_grad, bias_grad = finish_call(table_index, own, bias_sum, arrived, scale, ride)
    parts, _ = lax.optimization_barrier((parts, own))
    row_grad = rows_call(parts, slots)
    bias_grad = bias_grad.reshape(width)
    return (dense_grad, up_grad, down_grad, bias_grad, row_grad)


def solution(mesh):
    placed = (
        P(("table", "rep"), None),
        P(("table", "rep"), None),
        P(),
        P(),
        P(),
        P(("table", "rep"), None, None),
        P(("table", "rep"), None),
        P(),
    )
    return jax.shard_map(
        body,
        mesh=mesh,
        in_specs=placed,
        out_specs=(
            P(("table", "rep"), None),
            P("rep", "table"),
            P("rep", "table"),
            P(),
            P("rep", "table", None, None),
        ),
        check_vma=False,
    )
```
